32 devices in a mesh: dp: 16 (over z, x, core), tensor: 2 (over y).
Axes of the slice: x: 2, y: 2, z: 4, core: 2. Of those that a mesh axis runs over, the one named last changes fastest.
Arguments:
- layer_input: bfloat16 [16384, 1024], P(('dp', 'tensor')), may hold values from -6 to 6
- qkv_weight: bfloat16 [3, 1024, 1024], P(None, None, 'tensor'), may hold values from -0.1875 to 0.1875
- qv_bias: float32 [2, 1024], P(None, 'tensor'), may hold values from -3 to 3
- out_weight: bfloat16 [1024, 1024], P('tensor'), may hold values from -1.5 to 1.5
- out_bias: float32 [1024], replicated, may hold values from -3 to 3
- norm1_gain: float32 [1024], replicated, may hold values from 0.5 to 1.5
- norm1_shift: float32 [1024], replicated, may hold values from -3 to 3
- up_weight: bfloat16 [1024, 4096], P(None, 'tensor'), may hold values from -0.1875 to 0.1875
- up_bias: bfloat16 [4096], P('tensor'), may hold values from -3 to 3
- down_weight: bfloat16 [4096, 1024], P('tensor'), may hold values from -0.09375 to 0.09375
- down_bias: float32 [1024], replicated, may hold values from -3 to 3
- norm2_gain: float32 [1024], replicated, may hold values from 0.5 to 1.5
- norm2_shift: float32 [1024], replicated, may hold values from -3 to 3
- lengths: int32 [32], P('dp'), may hold values from 64 to 512, as said below
- grad_output: bfloat16 [16384, 1024], P(('dp', 'tensor')), may hold values from -6 to 6
Outputs:
- layer_output: bfloat16 [16384, 1024], P(('dp', 'tensor'))
- grad_input: float32 [16384, 1024], P(('dp', 'tensor'))
- grad_qkv_weight: float32 [3, 1024, 1024], P(None, None, 'tensor')
- grad_qv_bias: float32 [2, 1024], P(None, 'tensor')
- grad_out_weight: float32 [1024, 1024], P('tensor')
- grad_out_bias: float32 [1024], replicated
- grad_norm1_gain: float32 [1024], replicated
- grad_norm1_shift: float32 [1024], replicated
- grad_up_weight: float32 [1024, 4096], P(None, 'tensor')
- grad_up_bias: float32 [4096], P('tensor')
- grad_down_weight: float32 [4096, 1024], P('tensor')
- grad_down_bias: float32 [1024], replicated
- grad_norm2_gain: float32 [1024], replicated
- grad_norm2_shift: float32 [1024], replicated
The draws below stay inside these ranges and needn't reach their ends.
Inputs may be any that keep to these rules, and one draw needn't show every extreme that they name: `lengths`: each dp group holds 512 * 2 // 512 consecutive slots; in every group one slot, drawn from the seed, holds a full item of 512 residues, the others hold short items of 64 to 128 or long ones over 256.
All inputs are finite; a program needn't handle non-finite values.
Results may differ from the reference program's by a relative error of at most 0.013.
The reference program's roundings to bfloat16 on the way count: a program that leaves them out, or rounds other values in their place, can miss the bound.
Values may be sent and summed in bfloat16 or wider, within the bound.
No kernel may reach another device: no remote copies, remote signals or barrier semaphores. Data moves between devices by JAX's collectives and lax.ppermute only.
A program may use at most 192 MiB of HBM per device.

```python
from functools import partial
import jax
import jax.numpy as jnp
from jax import lax

D = 1024
HEADS = 16
HD = 64
FF = 4096
SEQ_LEN = 512
TOK_DEV = 512
TOKENS = 16384
SEQS = 32
N_TENSOR = 2


def draw_lengths(key, part):
    key = jax.random.fold_in(key, 11)
    per_group = TOK_DEV * N_TENSOR // SEQ_LEN
    groups = SEQS // per_group
    keys_all = jax.random.split(key, 5)
    share = jax.random.randint(keys_all[0], (groups, 1), 0, 5)
    picks = jax.random.randint(keys_all[1], (groups, per_group), 0, 4)
    long_len = jax.random.randint(keys_all[2], (groups, per_group), SEQ_LEN // 2 + 1, SEQ_LEN + 1)
    short_len = jax.random.randint(keys_all[3], (groups, per_group), SEQ_LEN // 8, SEQ_LEN // 4 + 1)
    chosen = jnp.where(picks < share, long_len, short_len)
    full_slot = jax.random.randint(keys_all[4], (groups, 1), 0, per_group)
    column = jnp.arange(per_group, dtype=jnp.int32)[None, :]
    chosen = jnp.where(column == full_slot, SEQ_LEN, chosen)
    return chosen.reshape(SEQS).astype(jnp.int32)


def shard_levels(rng, shape, cuts, least, high):
    def one(position, parts):
        draws = jax.random.uniform(jax.random.fold_in(jax.random.fold_in(rng, 6), position), (parts,), jnp.float32, least / len(cuts), high / len(cuts))
        return jnp.repeat(jnp.exp(draws), shape[position] // parts).reshape((-1,) + (1,) * (len(shape) - position - 1))

    level = one(*cuts[0])
    for cut in cuts[1:]:
        level = level * one(*cut)
    return level


def centred(stream_key, dims, scale, most, cuts=(), kind=jnp.bfloat16):
    level = shard_levels(stream_key, dims, cuts, -0.22, 0.18) if cuts else 1.0
    values = jax.random.normal(stream_key, dims, jnp.float32) * scale * level
    return jnp.minimum(jnp.maximum(values, -most), most).astype(kind)


def setup_inputs(seed: int = 0) -> dict:
    splits = jax.random.split(jax.random.key(seed), 16)
    layer_input = centred(splits[0], (TOKENS, D), 1.0, 6.0, ((0, 32),))
    qkv_weight = centred(splits[1], (3, D, D), D ** -0.5, 0.1875, ((2, 2),))
    qv_bias = centred(splits[2], (2, D), 0.5, 3.0, ((1, 2),), jnp.float32)
    out_weight = centred(splits[3], (D, D), (max(1, D // 64)) ** -0.5, 1.5, ((0, 2),))
    out_bias = centred(splits[4], (D,), 0.5, 3.0, (), jnp.float32)
    norm1_gain = jnp.clip(1.0 + 0.1 * jax.random.normal(splits[5], (D,), jnp.float32), 0.5, 1.5)
    norm1_shift = centred(splits[6], (D,), 0.5, 3.0, (), jnp.float32)
    up_weight = centred(splits[7], (D, FF), D ** -0.5, 0.1875, ((1, 2),))
    up_bias = centred(splits[8], (FF,), 0.5, 3.0, ((0, 2),))
    down_weight = centred(splits[9], (FF, D), FF ** -0.5, 0.09375, ((0, 2),))
    down_bias = centred(splits[10], (D,), 0.5, 3.0, (), jnp.float32)
    norm2_gain = jnp.clip(1.0 + 0.1 * jax.random.normal(splits[11], (D,), jnp.float32), 0.5, 1.5)
    norm2_shift = centred(splits[12], (D,), 0.5, 3.0, (), jnp.float32)
    lengths = draw_lengths(jax.random.fold_in(splits[15], 71), 0)
    grad_output = centred(splits[14], (TOKENS, D), 1.0, 6.0, ((0, 32),))
    return dict(layer_input=layer_input, qkv_weight=qkv_weight, qv_bias=qv_bias, out_weight=out_weight, out_bias=out_bias, norm1_gain=norm1_gain, norm1_shift=norm1_shift, up_weight=up_weight, up_bias=up_bias, down_weight=down_weight, down_bias=down_bias, norm2_gain=norm2_gain, norm2_shift=norm2_shift, lengths=lengths, grad_output=grad_output)


@jax.custom_vjp
def low(v):
    return lax.optimization_barrier(v.astype(jnp.bfloat16)).astype(jnp.float32)

@jax.custom_vjp
def low_back(v):
    return v

def low_keep(v):
    return (low(v), None)

def low_pass(kept, grad):
    return (grad,)

def back_keep(v):
    return (v, None)

def back_low(kept, grad):
    return (low(grad),)
low.defvjp(low_keep, low_pass)
low_back.defvjp(back_keep, back_low)

def matmul(left, right):
    return jnp.dot(left, right, precision=lax.Precision.HIGHEST, preferred_element_type=jnp.float32)

def norm_rows(hidden, gain, shift):
    center = hidden - lax.optimization_barrier(jnp.mean(hidden, axis=-1, keepdims=True))
    spread = lax.optimization_barrier(jnp.mean(center * center, axis=-1, keepdims=True))
    return center * lax.rsqrt(spread + 1e-05) * gain + shift

def attend_slot(member):
    query, keys, values, length = member
    scores = jnp.einsum('qhd,khd->hqk', query, keys, precision=lax.Precision.HIGHEST) * HD ** (-0.5)
    scores = low_back(scores)
    valid = jnp.arange(SEQ_LEN).astype(jnp.int32) < length
    scores = jnp.where(valid[None, None, :], scores, jnp.float32(-1000000000.0))
    highest = lax.optimization_barrier(jnp.max(scores, axis=-1, keepdims=True))
    expo = jnp.exp(scores - highest)
    probs = low(expo / lax.optimization_barrier(jnp.sum(expo, axis=-1, keepdims=True)))
    return jnp.einsum('hqk,khd->qhd', probs, values, precision=lax.Precision.HIGHEST)

def layer(lengths, layer_input, qkv_weight, qv_bias, out_weight, out_bias, norm1_gain, norm1_shift, up_weight, up_bias, down_weight, down_bias, norm2_gain, norm2_shift):
    projected = jnp.einsum('td,cde->cte', layer_input, qkv_weight, precision=lax.Precision.HIGHEST)
    query = low(low_back(projected[0] + qv_bias[0]))
    keys = low(low_back(projected[1]))
    values = low(low_back(projected[2] + qv_bias[1]))
    layout = (-1, SEQ_LEN, HEADS, HD)
    mixed = lax.map(jax.checkpoint(attend_slot), (query.reshape(layout), keys.reshape(layout), values.reshape(layout), lengths))
    mixed = low(low_back(mixed.reshape(layer_input.shape)))
    hidden_one = low_back(matmul(mixed, out_weight)) + out_bias + layer_input
    normed_one = norm_rows(hidden_one, norm1_gain, norm1_shift)
    upward = low_back(matmul(low(normed_one), up_weight) + up_bias)
    active = low(jax.nn.gelu(upward, approximate=False))
    hidden_two = low_back(matmul(active, down_weight)) + down_bias + normed_one
    return norm_rows(hidden_two, norm2_gain, norm2_shift)

def reference(layer_input, qkv_weight, qv_bias, out_weight, out_bias, norm1_gain, norm1_shift, up_weight, up_bias, down_weight, down_bias, norm2_gain, norm2_shift, lengths, grad_output):
    floats = tuple((member.astype(jnp.float32) for member in (layer_input, qkv_weight, qv_bias, out_weight, out_bias, norm1_gain, norm1_shift, up_weight, up_bias, down_weight, down_bias, norm2_gain, norm2_shift)))
    result, pull_back = jax.vjp(partial(layer, lengths), *floats)
    grads = pull_back(grad_output.astype(jnp.float32))
    return (result.astype(jnp.bfloat16), grads[0], grads[1], grads[2], grads[3], grads[4], grads[5], grads[6], grads[7], grads[8], grads[9], grads[10], grads[11], grads[12])
```

```python
import functools

import jax
import jax.numpy as jnp
from jax import lax
from jax.experimental import pallas as pl
from jax.experimental.pallas import tpu as pltpu
from jax.sharding import PartitionSpec as P

HD = 64
F32 = jnp.float32
BF16 = jnp.bfloat16
NEG = -1000000000.0

ERFC_P = 0.3275911
ERFC_C = (
    0.18510853909898187,
    0.17995808540893535,
    0.21032499893163595,
    0.011746556912990477,
    0.4777504794974274,
    -0.4314195259659222,
    0.5110037999525718,
    -0.14447299033990682,
)


def gelu_both(up):
    size = jnp.abs(up)
    t = 1.0 / (1.0 + (ERFC_P * 0.5**0.5) * size)
    poly = jnp.full_like(t, 0.5 * ERFC_C[-1])
    for c in ERFC_C[-2::-1]:
        poly = poly * t + 0.5 * c
    density = jnp.exp(-0.5 * up * up)
    tail = poly * t * density
    phi = jnp.where(up > 0, 1.0 - tail, tail)
    return up * phi, phi + up * (density * 0.3989422804014327)


def contract(a, b, ca, cb):
    return lax.dot_general(a, b, (((ca,), (cb,)), ((), ())), preferred_element_type=F32)


def attend_kernel(len_ref, q_ref, k_ref, v_ref, o_ref, lse_ref):
    length = len_ref[0]
    q, k, v = q_ref[...], k_ref[...], v_ref[...]
    rows, width = q.shape
    head = lax.broadcasted_iota(jnp.int32, (rows, width), 1) // HD
    key_pos = lax.broadcasted_iota(jnp.int32, (rows, rows), 0)
    out = None
    for h in range(width // HD):
        mine = head == h
        kh = jnp.where(mine, k, jnp.zeros_like(k)) * jnp.asarray(HD**-0.5, BF16)
        s = jnp.where(key_pos < length, contract(kh, q, 1, 1), F32(NEG))
        top = jnp.max(s, axis=0, keepdims=True)
        e = jnp.exp(s - top)
        total = jnp.sum(e, axis=0, keepdims=True)
        lse_ref[0, h : h + 1, :] = top + jnp.log(total)
        p = (e * (1.0 / total)).astype(BF16)
        o = contract(p, v, 0, 0)
        out = o if out is None else jnp.where(mine, o, out)
    o_ref[...] = out.astype(BF16)


def attend(length, q, k, v):
    rows, width = q.shape
    wide = min(2 * HD, width)
    steps = width // wide
    spec = pl.BlockSpec((rows, wide), lambda i: (0, i))
    return pl.pallas_call(
        attend_kernel,
        grid=(steps,),
        in_specs=[pl.BlockSpec(memory_space=pltpu.SMEM), spec, spec, spec],
        out_specs=[spec, pl.BlockSpec((1, wide // HD, rows), lambda i: (i, 0, 0))],
        out_shape=[
            jax.ShapeDtypeStruct((rows, width), BF16),
            jax.ShapeDtypeStruct((steps, wide // HD, rows), F32),
        ],
        compiler_params=pltpu.CompilerParams(vmem_limit_bytes=32 * 2**20),
        cost_estimate=pl.CostEstimate(
            flops=16 * rows * rows * width,
            bytes_accessed=8 * rows * width,
            transcendentals=rows * rows * width // HD,
        ),
        name="attend",
    )(length, q, k, v)


def attend_back_kernel(
    len_ref, q_ref, k_ref, v_ref, g_ref, lse_ref, dq_ref, dk_ref, dv_ref
):
    length = len_ref[0]
    q, k, v, g = q_ref[...], k_ref[...], v_ref[...], g_ref[...]
    rows, width = q.shape
    head = lax.broadcasted_iota(jnp.int32, (rows, width), 1) // HD
    head_t = lax.broadcasted_iota(jnp.int32, (width, rows), 0) // HD
    key_pos = lax.broadcasted_iota(jnp.int32, (rows, rows), 0)
    dq = dk = dv = None
    for h in range(width // HD):
        mine = head == h
        kh = jnp.where(mine, k, jnp.zeros_like(k)) * jnp.asarray(HD**-0.5, BF16)
        vh = jnp.where(mine, v, jnp.zeros_like(v))
        s = jnp.where(key_pos < length, contract(kh, q, 1, 1), F32(NEG))
        p = jnp.exp(s - lse_ref[0, h : h + 1, :])
        dp = contract(vh, g, 1, 1)
        dvh = contract(p.astype(BF16), g, 1, 0)
        center = jnp.sum(p * dp, axis=0, keepdims=True)
        ds = (p * (dp - center)).astype(BF16)
        dkh = contract(ds, q, 1, 0)
        dqh = contract(k, ds, 0, 0)
        dv = dvh if dv is None else jnp.where(mine, dvh, dv)
        dk = dkh if dk is None else jnp.where(mine, dkh, dk)
        dq = dqh if dq is None else jnp.where(head_t == h, dqh, dq)
    dq_ref[...] = (dq * (HD**-0.5)).T.astype(BF16)
    dk_ref[...] = (dk * (HD**-0.5)).astype(BF16)
    dv_ref[...] = dv.astype(BF16)


def attend_back(length, q, k, v, g, lse):
    rows, width = q.shape
    wide = min(2 * HD, width)
    spec = pl.BlockSpec((rows, wide), lambda i: (0, i))
    out = jax.ShapeDtypeStruct((rows, width), BF16)
    return pl.pallas_call(
        attend_back_kernel,
        grid=(width // wide,),
        in_specs=[pl.BlockSpec(memory_space=pltpu.SMEM), spec, spec, spec, spec]
        + [pl.BlockSpec((1, wide // HD, rows), lambda i: (i, 0, 0))],
        out_specs=[spec, spec, spec],
        out_shape=[out, out, out],
        compiler_params=pltpu.CompilerParams(vmem_limit_bytes=48 * 2**20),
        cost_estimate=pl.CostEstimate(
            flops=40 * rows * rows * width,
            bytes_accessed=14 * rows * width,
            transcendentals=rows * rows * width // HD,
        ),
        name="attend_back",
    )(length, q, k, v, g, lse)


class Moves:
    def __init__(self, n_dp, n_tensor):
        self.n_dp, self.n_tensor = n_dp, n_tensor
        self.dp = lax.axis_index("dp")
        self.core = self.dp & 1
        self.chip_bits = [b for b in (2, 4, 8, 16, 32, 64) if b < n_dp]

    def bit(self, mask):
        return (self.dp // mask) & 1

    def over_dp(self, a, mask):
        return lax.ppermute(a, "dp", [(i, i ^ mask) for i in range(self.n_dp)])

    def over_tensor(self, a, mask):
        return lax.ppermute(
            a, "tensor", [(i, i ^ mask) for i in range(self.n_tensor)]
        )

    def join(self, a, b, bit, axis):
        low, high = jnp.where(bit == 0, a, b), jnp.where(bit == 0, b, a)
        return jnp.concatenate([low, high], axis=axis)

    def fetch(self, w, masks, axis):
        index = sum(self.bit(m) << i for i, m in enumerate(masks))
        size = w.shape[axis] >> len(masks)
        piece = lax.dynamic_slice_in_dim(w, index * size, size, axis)
        parts = []
        for d in range(1, self.n_tensor):
            got = self.over_tensor(piece, d)
            for m in masks:
                got = self.join(got, self.over_dp(got, m), self.bit(m), axis)
            parts.append(got)
        return parts

    def reduce(self, parts):
        parts = list(parts)
        step = self.n_tensor // 2
        while step:
            for d in range(step):
                got = self.over_tensor(parts[d + step], step)
                parts[d] = add(parts[d], got)
            step //= 2
        own = parts[0]
        for m in self.chip_bits:
            half = own.shape[0] // 2
            bit = self.bit(m)
            send = lax.dynamic_slice_in_dim(own, (1 - bit) * half, half, 0)
            keep = lax.dynamic_slice_in_dim(own, bit * half, half, 0)
            own = add(keep, self.over_dp(send, m))
        for m in reversed(self.chip_bits):
            own = self.join(own, self.over_dp(own, m), self.bit(m), 0)
        return own


def add(a, b):
    return (a.astype(F32) + b.astype(F32)).astype(BF16)


def layer_norm(hidden):
    center = hidden - jnp.mean(hidden, axis=-1, keepdims=True)
    spread = jnp.mean(center * center, axis=-1, keepdims=True)
    scale = lax.rsqrt(spread + 1e-05)
    return center * scale, scale


def layer_norm_back(grad, normal, scale, gain):
    gy = grad * gain
    mean = jnp.mean(gy, axis=-1, keepdims=True)
    along = jnp.mean(gy * normal, axis=-1, keepdims=True)
    return scale * (gy - mean - normal * along)


def body(
    n_dp,
    n_tensor,
    layer_input,
    qkv_weight,
    qv_bias,
    out_weight,
    out_bias,
    norm1_gain,
    norm1_shift,
    up_weight,
    up_bias,
    down_weight,
    down_bias,
    norm2_gain,
    norm2_shift,
    lengths,
    grad_output,
):
    mv = Moves(n_dp, n_tensor)
    parts = range(n_tensor)
    width = layer_input.shape[1]
    half = width // 2
    core = mv.core
    hw = qkv_weight.shape[2]
    fw = up_weight.shape[1]
    x = layer_input
    length = lax.dynamic_slice_in_dim(lengths, lax.axis_index("tensor"), 1, 0)

    def swap(a):
        return mv.over_dp(a, 1)

    def my_half(a):
        return lax.dynamic_slice_in_dim(a, core * half, half, 1)

    def swap_half(a):
        return swap(lax.dynamic_slice_in_dim(a, (1 - core) * half, half, 1))

    qkv = [qkv_weight] + mv.fetch(qkv_weight, (1, 2, 4), 1)
    bias_pack = jnp.concatenate([qv_bias.reshape(-1), up_bias.astype(F32)])
    biases = [bias_pack] + [mv.over_tensor(bias_pack, d) for d in range(1, n_tensor)]
    out_w = [out_weight] + mv.fetch(out_weight, (1, 4, 2), 0)
    up_w = [up_weight] + mv.fetch(up_weight, (1, 2, 4), 0)
    down_w = [down_weight] + mv.fetch(down_weight, (1, 4, 2), 0)
    q_bias = [b[:hw] for b in biases]
    v_bias = [b[hw : 2 * hw] for b in biases]
    up_b = [b[2 * hw :] for b in biases]

    x_mine, x_sib = my_half(x), swap_half(x)
    q, k, v, mixed, lse = [], [], [], [], []
    for d in parts:
        q.append((contract(x, qkv[d][0], 1, 0) + q_bias[d]).astype(BF16))
        k.append(contract(x, qkv[d][1], 1, 0).astype(BF16))
        v.append((contract(x, qkv[d][2], 1, 0) + v_bias[d]).astype(BF16))
        m, l = attend(length, q[d], k[d], v[d])
        mixed.append(m)
        lse.append(l)
    hidden_one = x.astype(F32) + out_bias
    for d in parts:
        hidden_one = hidden_one + contract(mixed[d], out_w[d], 1, 0)
    normal_one, scale_one = layer_norm(hidden_one)
    normed_one = normal_one * norm1_gain + norm1_shift
    normed_b = normed_one.astype(BF16)
    nb_mine, nb_sib = my_half(normed_b), swap_half(normed_b)
    act, slope, act_sib = [], [], []
    for d in parts:
        a, s = gelu_both(contract(normed_b, up_w[d], 1, 0) + up_b[d])
        act.append(a.astype(BF16))
        slope.append(s.astype(BF16))
        act_sib.append(swap(act[d]))
    mixed_sib = [swap(m) for m in mixed]
    hidden_two = normed_one + down_bias
    for d in parts:
        hidden_two = hidden_two + contract(act[d], down_w[d], 1, 0)
    normal_two, scale_two = layer_norm(hidden_two)
    result = (normal_two * norm2_gain + norm2_shift).astype(BF16)

    grad = grad_output.astype(F32)
    g_gain2 = jnp.sum(grad * normal_two, axis=0)
    g_shift2 = jnp.sum(grad, axis=0)
    g_two = layer_norm_back(grad, normal_two, scale_two, norm2_gain)
    g_down_bias = jnp.sum(g_two, axis=0)
    g_two_b = g_two.astype(BF16)
    g2_mine, g2_sib = my_half(g_two_b), swap_half(g_two_b)

    order = list(parts)[::-1]
    down_sum = []
    chunk = fw // 2
    for lo in (0, chunk):
        made = [None] * n_tensor
        for d in order:
            made[d] = (
                contract(act[d][:, lo : lo + chunk], g2_mine, 0, 0)
                + contract(act_sib[d][:, lo : lo + chunk], g2_sib, 0, 0)
            ).astype(BF16)
        down_sum.append(mv.reduce(made))
    g_up, g_up_sib = [None] * n_tensor, [None] * n_tensor
    for d in order:
        g_up[d] = (contract(g_two_b, down_w[d], 1, 1) * slope[d]).astype(BF16)
        g_up_sib[d] = swap(g_up[d])
    g_up_bias = [jnp.sum(g.astype(F32), axis=0) for g in g_up]
    up_sum = []
    chunk = half // 2
    for lo in (0, chunk):
        made = [None] * n_tensor
        for d in order:
            made[d] = (
                contract(nb_mine[:, lo : lo + chunk], g_up[d], 0, 0)
                + contract(nb_sib[:, lo : lo + chunk], g_up_sib[d], 0, 0)
            ).astype(BF16)
        up_sum.append(mv.reduce(made))
    g_one_in = g_two
    for d in parts:
        g_one_in = g_one_in + contract(g_up[d], up_w[d], 1, 1)
    g_gain1 = jnp.sum(g_one_in * normal_one, axis=0)
    g_shift1 = jnp.sum(g_one_in, axis=0)
    g_one = layer_norm_back(g_one_in, normal_one, scale_one, norm1_gain)
    g_out_bias = jnp.sum(g_one, axis=0)
    g_one_b = g_one.astype(BF16)
    g1_mine, g1_sib = my_half(g_one_b), swap_half(g_one_b)
    made = [None] * n_tensor
    for d in order:
        made[d] = (
            contract(mixed[d], g1_mine, 0, 0) + contract(mixed_sib[d], g1_sib, 0, 0)
        ).astype(BF16)
    out_sum = mv.reduce(made)

    g_proj, g_proj_sib = [None] * n_tensor, [None] * n_tensor
    for d in order:
        g_mixed = contract(g_one_b, out_w[d], 1, 1).astype(BF16)
        g_proj[d] = attend_back(length, q[d], k[d], v[d], g_mixed, lse[d])
        g_proj_sib[d] = [swap(g) for g in g_proj[d]]
    qkv_sum = []
    for c in range(3):
        made = [None] * n_tensor
        for d in order:
            made[d] = (
                contract(x_mine, g_proj[d][c], 0, 0)
                + contract(x_sib, g_proj_sib[d][c], 0, 0)
            ).astype(BF16)
        qkv_sum.append(mv.reduce(made))
    g_input = g_one
    for d in parts:
        for c in range(3):
            g_input = g_input + contract(g_proj[d][c], qkv[d][c], 1, 1)

    whole = jnp.concatenate(
        [g_out_bias, g_gain1, g_shift1, g_down_bias, g_gain2, g_shift2]
    )
    packs = []
    for d in parts:
        gq = jnp.sum(g_proj[d][0].astype(F32), axis=0)
        gv = jnp.sum(g_proj[d][2].astype(F32), axis=0)
        packs.append(jnp.concatenate([whole, gq, gv, g_up_bias[d]]))
    step = n_tensor // 2
    while step:
        for d in range(step):
            packs[d] = packs[d] + mv.over_tensor(packs[d + step], step)
        step //= 2
    small = packs[0]
    for m in [1] + mv.chip_bits:
        small = small + mv.over_dp(small, m)

    def both_cores(sums, columns):
        pieces = [mv.join(s, swap(s), core, 1 if columns else 0) for s in sums]
        return pieces

    grad_down = jnp.concatenate(
        [p.astype(F32) for p in both_cores(down_sum, True)], axis=0
    )
    ups = [(s, swap(s)) for s in up_sum]
    mine = jnp.concatenate([a for a, _ in ups], axis=0)
    theirs = jnp.concatenate([b for _, b in ups], axis=0)
    grad_up = mv.join(mine, theirs, core, 0).astype(F32)
    grad_out = both_cores([out_sum], True)[0].astype(F32)
    grad_qkv = jnp.stack([p.astype(F32) for p in both_cores(qkv_sum, False)])
    vec = [small[i * width : (i + 1) * width] for i in range(6)]
    rest = small[6 * width :]
    grad_qv_bias = rest[: 2 * hw].reshape(2, hw)
    return (
        result,
        g_input,
        grad_qkv,
        grad_qv_bias,
        grad_out,
        vec[0],
        vec[1],
        vec[2],
        grad_up,
        rest[2 * hw :],
        grad_down,
        vec[3],
        vec[4],
        vec[5],
    )


def solution(mesh):
    return jax.shard_map(
        functools.partial(body, mesh.shape["dp"], mesh.shape["tensor"]),
        mesh=mesh,
        in_specs=(
            P(("dp", "tensor"), None),
            P(None, None, "tensor"),
            P(None, "tensor"),
            P("tensor", None),
            P(),
            P(),
            P(),
            P(None, "tensor"),
            P("tensor"),
            P("tensor", None),
            P(),
            P(),
            P(),
            P("dp"),
            P(("dp", "tensor"), None),
        ),
        out_specs=(
            P(("dp", "tensor"), None),
            P(("dp", "tensor"), None),
            P(None, None, "tensor"),
            P(None, "tensor"),
            P("tensor", None),
            P(),
            P(),
            P(),
            P(None, "tensor"),
            P("tensor"),
            P("tensor", None),
            P(),
            P(),
            P(),
        ),
        check_vma=False,
    )
```

```python
import functools

import jax
import jax.numpy as jnp
import numpy as np
from jax import lax
from jax.experimental import pallas as pl
from jax.experimental.pallas import tpu as pltpu
from jax.sharding import PartitionSpec as P

HD = 64
F32 = jnp.float32
BF16 = jnp.bfloat16
NEG = -1000000000.0
SCALE = 0
COST = [0.0]
LOG = []
FLOWN = []
HELD = []


def cost():
    flops = int(SCALE * COST[0] * 1.15e9)
    return pl.CostEstimate(flops=flops, bytes_accessed=0, transcendentals=0)


ERFC_P = 0.3275911
ERFC_C = (
    0.18510853909898187,
    0.17995808540893535,
    0.21032499893163595,
    0.011746556912990477,
    0.4777504794974274,
    -0.4314195259659222,
    0.5110037999525718,
    -0.14447299033990682,
)


def gelu_both(up):
    size = jnp.abs(up)
    t = 1.0 / (1.0 + (ERFC_P * 0.5**0.5) * size)
    poly = jnp.full_like(t, 0.5 * ERFC_C[-1])
    for c in ERFC_C[-2::-1]:
        poly = poly * t + 0.5 * c
    density = jnp.exp(-0.5 * up * up)
    tail = poly * t * density
    phi = jnp.where(up > 0, 1.0 - tail, tail)
    return up * phi, phi + up * (density * 0.3989422804014327)


def contract(a, b, ca, cb):
    return lax.dot_general(a, b, (((ca,), (cb,)), ((), ())), preferred_element_type=F32)


def params(mib):
    return pltpu.CompilerParams(vmem_limit_bytes=mib * 2**20)


def whole_spec(a):
    return pl.BlockSpec(a.shape, lambda *_: (0,) * len(a.shape))


BROUGHT = ((0, 0), (2, 0), (1, 0), (4, 0), (0, 1), (3, 0), (1, 1), (5, 0))


AT, CORES, DP, BITS = 0, 8, 10, 11


def attend_kernel(len_ref, q_ref, k_ref, v_ref, o_ref, lse_ref):
    length = len_ref[0]
    q, k, v = q_ref[0], k_ref[0], v_ref[0]
    rows, width = q.shape
    head = lax.broadcasted_iota(jnp.int32, (rows, width), 1) // HD
    key_pos = lax.broadcasted_iota(jnp.int32, (rows, rows), 0)
    out = None
    for h in range(width // HD):
        mine = head == h
        kh = jnp.where(mine, k, jnp.zeros_like(k)) * jnp.asarray(HD**-0.5, BF16)
        s = jnp.where(key_pos < length, contract(kh, q, 1, 1), F32(NEG))
        top = jnp.max(s, axis=0, keepdims=True)
        e = jnp.exp(s - top)
        total = jnp.sum(e, axis=0, keepdims=True)
        lse_ref[0, h : h + 1, :] = top + jnp.log(total)
        p = (e * (1.0 / total)).astype(BF16)
        o = contract(p, v, 0, 0)
        out = o if out is None else jnp.where(mine, o, out)
    o_ref[...] = out.astype(BF16)


def third(rows, wide, c):
    return pl.BlockSpec((1, rows, wide), lambda i, c=c: (c, 0, i))


def attend(length, qkv):
    _, rows, width = qkv.shape
    wide = min(2 * HD, width)
    steps = width // wide
    return pl.pallas_call(
        attend_kernel,
        grid=(steps,),
        in_specs=[pl.BlockSpec(memory_space=pltpu.SMEM)]
        + [third(rows, wide, c) for c in range(3)],
        out_specs=[
            pl.BlockSpec((rows, wide), lambda i: (0, i)),
            pl.BlockSpec((1, wide // HD, rows), lambda i: (i, 0, 0)),
        ],
        out_shape=[
            jax.ShapeDtypeStruct((rows, width), BF16),
            jax.ShapeDtypeStruct((steps, wide // HD, rows), F32),
        ],
        compiler_params=params(20),
        cost_estimate=cost(),
        name="attend",
    )(length, qkv, qkv, qkv)


def attend_back_kernel(
    len_ref, q_ref, k_ref, v_ref, g1_ref, w_ref, lse_ref, d_ref, sum_ref
):
    length = len_ref[0]
    q, k, v = q_ref[0], k_ref[0], v_ref[0]
    g = contract(g1_ref[...], w_ref[...], 1, 1).astype(BF16)
    rows, width = q.shape
    head = lax.broadcasted_iota(jnp.int32, (rows, width), 1) // HD
    head_t = lax.broadcasted_iota(jnp.int32, (width, rows), 0) // HD
    key_pos = lax.broadcasted_iota(jnp.int32, (rows, rows), 0)
    dq = dk = dv = None
    for h in range(width // HD):
        mine = head == h
        kh = jnp.where(mine, k, jnp.zeros_like(k)) * jnp.asarray(HD**-0.5, BF16)
        vh = jnp.where(mine, v, jnp.zeros_like(v))
        s = jnp.where(key_pos < length, contract(kh, q, 1, 1), F32(NEG))
        p = jnp.exp(s - lse_ref[0, h : h + 1, :])
        dp = contract(vh, g, 1, 1)
        dvh = contract(p.astype(BF16), g, 1, 0)
        center = jnp.sum(p * dp, axis=0, keepdims=True)
        ds = (p * (dp - center)).astype(BF16)
        dkh = contract(ds, q, 1, 0)
        dqh = contract(k, ds, 0, 0)
        dv = dvh if dv is None else jnp.where(mine, dvh, dv)
        dk = dkh if dk is None else jnp.where(mine, dkh, dk)
        dq = dqh if dq is None else jnp.where(head_t == h, dqh, dq)
    out = (
        (dq * (HD**-0.5)).T.astype(BF16),
        (dk * (HD**-0.5)).astype(BF16),
        dv.astype(BF16),
    )
    for c in range(3):
        d_ref[c] = out[c]
        sum_ref[c : c + 1, :] = jnp.sum(out[c].astype(F32), axis=0, keepdims=True)


def attend_back(length, qkv, g_one, out_w, lse):
    _, rows, width = qkv.shape
    wide = min(2 * HD, width)
    d = g_one.shape[1]
    return pl.pallas_call(
        attend_back_kernel,
        grid=(width // wide,),
        in_specs=[pl.BlockSpec(memory_space=pltpu.SMEM)]
        + [third(rows, wide, c) for c in range(3)]
        + [
            whole_spec(g_one),
            pl.BlockSpec((wide, d), lambda i: (i, 0)),
            pl.BlockSpec((1, wide // HD, rows), lambda i: (i, 0, 0)),
        ],
        out_specs=[
            pl.BlockSpec((3, rows, wide), lambda i: (0, 0, i)),
            pl.BlockSpec((3, wide), lambda i: (0, i)),
        ],
        out_shape=[
            jax.ShapeDtypeStruct((3, rows, width), BF16),
            jax.ShapeDtypeStruct((3, width), F32),
        ],
        compiler_params=params(28),
        cost_estimate=cost(),
        name="attend_back",
    )(length, qkv, qkv, qkv, g_one, out_w, lse)


def project(at, x, bias, *pieces):
    n = len(pieces)
    rows, depth = x.shape
    width = pieces[0].shape[2]
    size = depth // len(BROUGHT)

    def kernel(at_ref, x_ref, b_ref, *refs):
        w_ref = refs[0]
        if n > 1:
            w_ref = refs[n + 1]
            for i, (k, j) in enumerate(BROUGHT):
                row = pl.multiple_of(at_ref[i] * size, size)
                w_ref[0, pl.ds(row, size)] = refs[k][0, j * size : (j + 1) * size]
        refs[n][0] = (contract(x_ref[...], w_ref[0], 1, 0) + b_ref[0]).astype(BF16)

    out_specs = [pl.BlockSpec((1, rows, width), lambda c, at: (c, 0, 0))]
    out_shape = [jax.ShapeDtypeStruct((3, rows, width), BF16)]
    if n > 1:
        out_specs.append(pl.BlockSpec((1, depth, width), lambda c, at: (c, 0, 0)))
        out_shape.append(jax.ShapeDtypeStruct((3, depth, width), BF16))
    return pl.pallas_call(
        kernel,
        grid_spec=pltpu.PrefetchScalarGridSpec(
            num_scalar_prefetch=1,
            grid=(3,),
            in_specs=[
                whole_spec(x),
                pl.BlockSpec((1, 1, width), lambda c, at: (c, 0, 0)),
            ]
            + [
                pl.BlockSpec((1, p.shape[1], width), lambda c, at: (c, 0, 0))
                for p in pieces
            ],
            out_specs=out_specs,
        ),
        out_shape=out_shape,
        compiler_params=params(20),
        cost_estimate=cost(),
        name="project",
    )(at, x, bias, *pieces)


def norm(hidden):
    center = hidden - jnp.mean(hidden, axis=-1, keepdims=True)
    spread = jnp.mean(center * center, axis=-1, keepdims=True)
    scale = lax.rsqrt(spread + 1e-05)
    return center * scale, scale


def norm_back(grad, normal, scale, gain):
    gy = grad * gain
    mean = jnp.mean(gy, axis=-1, keepdims=True)
    along = jnp.mean(gy * normal, axis=-1, keepdims=True)
    return scale * (gy - mean - normal * along)


def attended(at, x, bias, gain, shift, mixed, weights):
    rows, d = x.shape
    step = min(128, rows)
    cut = [i for i, w in enumerate(weights) if len(w) > 1]
    flat = [p for w in weights for p in w]
    n = len(mixed)

    def kernel(at_ref, x_ref, b_ref, g_ref, s_ref, *refs):
        m, w = refs[:n], refs[n : n + len(flat)]
        low_ref, normal_ref, scale_ref = refs[n + len(flat) :][:3]
        outs = refs[n + len(flat) + 3 :]
        k = j = 0
        total = x_ref[...].astype(F32) + b_ref[...]
        for i, ps in enumerate(weights):
            if len(ps) > 1:
                size = ps[0].shape[0]
                held = outs[j]

                @pl.when(pl.program_id(0) == 0)
                def _(held=held, k=k, ps=ps, size=size):
                    for q in range(len(ps)):
                        row = pl.multiple_of(at_ref[CORES + q] * size, size)
                        held[pl.ds(row, size), :] = w[k + q][...]

                value = held[...]
                j += 1
            else:
                value = w[k][...]
            k += len(ps)
            total = total + contract(m[i][...], value, 1, 0)
        normal, scale = norm(total)
        normal_ref[...] = normal
        scale_ref[...] = scale
        low_ref[...] = (normal * g_ref[...] + s_ref[...]).astype(BF16)

    row = pl.BlockSpec((step, d), lambda i, at: (i, 0))
    out_specs = [row, row, pl.BlockSpec((step, 1), lambda i, at: (i, 0))]
    out_shape = [
        jax.ShapeDtypeStruct((rows, d), BF16),
        jax.ShapeDtypeStruct((rows, d), F32),
        jax.ShapeDtypeStruct((rows, 1), F32),
    ]
    for i in cut:
        out_shape.append(
            jax.ShapeDtypeStruct((len(weights[i]) * weights[i][0].shape[0], d), BF16)
        )
        out_specs.append(whole_spec(out_shape[-1]))
    vecs = [v.reshape(1, d) for v in (bias, gain, shift)]
    return pl.pallas_call(
        kernel,
        grid_spec=pltpu.PrefetchScalarGridSpec(
            num_scalar_prefetch=1,
            grid=(rows // step,),
            in_specs=[row]
            + [whole_spec(v) for v in vecs]
            + [pl.BlockSpec((step, m.shape[1]), lambda i, at: (i, 0)) for m in mixed]
            + [whole_spec(p) for p in flat],
            out_specs=out_specs,
        ),
        out_shape=out_shape,
        compiler_params=params(20),
        cost_estimate=cost(),
        name="attended",
    )(at, x, *vecs, *mixed, *flat)


def widened(at, low, bias, *pieces):
    rows, d = low.shape
    n = len(pieces)
    size, width = d // len(BROUGHT), pieces[0].shape[1]
    block, sub = bias.shape[2], min(128, rows)

    def kernel(at_ref, x_ref, b_ref, *refs):
        act_ref, slope_ref = refs[n : n + 2]
        w_ref = refs[0]
        if n > 1:
            w_ref = refs[n + 2]
            for i, (k, j) in enumerate(BROUGHT):
                row = pl.multiple_of(at_ref[i] * size, size)
                w_ref[pl.ds(row, size), :] = refs[k][j * size : (j + 1) * size, :]
        for i in range(0, rows, sub):
            up = contract(x_ref[i : i + sub, :], w_ref[...], 1, 0) + b_ref[0]
            act, slope = gelu_both(up)
            act_ref[i : i + sub, :] = act.astype(BF16)
            slope_ref[i : i + sub, :] = slope.astype(BF16)

    out = jax.ShapeDtypeStruct((rows, width), BF16)
    out_shape = [out, out]
    if n > 1:
        out_shape.append(jax.ShapeDtypeStruct((d, width), BF16))
    return pl.pallas_call(
        kernel,
        grid_spec=pltpu.PrefetchScalarGridSpec(
            num_scalar_prefetch=1,
            grid=(width // block,),
            in_specs=[
                whole_spec(low),
                pl.BlockSpec((1, 1, block), lambda i, at: (3 + i, 0, 0)),
            ]
            + [pl.BlockSpec((p.shape[0], block), lambda i, at: (0, i)) for p in pieces],
            out_specs=[
                pl.BlockSpec((o.shape[0], block), lambda i, at: (0, i))
                for o in out_shape
            ],
        ),
        out_shape=out_shape,
        compiler_params=params(24),
        cost_estimate=cost(),
        name="widened",
    )(at, low, bias, *pieces)


def narrowed(at, normal1, gain1, shift1, bias, gain, shift, grad_output, act, weights):
    rows, d = normal1.shape
    block = 256
    steps = d // block
    flat = [p for w in weights for p in w]
    cut = [w for w in weights if len(w) > 1]
    n = len(act)

    def kernel(at_ref, nm_ref, g1_ref, s1_ref, b_ref, g_ref, s_ref, go_ref, *refs):
        a, w = refs[:n], refs[n : n + len(flat)]
        low_ref, grad_ref, result_ref, sum_ref, acc = refs[n + len(flat) :][:5]
        held = list(refs[n + len(flat) + 5 :])
        total = nm_ref[...] * g1_ref[...] + s1_ref[...] + b_ref[...]
        k = 0
        for i, ps in enumerate(weights):
            value = w[k]
            if len(ps) > 1:
                value = held.pop(0)
                size = value.shape[0] // len(BROUGHT)
                for q, (m, j) in enumerate(BROUGHT):
                    row = pl.multiple_of(at_ref[q] * size, size)
                    value[pl.ds(row, size), :] = w[k + m][j * size : (j + 1) * size, :]
            total = total + contract(a[i][...], value[...], 1, 0)
            k += len(ps)
        acc[pl.program_id(0)] = total

        @pl.when(pl.program_id(0) == steps - 1)
        def _():
            sums = [jnp.zeros((1, d), F32) for _ in range(3)]
            for r in range(0, rows, 64):
                cut = slice(r, r + 64)
                hidden = jnp.concatenate([acc[i, cut, :] for i in range(steps)], axis=1)
                normal, scale = norm(hidden)
                result_ref[cut, :] = (normal * g_ref[...] + s_ref[...]).astype(BF16)
                grad = go_ref[cut, :].astype(F32)
                g_two = norm_back(grad, normal, scale, g_ref[...])
                grad_ref[cut, :] = g_two
                low_ref[cut, :] = g_two.astype(BF16)
                for j, v in enumerate((g_two, grad * normal, grad)):
                    sums[j] = sums[j] + jnp.sum(v, axis=0, keepdims=True)
            for j in range(3):
                sum_ref[j : j + 1, :] = sums[j]

    def col(rows):
        return pl.BlockSpec((rows, block), lambda s, at: (0, s))

    vecs = [v.reshape(1, d) for v in (gain1, shift1, bias, gain, shift)]
    out_shape = [
        jax.ShapeDtypeStruct((rows, d), BF16),
        jax.ShapeDtypeStruct((rows, d), F32),
        jax.ShapeDtypeStruct((rows, d), BF16),
        jax.ShapeDtypeStruct((3, d), F32),
    ]
    return pl.pallas_call(
        kernel,
        grid_spec=pltpu.PrefetchScalarGridSpec(
            num_scalar_prefetch=1,
            grid=(steps,),
            in_specs=[col(rows), col(1), col(1), col(1)]
            + [whole_spec(v) for v in vecs[3:]]
            + [whole_spec(grad_output)]
            + [whole_spec(a) for a in act]
            + [col(p.shape[0]) for p in flat],
            out_specs=[whole_spec(o) for o in out_shape],
            scratch_shapes=[pltpu.VMEM((steps, rows, block), F32)]
            + [pltpu.VMEM((act[0].shape[1], block), BF16) for _ in cut],
        ),
        out_shape=out_shape,
        compiler_params=params(32 if cut else 48),
        cost_estimate=cost(),
        name="narrowed",
    )(at, normal1, *vecs, grad_output, *act, *flat)


def gelu_back(at, g, slope, *pieces):
    rows, d = g.shape
    width = slope.shape[1]
    n = len(pieces)
    size = min(512, width)

    def kernel(at_ref, g_ref, s_ref, *refs):
        out_ref, sum_ref = refs[n : n + 2]
        w = refs[0][...]
        if n > 1:
            held, cut = refs[n + 2], width // len(BROUGHT)

            @pl.when(pl.program_id(0) == 0)
            def _():
                for i, (k, j) in enumerate(BROUGHT):
                    row = pl.multiple_of(at_ref[i] * cut, cut)
                    held[pl.ds(row, cut), :] = refs[k][j * cut : (j + 1) * cut, :]

            w = held[pl.ds(pl.multiple_of(pl.program_id(0) * size, size), size), :]
        low = (contract(g_ref[...], w, 1, 1) * s_ref[...].astype(F32)).astype(BF16)
        out_ref[...] = low
        sum_ref[...] = jnp.sum(low.astype(F32), axis=0, keepdims=True)

    def column(rows):
        return pl.BlockSpec((rows, size), lambda s, at: (0, s))

    w_specs = [pl.BlockSpec((size, d), lambda s, at: (s, 0))]
    return pl.pallas_call(
        kernel,
        grid_spec=pltpu.PrefetchScalarGridSpec(
            num_scalar_prefetch=1,
            grid=(width // size,),
            in_specs=[whole_spec(g), column(rows)]
            + ([whole_spec(p) for p in pieces] if n > 1 else w_specs),
            out_specs=[column(rows), column(1)],
            scratch_shapes=[pltpu.VMEM((width, d), BF16)] if n > 1 else [],
        ),
        out_shape=[
            jax.ShapeDtypeStruct((rows, width), BF16),
            jax.ShapeDtypeStruct((1, width), F32),
        ],
        compiler_params=params(24),
        cost_estimate=cost(),
        name="gelu_back",
    )(at, g, slope, *pieces)


def attended_back(g_two, normal, scale, gain, g_up, up_w):
    rows, d = g_two.shape
    block = 256
    steps, n = d // block, len(g_up)

    def kernel(g2_ref, nm_ref, sc_ref, gain_ref, *refs):
        g, w = refs[:n], refs[n : 2 * n]
        low_ref, grad_ref, sum_ref, acc = refs[2 * n :]
        total = g2_ref[...]
        for i in range(n):
            total = total + contract(g[i][...], w[i][...], 1, 1)
        acc[pl.program_id(0)] = total

        @pl.when(pl.program_id(0) == steps - 1)
        def _():
            sums = [jnp.zeros((1, d), F32) for _ in range(3)]
            for r in range(0, rows, 64):
                cut = slice(r, r + 64)
                g_in = jnp.concatenate([acc[i, cut, :] for i in range(steps)], axis=1)
                nm = nm_ref[cut, :]
                g_one = norm_back(g_in, nm, sc_ref[cut, :], gain_ref[...])
                grad_ref[cut, :] = g_one
                low_ref[cut, :] = g_one.astype(BF16)
                for j, v in enumerate((g_one, g_in * nm, g_in)):
                    sums[j] = sums[j] + jnp.sum(v, axis=0, keepdims=True)
            for j in range(3):
                sum_ref[j : j + 1, :] = sums[j]

    out_shape = [
        jax.ShapeDtypeStruct((rows, d), BF16),
        jax.ShapeDtypeStruct((rows, d), F32),
        jax.ShapeDtypeStruct((3, d), F32),
    ]
    gain = gain.reshape(1, d)
    return pl.pallas_call(
        kernel,
        grid=(steps,),
        in_specs=[pl.BlockSpec((rows, block), lambda s: (0, s))]
        + [whole_spec(a) for a in (normal, scale, gain, *g_up)]
        + [pl.BlockSpec((block, w.shape[1]), lambda s: (s, 0)) for w in up_w],
        out_specs=[whole_spec(o) for o in out_shape],
        out_shape=out_shape,
        scratch_shapes=[pltpu.VMEM((steps, rows, block), F32)],
        compiler_params=params(28 if n > 1 else 48),
        cost_estimate=cost(),
        name="attended_back",
    )(g_two, normal, scale, gain, *g_up, *up_w)


def input_grad(g_one, g_proj, qkv_w):
    rows, d = g_one.shape
    width, n = g_proj[0].shape[2], len(g_proj)
    block = 256

    def kernel(g1_ref, *refs):
        g, w, out_ref = refs[:n], refs[n : 2 * n], refs[-1]
        total = g1_ref[...]
        for i in range(n):
            for c in range(3):
                total = total + contract(g[i][c], w[i][c], 1, 1)
        out_ref[...] = total

    col = pl.BlockSpec((rows, block), lambda s: (0, s))
    return pl.pallas_call(
        kernel,
        grid=(d // block,),
        in_specs=[col]
        + [whole_spec(g) for g in g_proj]
        + [pl.BlockSpec((3, block, width), lambda s: (0, s, 0))] * n,
        out_specs=col,
        out_shape=jax.ShapeDtypeStruct((rows, d), F32),
        compiler_params=params(24),
        cost_estimate=cost(),
        name="input_grad",
    )(g_one, *g_proj, *qkv_w)


def pick(index, pieces):
    n = len(pieces)
    views = [(i, j) for i, p in enumerate(pieces) for j in range(len(p[3]))]

    def kernel(index_ref, *refs):
        for v, (i, j) in enumerate(views):
            axis, size = pieces[i][1:3]
            at = tuple([slice(None)] * axis + [slice(j * size, (j + 1) * size)])
            refs[len(views) + i][at] = refs[v][...]

    specs, shapes = [], []
    for i, j in views:
        a, axis, size, places = pieces[i]
        specs.append(
            pl.BlockSpec(
                a.shape[:axis] + (size,) + a.shape[axis + 1 :],
                lambda s, at, p=places[j], axis=axis, n=a.ndim: tuple(
                    at[p] if k == axis else 0 for k in range(n)
                ),
            )
        )
    for a, axis, size, places in pieces:
        shape = a.shape[:axis] + (size * len(places),) + a.shape[axis + 1 :]
        shapes.append(jax.ShapeDtypeStruct(shape, a.dtype))
    return pl.pallas_call(
        kernel,
        grid_spec=pltpu.PrefetchScalarGridSpec(
            num_scalar_prefetch=1,
            grid=(1,),
            in_specs=specs,
            out_specs=[whole_spec(s) for s in shapes],
        ),
        out_shape=shapes,
        compiler_params=params(60),
        cost_estimate=cost(),
        name="pick",
    )(index, *[pieces[i][0] for i, _ in views])


def add(a, b):
    return (a.astype(F32) + b.astype(F32)).astype(BF16)


def add_split(bits, which, a, b):
    rows, columns = a.shape
    half = rows // 2
    if half % 16:
        total, bit = add(a, b), bits[BITS + which]
        return (
            lax.dynamic_slice_in_dim(total, bit * half, half, 0),
            lax.dynamic_slice_in_dim(total, (1 - bit) * half, half, 0),
        )
    block = half // 2 if half >= 256 else half
    per = half // block

    def kernel(bits_ref, a0, b0, a1, b1, keep_ref, send_ref):
        send_ref[...] = add(a1[...], b1[...])
        keep_ref[...] = add(a0[...], b0[...])

    def spec(of):
        return pl.BlockSpec((block, columns), lambda s, bits: (of(s, bits), 0))

    kept = spec(lambda s, bits: bits[BITS + which] * per + s)
    sent = spec(lambda s, bits: (1 - bits[BITS + which]) * per + s)
    plain = spec(lambda s, bits: s)
    out = jax.ShapeDtypeStruct((half, columns), BF16)
    return pl.pallas_call(
        kernel,
        grid_spec=pltpu.PrefetchScalarGridSpec(
            num_scalar_prefetch=1,
            grid=(per,),
            in_specs=[kept, kept, sent, sent],
            out_specs=[plain, plain],
        ),
        out_shape=[out, out],
        compiler_params=params(12),
        cost_estimate=cost(),
        name="add_split",
    )(bits, a, b, a, b)


def grad_stack(bits, outs, rows, width):
    jobs = [job for out in outs for job in out]
    sizes = [sum(job[4] for job in out) for out in outs]

    def depth_of(a):
        a = a[0] if isinstance(a, tuple) else a
        return a.shape[-2]

    depth = depth_of(jobs[0][0])
    total = sum(sizes)

    def kernel(bits_ref, *refs):
        s = pl.program_id(0)
        at = first = 0
        j = 0
        for o, out in enumerate(outs):
            for job in out:

                @pl.when((s >= at) & (s < at + job[4]))
                def _(j=j, o=o):
                    x1, y1, x2, y2 = (
                        r[0] if len(r.shape) == 3 else r[...]
                        for r in refs[4 * j : 4 * j + 4]
                    )
                    value = contract(x1, y1, 0, 0) + contract(x2, y2, 0, 0)
                    refs[4 * len(jobs) + o][...] = value.astype(BF16)

                at += job[4]
                j += 1

    def column(place, bits):
        return place[0] + sum(k * bits[BITS + i] for i, k in enumerate(place[1:]) if k)

    def spec(a, block, of):
        if isinstance(a, tuple):
            return pl.BlockSpec((1, *block), lambda s, bits: (a[1], 0, of(s, bits)))
        return pl.BlockSpec(block, lambda s, bits: (0, of(s, bits)))

    specs, args, at = [], [], 0
    for a1, b1, a2, b2, n, a_at, b_at in jobs:

        def a_of(s, bits, at=at, n=n, p=a_at):
            return column(p, bits) + jnp.clip(s - at, 0, n - 1)

        def b_of(s, bits, p=b_at):
            return column(p, bits)

        for a, b in ((a1, b1), (a2, b2)):
            specs += [spec(a, (depth, rows), a_of), spec(b, (depth, width), b_of)]
            args += [a, b]
        at += n
    out_specs, at = [], 0
    for size in sizes:
        out_specs.append(
            pl.BlockSpec(
                (rows, width),
                lambda s, bits, at=at, n=size: (jnp.clip(s - at, 0, n - 1), 0),
            )
        )
        at += size
    return pl.pallas_call(
        kernel,
        grid_spec=pltpu.PrefetchScalarGridSpec(
            num_scalar_prefetch=1, grid=(total,), in_specs=specs, out_specs=out_specs
        ),
        out_shape=[jax.ShapeDtypeStruct((n * rows, width), BF16) for n in sizes],
        compiler_params=params(24),
        cost_estimate=cost(),
        name="grad_stack",
    )(bits, *[a[0] if isinstance(a, tuple) else a for a in args])


class Box:
    def __init__(self, value):
        self.value = value


class Steps:
    def __init__(self):
        self.kept = []

    def keep(self, value):
        self.kept.append(Box(value))
        return self.kept[-1]

    def fence(self):
        held = lax.optimization_barrier(tuple(b.value for b in self.kept))
        for b, value in zip(self.kept, held):
            b.value = value

    def __call__(self, name, work, *ins):
        self.fence()
        with jax.named_scope(name):
            out = work(*[b.value for b in ins])
        out = [self.keep(v) for v in jax.tree.leaves(out)]
        self.fence()
        return out

    def wait(self, flight):
        self.kept.append(flight)
        self.fence()


class Moves:
    def __init__(self, n_dp, n_tensor):
        self.n_dp, self.n_tensor = n_dp, n_tensor
        self.dp = lax.axis_index("dp")
        self.core = self.dp & 1
        self.chip_bits = [b for b in (2, 4, 8, 16, 32, 64) if b < n_dp]

    def bit(self, mask):
        return (self.dp // mask) & 1

    def index(self, masks):
        return sum(self.bit(m) << i for i, m in enumerate(masks))

    def over(self, a, axis, mask, name):
        with jax.named_scope(name):
            n = self.n_dp if axis == "dp" else self.n_tensor
            return Box(lax.ppermute(a.value, axis, [(i, i ^ mask) for i in range(n)]))


def widen(core, sources, block, out_shape, steps, name):
    n, count = len(sources), len(steps[0])
    tables = []
    for bit in (0, 1):
        rows = np.zeros((n + 1 + len(out_shape), count), np.int32)
        for q in range(n):
            used = [s for s in range(count) if steps[bit][s][0] == q]
            for s in range(count):
                later = [u for u in used if u >= s]
                at = later[0] if later else used[-1]
                rows[q, s] = steps[bit][at][1]
        for s in range(count):
            rows[n, s] = steps[bit][s][0]
            rows[n + 1 :, s] = steps[bit][s][2]
        tables.append(rows)
    table = jnp.where(core == 0, jnp.asarray(tables[0]), jnp.asarray(tables[1]))

    def kernel(table_ref, *refs):
        s = pl.program_id(0)
        for q in range(n):

            @pl.when(table_ref[n, s] == q)
            def _():
                refs[n][...] = refs[q][...].astype(F32).reshape(refs[n].shape)

    lead = len(out_shape) - 2
    return pl.pallas_call(
        kernel,
        grid_spec=pltpu.PrefetchScalarGridSpec(
            num_scalar_prefetch=1,
            grid=(count,),
            in_specs=[
                pl.BlockSpec(block, lambda s, t, q=q: (t[q, s], 0)) for q in range(n)
            ],
            out_specs=pl.BlockSpec(
                (1,) * lead + block,
                lambda s, t: tuple(t[n + 1 + j, s] for j in range(len(out_shape))),
            ),
        ),
        out_shape=jax.ShapeDtypeStruct(out_shape, F32),
        compiler_params=params(24),
        cost_estimate=cost(),
        name=name,
    )(table, *sources)


def spread(gathered, unit, tables, block, out_shape, name):
    count, views = len(tables), len(tables[0][0])
    columns = gathered.shape[-1]
    lead = len(out_shape) - 2
    table = np.asarray([list(t[0]) + list(t[1]) for t in tables], np.int32).T

    def kernel(table_ref, *refs):
        out = refs[views]
        for v in range(views):
            part = refs[v][0].astype(F32)
            if lead:
                out[0, v * unit : (v + 1) * unit, :] = part
            else:
                out[v * unit : (v + 1) * unit, :] = part

    return pl.pallas_call(
        kernel,
        grid_spec=pltpu.PrefetchScalarGridSpec(
            num_scalar_prefetch=1,
            grid=(count,),
            in_specs=[
                pl.BlockSpec((1, unit, columns), lambda s, t, v=v: (t[v, s], 0, 0))
                for v in range(views)
            ],
            out_specs=pl.BlockSpec(
                (1,) * lead + block,
                lambda s, t: tuple(t[views + j, s] for j in range(len(out_shape))),
            ),
        ),
        out_shape=jax.ShapeDtypeStruct(out_shape, F32),
        compiler_params=params(40),
        cost_estimate=cost(),
        name=name,
    )(jnp.asarray(table), *[gathered.reshape(-1, unit, columns)] * views)


START, LATENCY = 1.4, 3.0
RATES = {"y": 46e3, "x": 46e3, "z": 46e3, "core": 500e3}
GATHER = 52.0
FLIGHTS = 5
MARGIN, PATIENCE = 4.0, 8.0


class Plan:
    def __init__(self, mv):
        self.mv, self.steps = mv, Steps()
        self.box, self.when, self.free = {}, {}, {}
        self.tasks, self.flying, self.waiting = [], [], []
        self.clock, self.gap, self.sent, self.flown = 0.0, 0, {}, {}
        LOG.clear()
        FLOWN.clear()

    def given(self, **arrays):
        for key, value in arrays.items():
            self.box[key], self.when[key] = self.steps.keep(value), 0.0

    def task(self, name, rank, cost, needs, makes, work, sends=()):
        self.tasks.append((rank, len(self.tasks), name, cost, needs, makes, work, sends))

    def link(self, axis, mask):
        if axis == "tensor":
            return "y", mask
        if mask < 4:
            return ("core", "x")[mask // 2], 1
        return "z", mask // 4

    def send(self, new, key, axis, mask):
        a = self.box[key]
        if mask is None:
            with jax.named_scope(new):
                self.box[new] = Box(lax.all_gather(a.value, axis))
            self.clock += 0.7
            self.free["sc"] = max(self.free.get("sc", 0.0), self.clock) + GATHER
            self.when[new] = self.free["sc"]
            return
        while len(self.flying) >= FLIGHTS:
            self.land(min(self.flying, key=lambda k: self.when[k]))
        self.box[new] = self.mv.over(a, axis, mask, new)
        link, often = self.link(axis, mask)
        took = often * a.value.size * a.value.dtype.itemsize / RATES[link]
        self.clock += 0.5 if link == "core" else START
        self.free[link] = max(self.free.get(link, 0.0), self.clock) + took
        self.when[new] = self.free[link] + (1.0 if link == "core" else LATENCY)
        self.flying.append(new)
        self.sent[new] = (self.gap,)
        self.flown[new] = (a.value.size * a.value.dtype.itemsize, link, took)
        FLOWN.append((new, self.clock, self.when[new]))

    def send_due(self):
        for s in list(self.waiting):
            after = s[4] if len(s) > 4 else None
            if after and not (after in self.when and self.when[after] <= self.clock):
                continue
            if after in self.flying:
                self.land(after)
            self.waiting.remove(s)
            held = []
            if s[3] is not None:
                value = self.box[s[1]].value
                size = value.size * value.dtype.itemsize
                held = [
                    k
                    for k in self.flying
                    if self.sent[k][0] < self.gap and self.flown[k][0] <= size
                ]
                for k in [k for k in held if self.when[k] <= self.clock + PATIENCE]:
                    self.land(k)
                    held.remove(k)
            for k in held:
                self.free[self.flown[k][1]] = max(
                    [self.clock]
                    + [
                        self.when[j] - LATENCY
                        for j in self.flying
                        if j not in held and self.flown[j][1] == self.flown[k][1]
                    ]
                )
            self.send(*s[:4])
            for k in held:
                if k in self.flying:
                    _, link, took = self.flown[k]
                    self.sent[k] = (self.gap,)
                    self.free[link] = max(self.free[link], self.clock) + took
                    self.when[k] = self.free[link] + LATENCY
                    HELD.append((k, s[0]))

    def land(self, key):
        self.flying.remove(key)
        self.steps.wait(self.box[key])
        self.clock = max(self.clock, self.when[key])

    def run(self):
        while self.tasks:
            self.send_due()
            known = [
                t
                for t in sorted(self.tasks, key=lambda t: t[:2])
                if all(k in self.when for k in t[4])
            ]
            start = {
                t[1]: max([self.when[k] for k in t[4]] + [self.clock]) for t in known
            }
            soonest = min(start.values(), default=1e9)
            due = [self.when[s[4]] for s in self.waiting if s[4] in self.when]
            if due and min(due) <= soonest:
                self.clock = max(self.clock, min(due))
                continue
            chosen = next(t for t in known if start[t[1]] <= soonest + 0.01)
            self.tasks.remove(chosen)
            rank, _, name, cost, needs, makes, work, sends = chosen
            self.clock = begun = start[chosen[1]]
            for key in sorted(self.flying, key=lambda k: self.when[k]):
                if self.when[key] <= self.clock - MARGIN and key not in needs:
                    self.land(key)
            for key in needs:
                if key in self.flying:
                    self.flying.remove(key)
                    if work is None:
                        self.steps.wait(self.box[key])
            if work is not None:
                COST[0] = cost
                out = self.steps(name, work, *[self.box[k] for k in needs])
                self.clock += cost
                self.gap += 1
                for key, b in zip(makes, out, strict=True):
                    self.box[key], self.when[key] = b, self.clock
            LOG.append((name, begun, self.clock, [s[0] for s in sends]))
            self.waiting += sends


    def fetch(self, rank, name, d, masks, axis):
        y, sib = f"{name}.y{d}", f"{name}.sib{d}"
        cut = [f"{name}.cut{i}.{d}" for i in (0, 1)]
        come = [f"{name}.c{i}.{d}" for i in (0, 1)]
        far = [f"{name}.far{i}.{d}" for i in (0, 1)]
        self.task(f"{sib}.send", rank, 0.0, [y], [], None, [(sib, y, "dp", 1)])
        self.task(
            f"{name}.cut{d}",
            rank + 0.01,
            1.3,
            [y],
            cut,
            lambda a: jnp.split(a, 2, axis),
            [(c, k, "dp", m) for c, k, m in zip(come, cut, masks)],
        )
        for c, f in zip(come, far):
            self.task(f, rank, 0.0, [c], [], None, [(f, c, "dp", 1)])
        return [y, sib, *come, *far]


    def reduce(self, rank, name, levels, back=False):
        s = self.mv.n_tensor // 2
        cur = [f"{name}.p{d}" for d in range(2 * s)]
        while s > 1:
            new = [f"{name}.p{d}.{s}" for d in range(s)]
            for d in range(s):
                far = d >= s // 2
                self.task(
                    new[d],
                    rank,
                    1.5,
                    [cur[d], f"{name}.y{d + s}.{s}"],
                    [new[d]],
                    lambda a, b: [add(a, b)],
                    [(f"{name}.y{d}.{s // 2}", new[d], "tensor", s // 2)] * far,
                )
            cur, s = new, s // 2
        needs = [cur[0], f"{name}.y1.1"]
        costs = (2.0, 1.3, 0.9, 0.9, 0.9)
        for i, m in enumerate(levels):
            keep, send, come = f"{name}.k{i}", f"{name}.s{i}", f"{name}.d{i}"

            def work(info, a, b, m=m):
                return add_split(info, m.bit_length() - 1, a, b)

            self.task(
                send,
                rank,
                costs[i],
                ["info", *needs],
                [keep, send],
                work,
                [(come, send, "dp", m)],
            )
            needs = [keep, come]
        own, up = f"{name}.own", list(reversed(levels)) + [1]
        sends = [(f"{name}.u0", own, "dp", up[0])] if back else []
        self.task(own, rank, 0.5, needs, [own], lambda a, b: [add(a, b)], sends)
        for i, m in enumerate(up[:-1] if back else []):
            last = i + 2 == len(up)
            out = f"{name}.mine" if last else f"{name}.j{i}"
            come = f"{name}.other" if last else f"{name}.u{i + 1}"

            def work(a, b, m=m):
                bit = self.mv.bit(m)
                low, high = jnp.where(bit == 0, a, b), jnp.where(bit == 0, b, a)
                return [jnp.concatenate([low, high], axis=0)]

            self.task(
                out,
                rank,
                1.0,
                [own, f"{name}.u{i}"],
                [out],
                work,
                [(come, out, "dp", up[i + 1])],
            )
            own = out

    def gather(self, rank, name, chunks):
        self.task(
            name,
            rank,
            0.8,
            [f"{c}.own" for c in chunks],
            [name],
            lambda *a: [jnp.concatenate(a, axis=0) if len(a) > 1 else a[0]],
            [(f"{name}.all", name, "dp", None)],
        )


def plain(
    n_dp,
    n_tensor,
    x,
    qkv_weight,
    qv_bias,
    out_weight,
    out_bias,
    norm1_gain,
    norm1_shift,
    up_weight,
    up_bias,
    down_weight,
    down_bias,
    norm2_gain,
    norm2_shift,
    lengths,
    grad_output,
):
    width = x.shape[1]

    def whole(w, axis):
        return lax.all_gather(w, "tensor", axis=axis, tiled=True)

    info = jnp.zeros((BITS + 1,), jnp.int32)
    length = lax.dynamic_slice_in_dim(lengths, lax.axis_index("tensor"), 1, 0)
    q_bias, v_bias = whole(qv_bias, 1)
    bias = [q_bias, jnp.zeros_like(q_bias), v_bias, whole(up_bias, 0).astype(F32)]
    bias = jnp.concatenate(bias).reshape(-1, 1, width)
    qkv_w, out_w = whole(qkv_weight, 2), whole(out_weight, 0)
    up_w, down_w = whole(up_weight, 1), whole(down_weight, 0)
    (qkv,) = project(info, x, bias, qkv_w)
    mixed, lse = attend(length, qkv)
    normed, normal1, scale1 = attended(
        info, x, out_bias, norm1_gain, norm1_shift, [mixed], [[out_w]]
    )
    act, slope = widened(info, normed, bias, up_w)
    g2, g_two, result, sums2 = narrowed(
        info,
        normal1,
        norm1_gain,
        norm1_shift,
        down_bias,
        norm2_gain,
        norm2_shift,
        grad_output,
        [act],
        [[down_w]],
    )
    g_up, up_sum = gelu_back(info, g2, slope, down_w)
    g1, g_one, sums1 = attended_back(
        g_two, normal1, scale1, norm1_gain, [g_up], [up_w]
    )
    g_qkv, qkv_sum = attend_back(length, qkv, g1, out_w, lse)
    g_input = input_grad(g_one, [g_qkv], [qkv_w])

    def total(a, axis):
        part = lax.psum_scatter(a, "tensor", scatter_dimension=axis, tiled=True)
        return lax.psum(part, "dp")

    grad_qkv = jnp.stack([contract(x, g_qkv[c], 0, 0) for c in range(3)])
    small = lax.psum(jnp.concatenate([sums1, sums2]), ("dp", "tensor"))
    return (
        result,
        g_input,
        total(grad_qkv, 2),
        total(jnp.stack([qkv_sum[0], qkv_sum[2]]), 1),
        total(contract(mixed, g1, 0, 0), 0),
        small[0],
        small[1],
        small[2],
        total(contract(normed, g_up, 0, 0), 1),
        total(up_sum[0], 0),
        total(contract(act, g2, 0, 0), 0),
        small[3],
        small[4],
        small[5],
    )


def body(
    n_dp,
    n_tensor,
    x,
    qkv_weight,
    qv_bias,
    out_weight,
    out_bias,
    norm1_gain,
    norm1_shift,
    up_weight,
    up_bias,
    down_weight,
    down_bias,
    norm2_gain,
    norm2_shift,
    lengths,
    grad_output,
):
    mv = Moves(n_dp, n_tensor)
    plan = Plan(mv)
    task = plan.task
    parts = range(n_tensor)
    back = list(parts)[::-1]
    width = x.shape[1]
    half = width // 2
    core = mv.core
    hw = qkv_weight.shape[2]
    fw = up_weight.shape[1]
    same = hw == half
    X, Z1, Z = 2, 4, tuple(mv.chip_bits[1:])

    mine_x, mine_z = mv.index((X, 1)), mv.index((Z1, 1))
    place = [mine_x ^ i for i in range(4)] + [4 + (mine_z ^ i) for i in range(4)]
    place += [core, 1 - core, mv.dp]
    place += [mv.bit(m) for m in (1, *mv.chip_bits)]

    plan.given(
        info=jnp.stack(place).astype(jnp.int32),
        lengths=lengths,
        x=x,
        qkv_w0=qkv_weight,
        out_w0=out_weight,
        up_w0=up_weight,
        down_w0=down_weight,
        qv_bias=qv_bias,
        up_bias=up_bias,
        grad_output=grad_output,
    )

    def others(name):
        return [(f"{name}.y{d}", name, "tensor", d) for d in parts[1:]]

    def swap(key):
        return (f"{key}.sib", key, "dp", 1)

    def keys(name):
        return [f"{name}{d}" for d in parts]

    both = (AT, AT + 4)

    def pick_q(info, q):
        return pick(info, [(q, 1, width // 8, both)])

    def pick_ou(info, o, u, _):
        return pick(info, [(o, 0, hw // 2, (CORES,)), (u, 0, width // 8, both)])

    def pick_d(info, d, _):
        return pick(info, [(d, 0, fw // 8, both)])

    task(
        "pick_q",
        0,
        2.8,
        ["info", "qkv_w0"],
        ["q"],
        pick_q,
        [(*s, "bias1") for s in others("q")],
    )
    task(
        "length",
        0.5,
        1.0,
        ["lengths"],
        ["length"],
        lambda n: [lax.dynamic_slice_in_dim(n, lax.axis_index("tensor"), 1, 0)],
    )

    def bias_rows(qv, up):
        q, v = qv[0], qv[1]
        rows = jnp.concatenate([q, jnp.zeros_like(q), v, up.astype(F32)])
        return [rows.reshape(-1, 1, hw)]

    task(
        "bias0",
        -1,
        1.5,
        ["qv_bias", "up_bias"],
        ["bias0"],
        bias_rows,
        [(f"bias{d}", "bias0", "tensor", d) for d in parts[1:]],
    )
    task(
        "pick_ou",
        1.0,
        3.2,
        ["info", "out_w0", "up_w0", "qkv0"],
        ["o", "u"],
        pick_ou,
        [(*s, "q.y1") for s in others("o")] + [(*s, "o.y1") for s in others("u")],
    )
    task(
        "pick_d",
        2.5,
        3.0,
        ["info", "down_w0", "heads0"],
        ["d"],
        pick_d,
        [(*s, "u.y1") for s in others("d")],
    )
    qkv_from, out_from = [["qkv_w0"]], [["out_w0"]]
    up_from, down_from = [["up_w0"]], [["down_w0"]]
    for d in parts[1:]:
        qkv_from.append(plan.fetch(0.2, "q", d, (X, Z1), 1))
        o = f"o.y{d}"
        task(f"o.sib{d}", 0.3, 0.0, [o], [], None, [(f"o.sib{d}", o, "dp", 1)])
        out_from.append([o, f"o.sib{d}"])
        up_from.append(plan.fetch(0.4, "u", d, (X, Z1), 0))
        down_from.append(plan.fetch(0.5, "d", d, (X, Z1), 0))

    for d in parts:
        made = [f"qkv{d}", f"qkv_w{d}"] if d else [f"qkv{d}"]
        task(
            f"project{d}",
            2 + d,
            4.5 if d else 3.5,
            ["info", "x", f"bias{d}", *qkv_from[d]],
            made,
            lambda info, x, b, *w: project(info, x, b, *w),
        )
        task(
            f"heads{d}",
            2 + d,
            6.5,
            ["length", f"qkv{d}"],
            [f"heads{d}", f"lse{d}"],
            attend,
            [],
        )

    def split_args(a, groups):
        out, at = [], 0
        for g in groups:
            out.append(a[at : at + len(g)])
            at += len(g)
        return out

    def attended_task(info, x, *rest):
        mixed, weights = rest[:n_tensor], split_args(rest[n_tensor:], out_from)
        return attended(
            info, x, out_bias, norm1_gain, norm1_shift, mixed, weights
        )

    task(
        "attended",
        20,
        5.0,
        ["info", "x", *keys("heads"), *[k for g in out_from for k in g]],
        ["normed", "normal1", "scale1", *keys("out_w")[1:]],
        attended_task,
        [(*swap("normed"), "u.y1")],
    )
    for d in parts:
        task(
            f"widened{d}",
            21 + d,
            10.0,
            ["info", "normed", f"bias{d}", *up_from[d]],
            [f"act{d}", f"slope{d}"] + [f"up_w{d}"] * (d > 0),
            widened,
            [(*swap(f"act{d}"), "d.y1")],
        )

    def narrowed_task(info, normal1, grad_output, *rest):
        act, weights = rest[:n_tensor], split_args(rest[n_tensor:], down_from)
        low, g_two, result, sums = narrowed(
            info,
            normal1,
            norm1_gain,
            norm1_shift,
            down_bias,
            norm2_gain,
            norm2_shift,
            grad_output,
            act,
            weights,
        )
        return low, g_two, result, sums

    task(
        "narrowed",
        40,
        14.5,
        ["info", "normal1", "grad_output", *keys("act")]
        + [k for g in down_from for k in g],
        ["g2", "g_two", "result", "sums2"],
        narrowed_task,
        [swap("g2")] + [swap(k) for k in ("x", *keys("heads"))],
    )

    block = fw // 4

    def made(name, rank, cost, items, rows, columns, after=None, of=back):
        args = []
        for d in of:
            for a, _, b, _, *_ in items(d):
                args += [a, b, f"{a}.sib", f"{b}.sib"]

        def work(info, *a):
            outs, at = [], 0
            for d in of:
                jobs = []
                for _, ai, _, bi, *rest in items(d):
                    a1, b1, a2, b2 = a[at : at + 4]
                    a1, a2 = ((v if ai is None else (v, ai)) for v in (a1, a2))
                    b1, b2 = ((v if bi is None else (v, bi)) for v in (b1, b2))
                    jobs.append((a1, b1, a2, b2, *rest))
                    at += 4
                outs.append(jobs)
            return grad_stack(info, outs, rows, columns)

        s = n_tensor // 2
        task(
            f"{name}.p{of[0]}",
            rank,
            cost,
            ["info", *args],
            [f"{name}.p{d}" for d in of],
            work,
            [
                (f"{name}.y{d}.{s}", f"{name}.p{d}", "tensor", s, after)
                for d in of
                if d >= s
            ],
        )

    chunks = {}
    first_y = f"{n_tensor // 2}.{n_tensor // 2}"

    def chunk(rank, name, levels, rows, back=False):
        chunks[name] = (levels, rows)
        plan.reduce(rank, name, levels, back)

    made(
        "down",
        51.5,
        9.5,
        lambda d: [(f"act{d}", None, "g2", None, 4, (0,), (0, 1))],
        block,
        half,
    )
    chunk(1.0, "down", (X, *Z), fw)
    for i, d in enumerate(back):
        task(
            f"gelu_back{d}",
            51 + i,
            6.5,
            ["info", "g2", f"slope{d}", *down_from[d]],
            [f"g_up{d}", f"up_sum{d}"],
            gelu_back,
            [(*swap(f"g_up{d}"), None if d else f"down.y{first_y}")],
        )
    for i, of in enumerate((back[: n_tensor // 2], back[n_tensor // 2 :])):
        made(
            "up",
            64 + 4 * i,
            5.5,
            lambda d: [("normed", None, f"g_up{d}", None, 2, (0, 2), (0,))],
            half // 2,
            fw,
            f"down.y{first_y}",
            of,
        )
    chunk(1.2, "up", (X, *Z), half)

    def attended_back_task(g_two, normal, scale, *rest):
        return attended_back(
            g_two, normal, scale, norm1_gain, rest[:n_tensor], rest[n_tensor:]
        )

    task(
        "attended_back",
        56,
        11.5,
        ["g_two", "normal1", "scale1", *keys("g_up"), *keys("up_w")],
        ["g1", "g_one", "sums1"],
        attended_back_task,
        [(*swap("g1"), f"down.y{first_y}")],
    )
    for i, d in enumerate(back):
        task(
            f"heads_back{d}",
            62 + i,
            12.0,
            ["length", f"qkv{d}", "g1", f"out_w{d}", f"lse{d}"],
            [f"g_qkv{d}", f"qkv_sum{d}"],
            attend_back,
            [(*swap(f"g_qkv{d}"), f"down.y{first_y}")],
        )

    def out_item(d):
        return (f"heads{d}", None, "g1", None, 1, (0,), (0, 1))

    def qkv_item(c):
        return lambda d: ("x", None, f"g_qkv{d}", c, 1, (0, 1), (0,))

    if same:
        groups = {"att0": [out_item, qkv_item(2)], "att1": [qkv_item(1), qkv_item(0)]}
    else:
        groups = {"att0": [out_item], "att1": [qkv_item(c) for c in (2, 1, 0)]}
    for i, (name, items) in enumerate(groups.items()):
        rows = hw if items[0] is out_item else half
        made(
            name,
            66 + i,
            7.5,
            lambda d, items=items: [it(d) for it in items],
            rows,
            half if items[0] is out_item else hw,
            f"{('up', 'att0')[i]}.y{first_y}",
        )
        chunk(1.4 + 0.1 * i, name, (X, *Z), rows * len(items), back=True)

    def pack(one, two, *rest):
        packs = []
        for d in parts:
            g, up = rest[2 * d : 2 * d + 2]
            packs.append(
                jnp.concatenate([one.ravel(), two.ravel(), g[0], g[2], up[0]])
            )
        return packs

    needs = [k for d in parts for k in (f"qkv_sum{d}", f"up_sum{d}")]
    packs, s = keys("pack"), n_tensor // 2
    task(
        "pack",
        70,
        3.0,
        ["sums1", "sums2", *needs],
        packs,
        pack,
        [
            (f"pack{d}.y", f"pack{d}", "tensor", s, f"att1.y{first_y}")
            for d in range(s, n_tensor)
        ],
    )
    while s:
        new = [f"small{s}.{d}" for d in range(s)]
        for d in range(s):
            if s > 1:
                sends = [(f"{new[d]}.y", new[d], "tensor", s // 2)] * (d >= s // 2)
            else:
                sends = [("small.1", new[0], "dp", 1)]
            task(
                new[d],
                2.0,
                0.6,
                [packs[d], f"{packs[d + s]}.y"],
                [new[d]],
                lambda a, b: [a + b],
                sends,
            )
        packs, s = new, s // 2
    last, masks = packs[0], [1, *mv.chip_bits]
    for i, m in enumerate(masks):
        out = f"small.at{m}"
        nxt = masks[i + 1] if i + 1 < len(masks) else None
        sends = [(f"small.{nxt}", out, "dp", nxt)] if nxt else []
        task(out, 2.0, 0.6, [last, f"small.{m}"], [out], lambda a, b: [a + b], sends)
        last = out

    task(
        "input_grad",
        80,
        9.0,
        ["g_one", *keys("g_qkv"), *keys("qkv_w")],
        ["g_input"],
        lambda g, *a: [input_grad(g, a[:n_tensor], a[n_tensor:])],
    )

    def results(group, names, outputs):
        plan.gather(1.9, group, names)
        per_device = [chunks[n][1] // (n_dp // 2) for n in names]
        unit = min(per_device)
        total = sum(per_device) // unit
        first = {n: sum(per_device[:i]) // unit for i, n in enumerate(names)}

        def at(c, name, row):
            levels, rows = chunks[name]
            own = rows // (n_dp // 2)
            r, dp = row // own, c
            for i, m in enumerate(reversed(levels)):
                dp |= m * ((r >> i) & 1)
            return dp * total + first[name] + row % own // unit

        for name, cost, blocks, block, shape in outputs:
            tables = [
                ([at(c, n, row + r) for r in range(0, block[0], unit)], place)
                for c, n, row, place in blocks
            ]
            task(
                name,
                85,
                cost,
                [f"{group}.all"],
                [name],
                lambda a, *, rest=(unit, tables, block, shape, name): [
                    spread(a, *rest)
                ],
            )

    results(
        "down_all",
        ("down",),
        [
            (
                "grad_down",
                6.0,
                [(c, "down", r * block, (r, c)) for r in range(4) for c in (0, 1)],
                (block, half),
                (fw, width),
            )
        ],
    )
    rows = half // 4
    results(
        "up_all",
        ("up",),
        [
            (
                "grad_up",
                6.0,
                [
                    (c, "up", r * rows, (4 * c + r, 0))
                    for c in (0, 1)
                    for r in range(4)
                ],
                (rows, fw),
                (width, fw),
            )
        ],
    )

    def sources(*names):
        return [f"{n}.{k}" for n in names for k in ("mine", "other")]

    def cores_result(name, cost, names, blocks, block, shape):
        tables = [
            [(2 * names.index(n) + (c != bit), r, at) for c, n, r, at in blocks]
            for bit in (0, 1)
        ]
        task(
            name,
            85,
            cost,
            sources(*names),
            [name],
            lambda *a: [widen(core, a, block, shape, tables, name)],
        )

    cores_result(
        "grad_out",
        3.0,
        ("att0",),
        [(c, "att0", 0, (0, c)) for c in (0, 1)],
        (hw, half),
        (hw, width),
    )
    place = {2: ("att0", 1), 1: ("att1", 0), 0: ("att1", 1)}
    if not same:
        place = {c: ("att1", 2 - c) for c in range(3)}
    cores_result(
        "grad_qkv",
        5.0,
        ("att0", "att1") if same else ("att1",),
        [(c, *place[i], (i, c, 0)) for i in range(3) for c in (0, 1)],
        (half, hw),
        (3, width, hw),
    )

    plan.run()
    value = {k: b.value for k, b in plan.box.items()}
    small = value[last]
    vec = [small[i * width : (i + 1) * width] for i in range(6)]
    rest = small[6 * width :]
    return (
        value["result"],
        value["g_input"],
        value["grad_qkv"],
        rest[: 2 * hw].reshape(2, hw),
        value["grad_out"],
        vec[0],
        vec[1],
        vec[2],
        value["grad_up"],
        rest[2 * hw :],
        value["grad_down"],
        vec[3],
        vec[4],
        vec[5],
    )


def solution(mesh):
    n_dp, n_tensor = mesh.shape["dp"], mesh.shape["tensor"]
    pairs = n_tensor == 2 and n_dp >= 8 and n_dp & (n_dp - 1) == 0
    return jax.shard_map(
        functools.partial(body if pairs else plain, n_dp, n_tensor),
        mesh=mesh,
        in_specs=(
            P(("dp", "tensor"), None),
            P(None, None, "tensor"),
            P(None, "tensor"),
            P("tensor", None),
            P(),
            P(),
            P(),
            P(None, "tensor"),
            P("tensor"),
            P("tensor", None),
            P(),
            P(),
            P(),
            P("dp"),
            P(("dp", "tensor"), None),
        ),
        out_specs=(
            P(("dp", "tensor"), None),
            P(("dp", "tensor"), None),
            P(None, None, "tensor"),
            P(None, "tensor"),
            P("tensor", None),
            P(),
            P(),
            P(),
            P(None, "tensor"),
            P("tensor"),
            P("tensor", None),
            P(),
            P(),
            P(),
        ),
        check_vma=False,
    )
```

```python
import functools

import jax
import jax.numpy as jnp
import numpy as np
from jax import lax
from jax.experimental import pallas as pl
from jax.experimental.pallas import tpu as pltpu
from jax.sharding import PartitionSpec as P

HD = 64
TENSOR, DATA = "tensor", "dp"
F32 = jnp.float32
BF16 = jnp.bfloat16
NEG = -1000000000.0
SCALE = 0
COST = [0.0]
LOG = []
FLOWN = []
HELD = []


def cost():
    flops = int(SCALE * COST[0] * 1.15e9)
    return pl.CostEstimate(flops=flops, bytes_accessed=0, transcendentals=0)


ERFC_P = 0.3275911
ERFC_C = (
    0.18510853909898187,
    0.17995808540893535,
    0.21032499893163595,
    0.011746556912990477,
    0.4777504794974274,
    -0.4314195259659222,
    0.5110037999525718,
    -0.14447299033990682,
)


def gelu_both(up):
    size = jnp.abs(up)
    t = 1.0 / (1.0 + (ERFC_P * 0.5**0.5) * size)
    poly = jnp.full_like(t, 0.5 * ERFC_C[-1])
    for c in ERFC_C[-2::-1]:
        poly = poly * t + 0.5 * c
    density = jnp.exp(-0.5 * up * up)
    tail = poly * t * density
    phi = jnp.where(up > 0, 1.0 - tail, tail)
    return up * phi, phi + up * (density * 0.3989422804014327)


def contract(a, b, ca, cb):
    return lax.dot_general(a, b, (((ca,), (cb,)), ((), ())), preferred_element_type=F32)


def params(mib):
    return pltpu.CompilerParams(vmem_limit_bytes=mib * 2**20)


def whole_spec(a):
    return pl.BlockSpec(a.shape, lambda *_: (0,) * len(a.shape))


BROUGHT = ((0, 0), (2, 0), (1, 0), (4, 0), (0, 1), (3, 0), (1, 1), (5, 0))


AT, CORES, DP, BITS = 0, 8, 10, 11


def attend_kernel(len_ref, q_ref, k_ref, v_ref, o_ref, lse_ref):
    length = len_ref[0]
    q, k, v = q_ref[0], k_ref[0], v_ref[0]
    rows, width = q.shape
    head = lax.broadcasted_iota(jnp.int32, (rows, width), 1) // HD
    key_pos = lax.broadcasted_iota(jnp.int32, (rows, rows), 0)
    out = None
    for h in range(width // HD):
        mine = head == h
        kh = jnp.where(mine, k, jnp.zeros_like(k)) * jnp.asarray(HD**-0.5, BF16)
        s = jnp.where(key_pos < length, contract(kh, q, 1, 1), F32(NEG))
        top = jnp.max(s, axis=0, keepdims=True)
        e = jnp.exp(s - top)
        total = jnp.sum(e, axis=0, keepdims=True)
        lse_ref[0, h : h + 1, :] = top + jnp.log(total)
        p = (e * (1.0 / total)).astype(BF16)
        o = contract(p, v, 0, 0)
        out = o if out is None else jnp.where(mine, o, out)
    o_ref[...] = out.astype(BF16)


def third(rows, wide, c):
    return pl.BlockSpec((1, rows, wide), lambda i, c=c: (c, 0, i))


def attend(length, qkv):
    _, rows, width = qkv.shape
    wide = min(2 * HD, width)
    steps = width // wide
    return pl.pallas_call(
        attend_kernel,
        grid=(steps,),
        in_specs=[pl.BlockSpec(memory_space=pltpu.SMEM)]
        + [third(rows, wide, c) for c in range(3)],
        out_specs=[
            pl.BlockSpec((rows, wide), lambda i: (0, i)),
            pl.BlockSpec((1, wide // HD, rows), lambda i: (i, 0, 0)),
        ],
        out_shape=[
            jax.ShapeDtypeStruct((rows, width), BF16),
            jax.ShapeDtypeStruct((steps, wide // HD, rows), F32),
        ],
        compiler_params=params(20),
        cost_estimate=cost(),
    )(length, qkv, qkv, qkv)


def attend_back_kernel(
    len_ref, q_ref, k_ref, v_ref, g1_ref, w_ref, lse_ref, d_ref, sum_ref
):
    length = len_ref[0]
    q, k, v = q_ref[0], k_ref[0], v_ref[0]
    g = contract(g1_ref[...], w_ref[...], 1, 1).astype(BF16)
    rows, width = q.shape
    head = lax.broadcasted_iota(jnp.int32, (rows, width), 1) // HD
    head_t = lax.broadcasted_iota(jnp.int32, (width, rows), 0) // HD
    key_pos = lax.broadcasted_iota(jnp.int32, (rows, rows), 0)
    dq = dk = dv = None
    for h in range(width // HD):
        mine = head == h
        kh = jnp.where(mine, k, jnp.zeros_like(k)) * jnp.asarray(HD**-0.5, BF16)
        vh = jnp.where(mine, v, jnp.zeros_like(v))
        s = jnp.where(key_pos < length, contract(kh, q, 1, 1), F32(NEG))
        p = jnp.exp(s - lse_ref[0, h : h + 1, :])
        dp = contract(vh, g, 1, 1)
        dvh = contract(p.astype(BF16), g, 1, 0)
        center = jnp.sum(p * dp, axis=0, keepdims=True)
        ds = (p * (dp - center)).astype(BF16)
        dkh = contract(ds, q, 1, 0)
        dqh = contract(k, ds, 0, 0)
        dv = dvh if dv is None else jnp.where(mine, dvh, dv)
        dk = dkh if dk is None else jnp.where(mine, dkh, dk)
        dq = dqh if dq is None else jnp.where(head_t == h, dqh, dq)
    out = (
        (dq * (HD**-0.5)).T.astype(BF16),
        (dk * (HD**-0.5)).astype(BF16),
        dv.astype(BF16),
    )
    for c in range(3):
        d_ref[c] = out[c]
        sum_ref[c : c + 1, :] = jnp.sum(out[c].astype(F32), axis=0, keepdims=True)


def attend_back(length, qkv, g_one, out_w, lse):
    _, rows, width = qkv.shape
    wide = min(2 * HD, width)
    d = g_one.shape[1]
    return pl.pallas_call(
        attend_back_kernel,
        grid=(width // wide,),
        in_specs=[pl.BlockSpec(memory_space=pltpu.SMEM)]
        + [third(rows, wide, c) for c in range(3)]
        + [
            whole_spec(g_one),
            pl.BlockSpec((wide, d), lambda i: (i, 0)),
            pl.BlockSpec((1, wide // HD, rows), lambda i: (i, 0, 0)),
        ],
        out_specs=[
            pl.BlockSpec((3, rows, wide), lambda i: (0, 0, i)),
            pl.BlockSpec((3, wide), lambda i: (0, i)),
        ],
        out_shape=[
            jax.ShapeDtypeStruct((3, rows, width), BF16),
            jax.ShapeDtypeStruct((3, width), F32),
        ],
        compiler_params=params(28),
        cost_estimate=cost(),
    )(length, qkv, qkv, qkv, g_one, out_w, lse)


def project(at, x, bias, *pieces):
    n = len(pieces)
    rows, depth = x.shape
    width = pieces[0].shape[2]
    size = depth // len(BROUGHT)

    def kernel(at_ref, x_ref, b_ref, *refs):
        w_ref = refs[0]
        if n > 1:
            w_ref = refs[n + 1]
            for i, (k, j) in enumerate(BROUGHT):
                row = pl.multiple_of(at_ref[i] * size, size)
                w_ref[0, pl.ds(row, size)] = refs[k][0, j * size : (j + 1) * size]
        refs[n][0] = (contract(x_ref[...], w_ref[0], 1, 0) + b_ref[0]).astype(BF16)

    out_specs = [pl.BlockSpec((1, rows, width), lambda c, at: (c, 0, 0))]
    out_shape = [jax.ShapeDtypeStruct((3, rows, width), BF16)]
    if n > 1:
        out_specs.append(pl.BlockSpec((1, depth, width), lambda c, at: (c, 0, 0)))
        out_shape.append(jax.ShapeDtypeStruct((3, depth, width), BF16))
    return pl.pallas_call(
        kernel,
        grid_spec=pltpu.PrefetchScalarGridSpec(
            num_scalar_prefetch=1,
            grid=(3,),
            in_specs=[
                whole_spec(x),
                pl.BlockSpec((1, 1, width), lambda c, at: (c, 0, 0)),
            ]
            + [
                pl.BlockSpec((1, p.shape[1], width), lambda c, at: (c, 0, 0))
                for p in pieces
            ],
            out_specs=out_specs,
        ),
        out_shape=out_shape,
        compiler_params=params(20),
        cost_estimate=cost(),
    )(at, x, bias, *pieces)


def norm(hidden):
    center = hidden - jnp.mean(hidden, axis=-1, keepdims=True)
    spread = jnp.mean(center * center, axis=-1, keepdims=True)
    scale = lax.rsqrt(spread + 1e-05)
    return center * scale, scale


def norm_back(grad, normal, scale, gain):
    gy = grad * gain
    mean = jnp.mean(gy, axis=-1, keepdims=True)
    along = jnp.mean(gy * normal, axis=-1, keepdims=True)
    return scale * (gy - mean - normal * along)


def attended(at, x, bias, gain, shift, mixed, weights):
    rows, d = x.shape
    step = min(128, rows)
    cut = [i for i, w in enumerate(weights) if len(w) > 1]
    flat = [p for w in weights for p in w]
    n = len(mixed)

    def kernel(at_ref, x_ref, b_ref, g_ref, s_ref, *refs):
        m, w = refs[:n], refs[n : n + len(flat)]
        low_ref, normal_ref, scale_ref = refs[n + len(flat) :][:3]
        outs = refs[n + len(flat) + 3 :]
        k = j = 0
        total = x_ref[...].astype(F32) + b_ref[...]
        for i, ps in enumerate(weights):
            if len(ps) > 1:
                size = ps[0].shape[0]
                held = outs[j]

                @pl.when(pl.program_id(0) == 0)
                def _(held=held, k=k, ps=ps, size=size):
                    for q in range(len(ps)):
                        row = pl.multiple_of(at_ref[CORES + q] * size, size)
                        held[pl.ds(row, size), :] = w[k + q][...]

                value = held[...]
                j += 1
            else:
                value = w[k][...]
            k += len(ps)
            total = total + contract(m[i][...], value, 1, 0)
        normal, scale = norm(total)
        normal_ref[...] = normal
        scale_ref[...] = scale
        low_ref[...] = (normal * g_ref[...] + s_ref[...]).astype(BF16)

    row = pl.BlockSpec((step, d), lambda i, at: (i, 0))
    out_specs = [row, row, pl.BlockSpec((step, 1), lambda i, at: (i, 0))]
    out_shape = [
        jax.ShapeDtypeStruct((rows, d), BF16),
        jax.ShapeDtypeStruct((rows, d), F32),
        jax.ShapeDtypeStruct((rows, 1), F32),
    ]
    for i in cut:
        out_shape.append(
            jax.ShapeDtypeStruct((len(weights[i]) * weights[i][0].shape[0], d), BF16)
        )
        out_specs.append(whole_spec(out_shape[-1]))
    vecs = [v.reshape(1, d) for v in (bias, gain, shift)]
    return pl.pallas_call(
        kernel,
        grid_spec=pltpu.PrefetchScalarGridSpec(
            num_scalar_prefetch=1,
            grid=(rows // step,),
            in_specs=[row]
            + [whole_spec(v) for v in vecs]
            + [pl.BlockSpec((step, m.shape[1]), lambda i, at: (i, 0)) for m in mixed]
            + [whole_spec(p) for p in flat],
            out_specs=out_specs,
        ),
        out_shape=out_shape,
        compiler_params=params(20),
        cost_estimate=cost(),
    )(at, x, *vecs, *mixed, *flat)


def widened(at, low, bias, *pieces):
    rows, d = low.shape
    n = len(pieces)
    size, width = d // len(BROUGHT), pieces[0].shape[1]
    block, sub = bias.shape[2], min(128, rows)

    def kernel(at_ref, x_ref, b_ref, *refs):
        act_ref, slope_ref = refs[n : n + 2]
        w_ref = refs[0]
        if n > 1:
            w_ref = refs[n + 2]
            for i, (k, j) in enumerate(BROUGHT):
                row = pl.multiple_of(at_ref[i] * size, size)
                w_ref[pl.ds(row, size), :] = refs[k][j * size : (j + 1) * size, :]
        for i in range(0, rows, sub):
            up = contract(x_ref[i : i + sub, :], w_ref[...], 1, 0) + b_ref[0]
            act, slope = gelu_both(up)
            act_ref[i : i + sub, :] = act.astype(BF16)
            slope_ref[i : i + sub, :] = slope.astype(BF16)

    out = jax.ShapeDtypeStruct((rows, width), BF16)
    out_shape = [out, out]
    if n > 1:
        out_shape.append(jax.ShapeDtypeStruct((d, width), BF16))
    return pl.pallas_call(
        kernel,
        grid_spec=pltpu.PrefetchScalarGridSpec(
            num_scalar_prefetch=1,
            grid=(width // block,),
            in_specs=[
                whole_spec(low),
                pl.BlockSpec((1, 1, block), lambda i, at: (3 + i, 0, 0)),
            ]
            + [pl.BlockSpec((p.shape[0], block), lambda i, at: (0, i)) for p in pieces],
            out_specs=[
                pl.BlockSpec((o.shape[0], block), lambda i, at: (0, i))
                for o in out_shape
            ],
        ),
        out_shape=out_shape,
        compiler_params=params(24),
        cost_estimate=cost(),
    )(at, low, bias, *pieces)


def narrowed(at, normal1, gain1, shift1, bias, gain, shift, grad_output, act, weights):
    rows, d = normal1.shape
    block = 256
    steps = d // block
    flat = [p for w in weights for p in w]
    cut = [w for w in weights if len(w) > 1]
    n = len(act)

    def kernel(at_ref, nm_ref, g1_ref, s1_ref, b_ref, g_ref, s_ref, go_ref, *refs):
        a, w = refs[:n], refs[n : n + len(flat)]
        low_ref, grad_ref, result_ref, sum_ref, acc = refs[n + len(flat) :][:5]
        held = list(refs[n + len(flat) + 5 :])
        total = nm_ref[...] * g1_ref[...] + s1_ref[...] + b_ref[...]
        k = 0
        for i, ps in enumerate(weights):
            value = w[k]
            if len(ps) > 1:
                value = held.pop(0)
                size = value.shape[0] // len(BROUGHT)
                for q, (m, j) in enumerate(BROUGHT):
                    row = pl.multiple_of(at_ref[q] * size, size)
                    value[pl.ds(row, size), :] = w[k + m][j * size : (j + 1) * size, :]
            total = total + contract(a[i][...], value[...], 1, 0)
            k += len(ps)
        acc[pl.program_id(0)] = total

        @pl.when(pl.program_id(0) == steps - 1)
        def _():
            sums = [jnp.zeros((1, d), F32) for _ in range(3)]
            for r in range(0, rows, 64):
                cut = slice(r, r + 64)
                hidden = jnp.concatenate([acc[i, cut, :] for i in range(steps)], axis=1)
                normal, scale = norm(hidden)
                result_ref[cut, :] = (normal * g_ref[...] + s_ref[...]).astype(BF16)
                grad = go_ref[cut, :].astype(F32)
                g_two = norm_back(grad, normal, scale, g_ref[...])
                grad_ref[cut, :] = g_two
                low_ref[cut, :] = g_two.astype(BF16)
                for j, v in enumerate((g_two, grad * normal, grad)):
                    sums[j] = sums[j] + jnp.sum(v, axis=0, keepdims=True)
            for j in range(3):
                sum_ref[j : j + 1, :] = sums[j]

    def col(rows):
        return pl.BlockSpec((rows, block), lambda s, at: (0, s))

    vecs = [v.reshape(1, d) for v in (gain1, shift1, bias, gain, shift)]
    out_shape = [
        jax.ShapeDtypeStruct((rows, d), BF16),
        jax.ShapeDtypeStruct((rows, d), F32),
        jax.ShapeDtypeStruct((rows, d), BF16),
        jax.ShapeDtypeStruct((3, d), F32),
    ]
    return pl.pallas_call(
        kernel,
        grid_spec=pltpu.PrefetchScalarGridSpec(
            num_scalar_prefetch=1,
            grid=(steps,),
            in_specs=[col(rows), col(1), col(1), col(1)]
            + [whole_spec(v) for v in vecs[3:]]
            + [whole_spec(grad_output)]
            + [whole_spec(a) for a in act]
            + [col(p.shape[0]) for p in flat],
            out_specs=[whole_spec(o) for o in out_shape],
            scratch_shapes=[pltpu.VMEM((steps, rows, block), F32)]
            + [pltpu.VMEM((act[0].shape[1], block), BF16) for _ in cut],
        ),
        out_shape=out_shape,
        compiler_params=params(32 if cut else 48),
        cost_estimate=cost(),
    )(at, normal1, *vecs, grad_output, *act, *flat)


def gelu_back(at, g, slope, *pieces):
    rows, d = g.shape
    width = slope.shape[1]
    n = len(pieces)
    size = min(512, width)

    def kernel(at_ref, g_ref, s_ref, *refs):
        out_ref, sum_ref = refs[n : n + 2]
        w = refs[0][...]
        if n > 1:
            held, cut = refs[n + 2], width // len(BROUGHT)

            @pl.when(pl.program_id(0) == 0)
            def _():
                for i, (k, j) in enumerate(BROUGHT):
                    row = pl.multiple_of(at_ref[i] * cut, cut)
                    held[pl.ds(row, cut), :] = refs[k][j * cut : (j + 1) * cut, :]

            w = held[pl.ds(pl.multiple_of(pl.program_id(0) * size, size), size), :]
        low = (contract(g_ref[...], w, 1, 1) * s_ref[...].astype(F32)).astype(BF16)
        out_ref[...] = low
        sum_ref[...] = jnp.sum(low.astype(F32), axis=0, keepdims=True)

    def column(rows):
        return pl.BlockSpec((rows, size), lambda s, at: (0, s))

    w_specs = [pl.BlockSpec((size, d), lambda s, at: (s, 0))]
    return pl.pallas_call(
        kernel,
        grid_spec=pltpu.PrefetchScalarGridSpec(
            num_scalar_prefetch=1,
            grid=(width // size,),
            in_specs=[whole_spec(g), column(rows)]
            + ([whole_spec(p) for p in pieces] if n > 1 else w_specs),
            out_specs=[column(rows), column(1)],
            scratch_shapes=[pltpu.VMEM((width, d), BF16)] if n > 1 else [],
        ),
        out_shape=[
            jax.ShapeDtypeStruct((rows, width), BF16),
            jax.ShapeDtypeStruct((1, width), F32),
        ],
        compiler_params=params(24),
        cost_estimate=cost(),
    )(at, g, slope, *pieces)


def attended_back(g_two, normal, scale, gain, g_up, up_w):
    rows, d = g_two.shape
    block = 256
    steps, n = d // block, len(g_up)

    def kernel(g2_ref, nm_ref, sc_ref, gain_ref, *refs):
        g, w = refs[:n], refs[n : 2 * n]
        low_ref, grad_ref, sum_ref, acc = refs[2 * n :]
        total = g2_ref[...]
        for i in range(n):
            total = total + contract(g[i][...], w[i][...], 1, 1)
        acc[pl.program_id(0)] = total

        @pl.when(pl.program_id(0) == steps - 1)
        def _():
            sums = [jnp.zeros((1, d), F32) for _ in range(3)]
            for r in range(0, rows, 64):
                cut = slice(r, r + 64)
                g_in = jnp.concatenate([acc[i, cut, :] for i in range(steps)], axis=1)
                nm = nm_ref[cut, :]
                g_one = norm_back(g_in, nm, sc_ref[cut, :], gain_ref[...])
                grad_ref[cut, :] = g_one
                low_ref[cut, :] = g_one.astype(BF16)
                for j, v in enumerate((g_one, g_in * nm, g_in)):
                    sums[j] = sums[j] + jnp.sum(v, axis=0, keepdims=True)
            for j in range(3):
                sum_ref[j : j + 1, :] = sums[j]

    out_shape = [
        jax.ShapeDtypeStruct((rows, d), BF16),
        jax.ShapeDtypeStruct((rows, d), F32),
        jax.ShapeDtypeStruct((3, d), F32),
    ]
    gain = gain.reshape(1, d)
    return pl.pallas_call(
        kernel,
        grid=(steps,),
        in_specs=[pl.BlockSpec((rows, block), lambda s: (0, s))]
        + [whole_spec(a) for a in (normal, scale, gain, *g_up)]
        + [pl.BlockSpec((block, w.shape[1]), lambda s: (s, 0)) for w in up_w],
        out_specs=[whole_spec(o) for o in out_shape],
        out_shape=out_shape,
        scratch_shapes=[pltpu.VMEM((steps, rows, block), F32)],
        compiler_params=params(28 if n > 1 else 48),
        cost_estimate=cost(),
    )(g_two, normal, scale, gain, *g_up, *up_w)


def input_grad(g_one, g_proj, qkv_w):
    rows, d = g_one.shape
    width, n = g_proj[0].shape[2], len(g_proj)
    block = 256

    def kernel(g1_ref, *refs):
        g, w, out_ref = refs[:n], refs[n : 2 * n], refs[-1]
        total = g1_ref[...]
        for i in range(n):
            for c in range(3):
                total = total + contract(g[i][c], w[i][c], 1, 1)
        out_ref[...] = total

    col = pl.BlockSpec((rows, block), lambda s: (0, s))
    return pl.pallas_call(
        kernel,
        grid=(d // block,),
        in_specs=[col]
        + [whole_spec(g) for g in g_proj]
        + [pl.BlockSpec((3, block, width), lambda s: (0, s, 0))] * n,
        out_specs=col,
        out_shape=jax.ShapeDtypeStruct((rows, d), F32),
        compiler_params=params(24),
        cost_estimate=cost(),
    )(g_one, *g_proj, *qkv_w)


def pick(index, pieces):
    n = len(pieces)
    views = [(i, j) for i, p in enumerate(pieces) for j in range(len(p[3]))]

    def kernel(index_ref, *refs):
        for v, (i, j) in enumerate(views):
            axis, size = pieces[i][1:3]
            at = tuple([slice(None)] * axis + [slice(j * size, (j + 1) * size)])
            refs[len(views) + i][at] = refs[v][...]

    specs, shapes = [], []
    for i, j in views:
        a, axis, size, places = pieces[i]
        specs.append(
            pl.BlockSpec(
                a.shape[:axis] + (size,) + a.shape[axis + 1 :],
                lambda s, at, p=places[j], axis=axis, n=a.ndim: tuple(
                    at[p] if k == axis else 0 for k in range(n)
                ),
            )
        )
    for a, axis, size, places in pieces:
        shape = a.shape[:axis] + (size * len(places),) + a.shape[axis + 1 :]
        shapes.append(jax.ShapeDtypeStruct(shape, a.dtype))
    return pl.pallas_call(
        kernel,
        grid_spec=pltpu.PrefetchScalarGridSpec(
            num_scalar_prefetch=1,
            grid=(1,),
            in_specs=specs,
            out_specs=[whole_spec(s) for s in shapes],
        ),
        out_shape=shapes,
        compiler_params=params(60),
        cost_estimate=cost(),
    )(index, *[pieces[i][0] for i, _ in views])


def add(a, b):
    return (a.astype(F32) + b.astype(F32)).astype(BF16)


def add_split(bits, which, a, b):
    rows, columns = a.shape
    half = rows // 2
    if half % 16:
        total, bit = add(a, b), bits[BITS + which]
        return (
            lax.dynamic_slice_in_dim(total, bit * half, half, 0),
            lax.dynamic_slice_in_dim(total, (1 - bit) * half, half, 0),
        )
    block = half // 2 if half >= 256 else half
    per = half // block

    def kernel(bits_ref, a0, b0, a1, b1, keep_ref, send_ref):
        send_ref[...] = add(a1[...], b1[...])
        keep_ref[...] = add(a0[...], b0[...])

    def spec(of):
        return pl.BlockSpec((block, columns), lambda s, bits: (of(s, bits), 0))

    kept = spec(lambda s, bits: bits[BITS + which] * per + s)
    sent = spec(lambda s, bits: (1 - bits[BITS + which]) * per + s)
    plain = spec(lambda s, bits: s)
    out = jax.ShapeDtypeStruct((half, columns), BF16)
    return pl.pallas_call(
        kernel,
        grid_spec=pltpu.PrefetchScalarGridSpec(
            num_scalar_prefetch=1,
            grid=(per,),
            in_specs=[kept, kept, sent, sent],
            out_specs=[plain, plain],
        ),
        out_shape=[out, out],
        compiler_params=params(12),
        cost_estimate=cost(),
    )(bits, a, b, a, b)


def grad_stack(bits, outs, rows, width):
    jobs = [job for out in outs for job in out]
    sizes = [sum(job[4] for job in out) for out in outs]

    def depth_of(a):
        a = a[0] if isinstance(a, tuple) else a
        return a.shape[-2]

    depth = depth_of(jobs[0][0])
    total = sum(sizes)

    def kernel(bits_ref, *refs):
        s = pl.program_id(0)
        at = first = 0
        j = 0
        for o, out in enumerate(outs):
            for job in out:

                @pl.when((s >= at) & (s < at + job[4]))
                def _(j=j, o=o):
                    x1, y1, x2, y2 = (
                        r[0] if len(r.shape) == 3 else r[...]
                        for r in refs[4 * j : 4 * j + 4]
                    )
                    value = contract(x1, y1, 0, 0) + contract(x2, y2, 0, 0)
                    refs[4 * len(jobs) + o][...] = value.astype(BF16)

                at += job[4]
                j += 1

    def column(place, bits):
        return place[0] + sum(k * bits[BITS + i] for i, k in enumerate(place[1:]) if k)

    def spec(a, block, of):
        if isinstance(a, tuple):
            return pl.BlockSpec((1, *block), lambda s, bits: (a[1], 0, of(s, bits)))
        return pl.BlockSpec(block, lambda s, bits: (0, of(s, bits)))

    specs, args, at = [], [], 0
    for a1, b1, a2, b2, n, a_at, b_at in jobs:

        def a_of(s, bits, at=at, n=n, p=a_at):
            return column(p, bits) + jnp.clip(s - at, 0, n - 1)

        def b_of(s, bits, p=b_at):
            return column(p, bits)

        for a, b in ((a1, b1), (a2, b2)):
            specs += [spec(a, (depth, rows), a_of), spec(b, (depth, width), b_of)]
            args += [a, b]
        at += n
    out_specs, at = [], 0
    for size in sizes:
        out_specs.append(
            pl.BlockSpec(
                (rows, width),
                lambda s, bits, at=at, n=size: (jnp.clip(s - at, 0, n - 1), 0),
            )
        )
        at += size
    return pl.pallas_call(
        kernel,
        grid_spec=pltpu.PrefetchScalarGridSpec(
            num_scalar_prefetch=1, grid=(total,), in_specs=specs, out_specs=out_specs
        ),
        out_shape=[jax.ShapeDtypeStruct((n * rows, width), BF16) for n in sizes],
        compiler_params=params(24),
        cost_estimate=cost(),
    )(bits, *[a[0] if isinstance(a, tuple) else a for a in args])


class Box:
    def __init__(self, value):
        self.value = value


class Steps:
    def __init__(self):
        self.kept = []

    def keep(self, value):
        self.kept.append(Box(value))
        return self.kept[-1]

    def fence(self):
        held = lax.optimization_barrier(tuple(b.value for b in self.kept))
        for b, value in zip(self.kept, held):
            b.value = value

    def __call__(self, name, work, *ins):
        self.fence()
        with jax.named_scope(name):
            out = work(*[b.value for b in ins])
        out = [self.keep(v) for v in jax.tree.leaves(out)]
        self.fence()
        return out

    def wait(self, flight):
        self.kept.append(flight)
        self.fence()


class Moves:
    def __init__(self, n_dp, n_tensor):
        self.n_dp, self.n_tensor = n_dp, n_tensor
        self.dp = lax.axis_index(DATA)
        self.core = self.dp & 1
        self.chip_bits = [b for b in (2, 4, 8, 16, 32, 64) if b < n_dp]

    def bit(self, mask):
        return (self.dp // mask) & 1

    def index(self, masks):
        return sum(self.bit(m) << i for i, m in enumerate(masks))

    def over(self, a, axis, mask, name):
        with jax.named_scope(name):
            n = self.n_dp if axis == DATA else self.n_tensor
            return Box(lax.ppermute(a.value, axis, [(i, i ^ mask) for i in range(n)]))


def widen(core, sources, block, out_shape, steps, name):
    n, count = len(sources), len(steps[0])
    tables = []
    for bit in (0, 1):
        rows = np.zeros((n + 1 + len(out_shape), count), np.int32)
        for q in range(n):
            used = [s for s in range(count) if steps[bit][s][0] == q]
            for s in range(count):
                later = [u for u in used if u >= s]
                at = later[0] if later else used[-1]
                rows[q, s] = steps[bit][at][1]
        for s in range(count):
            rows[n, s] = steps[bit][s][0]
            rows[n + 1 :, s] = steps[bit][s][2]
        tables.append(rows)
    table = jnp.where(core == 0, jnp.asarray(tables[0]), jnp.asarray(tables[1]))

    def kernel(table_ref, *refs):
        s = pl.program_id(0)
        for q in range(n):

            @pl.when(table_ref[n, s] == q)
            def _():
                refs[n][...] = refs[q][...].astype(F32).reshape(refs[n].shape)

    lead = len(out_shape) - 2
    return pl.pallas_call(
        kernel,
        grid_spec=pltpu.PrefetchScalarGridSpec(
            num_scalar_prefetch=1,
            grid=(count,),
            in_specs=[
                pl.BlockSpec(block, lambda s, t, q=q: (t[q, s], 0)) for q in range(n)
            ],
            out_specs=pl.BlockSpec(
                (1,) * lead + block,
                lambda s, t: tuple(t[n + 1 + j, s] for j in range(len(out_shape))),
            ),
        ),
        out_shape=jax.ShapeDtypeStruct(out_shape, F32),
        compiler_params=params(24),
        cost_estimate=cost(),
        name=name,
    )(table, *sources)


def spread(gathered, unit, tables, block, out_shape, name):
    count, views = len(tables), len(tables[0][0])
    columns = gathered.shape[-1]
    lead = len(out_shape) - 2
    table = np.asarray([list(t[0]) + list(t[1]) for t in tables], np.int32).T

    def kernel(table_ref, *refs):
        out = refs[views]
        for v in range(views):
            part = refs[v][0].astype(F32)
            if lead:
                out[0, v * unit : (v + 1) * unit, :] = part
            else:
                out[v * unit : (v + 1) * unit, :] = part

    return pl.pallas_call(
        kernel,
        grid_spec=pltpu.PrefetchScalarGridSpec(
            num_scalar_prefetch=1,
            grid=(count,),
            in_specs=[
                pl.BlockSpec((1, unit, columns), lambda s, t, v=v: (t[v, s], 0, 0))
                for v in range(views)
            ],
            out_specs=pl.BlockSpec(
                (1,) * lead + block,
                lambda s, t: tuple(t[views + j, s] for j in range(len(out_shape))),
            ),
        ),
        out_shape=jax.ShapeDtypeStruct(out_shape, F32),
        compiler_params=params(40),
        cost_estimate=cost(),
        name=name,
    )(jnp.asarray(table), *[gathered.reshape(-1, unit, columns)] * views)


START, LATENCY = 1.5, 2.5
RATES = {"y": 46.5e3, "x": 46.5e3, "z": 46.5e3, "core": 500e3}
GATHER = 52.0
FLIGHTS = 5
MARGIN, PATIENCE, EARLY = 4.0, 8.0, 2.0


class Plan:
    def __init__(self, mv):
        self.mv, self.steps = mv, Steps()
        self.box, self.when, self.free = {}, {}, {}
        self.tasks, self.flying, self.waiting = [], [], []
        self.clock, self.gap, self.sent, self.flown = 0.0, 0, {}, {}
        LOG.clear()
        FLOWN.clear()

    def given(self, **arrays):
        for key, value in arrays.items():
            self.box[key], self.when[key] = self.steps.keep(value), 0.0

    def task(self, name, rank, cost, needs, makes, work, sends=()):
        self.tasks.append((rank, len(self.tasks), name, cost, needs, makes, work, sends))

    def link(self, axis, mask):
        if axis == TENSOR:
            return "y", mask
        if mask < 4:
            return ("core", "x")[mask // 2], 1
        return "z", mask // 4

    def send(self, new, key, axis, mask):
        a = self.box[key]
        if mask is None:
            with jax.named_scope(new):
                self.box[new] = Box(lax.all_gather(a.value, axis))
            self.clock += 0.7
            self.free["sc"] = max(self.free.get("sc", 0.0), self.clock) + GATHER
            self.when[new] = self.free["sc"]
            return
        while len(self.flying) >= FLIGHTS:
            self.land(min(self.flying, key=lambda k: self.when[k]))
        self.box[new] = self.mv.over(a, axis, mask, new)
        link, often = self.link(axis, mask)
        took = often * a.value.size * a.value.dtype.itemsize / RATES[link]
        self.clock += 0.5 if link == "core" else START
        self.free[link] = max(self.free.get(link, 0.0), self.clock) + took
        self.when[new] = self.free[link] + (1.0 if link == "core" else LATENCY)
        self.flying.append(new)
        self.sent[new] = (self.gap,)
        self.flown[new] = (a.value.size * a.value.dtype.itemsize, link, took)
        FLOWN.append((new, self.clock, self.when[new]))

    def send_due(self):
        for s in list(self.waiting):
            after = s[4] if len(s) > 4 else None
            if after and not (after in self.when and self.when[after] <= self.clock):
                continue
            if after in self.flying:
                self.land(after)
            self.waiting.remove(s)
            value = self.box[s[1]].value
            size = 1e9 if s[3] is None else value.size * value.dtype.itemsize
            held = [
                k
                for k in self.flying
                if self.sent[k][0] < self.gap and self.flown[k][0] <= size
            ]
            for k in [k for k in held if self.when[k] <= self.clock + PATIENCE]:
                self.land(k)
                held.remove(k)
            for k in held:
                self.free[self.flown[k][1]] = max(
                    [self.clock]
                    + [
                        self.when[j] - LATENCY
                        for j in self.flying
                        if j not in held and self.flown[j][1] == self.flown[k][1]
                    ]
                )
            self.send(*s[:4])
            for k in held:
                if k in self.flying:
                    _, link, took = self.flown[k]
                    self.sent[k] = (self.gap,)
                    self.free[link] = max(self.free[link], self.clock) + took
                    self.when[k] = self.free[link] + LATENCY
                    HELD.append((k, s[0]))

    def land(self, key):
        self.flying.remove(key)
        self.steps.wait(self.box[key])
        if self.when[key] > self.clock:
            self.clock = self.when[key]
            self.gap += 1

    def run(self):
        while self.tasks:
            self.send_due()
            known = [
                t
                for t in sorted(self.tasks, key=lambda t: t[:2])
                if all(k in self.when for k in t[4])
            ]
            start = {
                t[1]: max([self.when[k] for k in t[4]] + [self.clock]) for t in known
            }
            soonest = min(start.values(), default=1e9)
            due = [self.when[s[4]] for s in self.waiting if s[4] in self.when]
            if due and min(due) <= soonest:
                if min(due) > self.clock:
                    self.clock = min(due)
                    self.gap += 1
                continue
            ready = [t for t in known if start[t[1]] <= soonest + 0.01]
            chosen = ready[0]
            soon = min((t for t in due if t > soonest), default=1e9)
            if soonest + chosen[3] > soon + EARLY:
                fits = [t for t in ready if soonest + t[3] <= soon + EARLY]
                if not fits:
                    self.clock = soon
                    self.gap += 1
                    continue
                chosen = fits[0]
            self.tasks.remove(chosen)
            rank, _, name, cost, needs, makes, work, sends = chosen
            if start[chosen[1]] > self.clock:
                self.gap += 1
            self.clock = begun = start[chosen[1]]
            for key in sorted(self.flying, key=lambda k: self.when[k]):
                if self.when[key] <= self.clock - MARGIN and key not in needs:
                    self.land(key)
            for key in needs:
                if key in self.flying:
                    self.flying.remove(key)
                    if work is None:
                        self.steps.wait(self.box[key])
                        self.gap += 1
            if work is not None:
                COST[0] = cost
                out = self.steps(name, work, *[self.box[k] for k in needs])
                self.clock += cost
                self.gap += 1
                for key, b in zip(makes, out, strict=True):
                    self.box[key], self.when[key] = b, self.clock
            LOG.append((name, begun, self.clock, [s[0] for s in sends]))
            self.waiting += sends


    def fetch(self, rank, name, d, masks, axis):
        y, sib = f"{name}.y{d}", f"{name}.sib{d}"
        cut = [f"{name}.cut{i}.{d}" for i in (0, 1)]
        come = [f"{name}.c{i}.{d}" for i in (0, 1)]
        far = [f"{name}.far{i}.{d}" for i in (0, 1)]
        self.task(f"{sib}.send", rank, 0.0, [y], [], None, [(sib, y, DATA, 1)])
        self.task(
            f"{name}.cut{d}",
            rank + 0.01,
            0.4,
            [y],
            cut,
            lambda a: jnp.split(a, 2, axis),
            [(c, k, DATA, m) for c, k, m in zip(come, cut, masks)],
        )
        for c, f in zip(come, far):
            self.task(f, rank, 0.0, [c], [], None, [(f, c, DATA, 1)])
        return [y, sib, *come, *far]


    def reduce(self, rank, name, levels, back=False):
        s = self.mv.n_tensor // 2
        cur = [f"{name}.p{d}" for d in range(2 * s)]
        while s > 1:
            new = [f"{name}.p{d}.{s}" for d in range(s)]
            for d in range(s):
                far = d >= s // 2
                self.task(
                    new[d],
                    rank,
                    1.5,
                    [cur[d], f"{name}.y{d + s}.{s}"],
                    [new[d]],
                    lambda a, b: [add(a, b)],
                    [(f"{name}.y{d}.{s // 2}", new[d], TENSOR, s // 2)] * far,
                )
            cur, s = new, s // 2
        needs = [cur[0], f"{name}.y1.1"]
        costs = (2.0, 1.3, 0.9, 0.9, 0.9)
        for i, m in enumerate(levels):
            keep, send, come = f"{name}.k{i}", f"{name}.s{i}", f"{name}.d{i}"

            def work(info, a, b, m=m):
                return add_split(info, m.bit_length() - 1, a, b)

            self.task(
                send,
                rank,
                costs[i],
                ["i", *needs],
                [keep, send],
                work,
                [(come, send, DATA, m)],
            )
            needs = [keep, come]
        own, up = f"{name}.own", list(reversed(levels)) + [1]
        sends = [(f"{name}.u0", own, DATA, up[0])] if back else []
        self.task(own, rank, 0.5, needs, [own], lambda a, b: [add(a, b)], sends)
        for i, m in enumerate(up[:-1] if back else []):
            last = i + 2 == len(up)
            out = f"{name}.mine" if last else f"{name}.j{i}"
            come = f"{name}.other" if last else f"{name}.u{i + 1}"

            def work(a, b, m=m):
                bit = self.mv.bit(m)
                low, high = jnp.where(bit == 0, a, b), jnp.where(bit == 0, b, a)
                return [jnp.concatenate([low, high], axis=0)]

            self.task(
                out,
                rank,
                1.0,
                [own, f"{name}.u{i}"],
                [out],
                work,
                [(come, out, DATA, up[i + 1])],
            )
            own = out

    def gather(self, rank, name, chunks, after):
        self.task(
            name,
            rank,
            0.8,
            [f"{c}.own" for c in chunks],
            [name],
            lambda *a: [jnp.concatenate(a, axis=0) if len(a) > 1 else a[0]],
            [(f"{name}.all", name, DATA, None, after)],
        )


def plain(
    n_dp,
    n_tensor,
    x,
    qkv_weight,
    qv_bias,
    out_weight,
    out_bias,
    norm1_gain,
    norm1_shift,
    up_weight,
    up_bias,
    down_weight,
    down_bias,
    norm2_gain,
    norm2_shift,
    lengths,
    grad_output,
):
    width = x.shape[1]

    def whole(w, axis):
        return lax.all_gather(w, TENSOR, axis=axis, tiled=True)

    info = jnp.zeros((BITS + 1,), jnp.int32)
    length = lax.dynamic_slice_in_dim(lengths, lax.axis_index(TENSOR), 1, 0)
    q_bias, v_bias = whole(qv_bias, 1)
    bias = [q_bias, jnp.zeros_like(q_bias), v_bias, whole(up_bias, 0).astype(F32)]
    bias = jnp.concatenate(bias).reshape(-1, 1, width)
    qkv_w, out_w = whole(qkv_weight, 2), whole(out_weight, 0)
    up_w, down_w = whole(up_weight, 1), whole(down_weight, 0)
    (qkv,) = project(info, x, bias, qkv_w)
    mixed, lse = attend(length, qkv)
    normed, normal1, scale1 = attended(
        info, x, out_bias, norm1_gain, norm1_shift, [mixed], [[out_w]]
    )
    act, slope = widened(info, normed, bias, up_w)
    g2, g_two, result, sums2 = narrowed(
        info,
        normal1,
        norm1_gain,
        norm1_shift,
        down_bias,
        norm2_gain,
        norm2_shift,
        grad_output,
        [act],
        [[down_w]],
    )
    g_up, up_sum = gelu_back(info, g2, slope, down_w)
    g1, g_one, sums1 = attended_back(
        g_two, normal1, scale1, norm1_gain, [g_up], [up_w]
    )
    g_qkv, qkv_sum = attend_back(length, qkv, g1, out_w, lse)
    g_input = input_grad(g_one, [g_qkv], [qkv_w])

    def total(a, axis):
        part = lax.psum_scatter(a, TENSOR, scatter_dimension=axis, tiled=True)
        return lax.psum(part, DATA)

    grad_qkv = jnp.stack([contract(x, g_qkv[c], 0, 0) for c in range(3)])
    small = lax.psum(jnp.concatenate([sums1, sums2]), (DATA, TENSOR))
    return (
        result,
        g_input,
        total(grad_qkv, 2),
        total(jnp.stack([qkv_sum[0], qkv_sum[2]]), 1),
        total(contract(mixed, g1, 0, 0), 0),
        small[0],
        small[1],
        small[2],
        total(contract(normed, g_up, 0, 0), 1),
        total(up_sum[0], 0),
        total(contract(act, g2, 0, 0), 0),
        small[3],
        small[4],
        small[5],
    )


def body(
    n_dp,
    n_tensor,
    x,
    qkv_weight,
    qv_bias,
    out_weight,
    out_bias,
    norm1_gain,
    norm1_shift,
    up_weight,
    up_bias,
    down_weight,
    down_bias,
    norm2_gain,
    norm2_shift,
    lengths,
    grad_output,
):
    mv = Moves(n_dp, n_tensor)
    plan = Plan(mv)
    task = plan.task
    parts = range(n_tensor)
    back = list(parts)[::-1]
    width = x.shape[1]
    half = width // 2
    core = mv.core
    hw = qkv_weight.shape[2]
    fw = up_weight.shape[1]
    same = hw == half
    X, Z1, Z = 2, 4, tuple(mv.chip_bits[1:])

    mine_x, mine_z = mv.index((X, 1)), mv.index((Z1, 1))
    place = [mine_x ^ i for i in range(4)] + [4 + (mine_z ^ i) for i in range(4)]
    place += [core, 1 - core, mv.dp]
    place += [mv.bit(m) for m in (1, *mv.chip_bits)]

    plan.given(
        i=jnp.stack(place).astype(jnp.int32),
        lns=lengths,
        x=x,
        qkv_w0=qkv_weight,
        out_w0=out_weight,
        up_w0=up_weight,
        down_w0=down_weight,
        qvb=qv_bias,
        upb=up_bias,
        go=grad_output,
    )

    def others(name):
        return [(f"{name}.y{d}", name, TENSOR, d) for d in parts[1:]]

    def swap(key):
        return (f"{key}.sib", key, DATA, 1)

    def keys(name):
        return [f"{name}{d}" for d in parts]

    both = (AT, AT + 4)

    def pick_q(info, q):
        return pick(info, [(q, 1, width // 8, both)])

    def pick_ou(info, o, u, _):
        return pick(info, [(o, 0, hw // 2, (CORES,)), (u, 0, width // 8, both)])

    def pick_d(info, d, _):
        return pick(info, [(d, 0, fw // 8, both)])

    task(
        "pick_q",
        0,
        2.8,
        ["i", "qkv_w0"],
        ["q"],
        pick_q,
        [(*s, "b1") for s in others("q")],
    )
    task(
        "ln",
        0.5,
        1.0,
        ["lns"],
        ["ln"],
        lambda n: [lax.dynamic_slice_in_dim(n, lax.axis_index(TENSOR), 1, 0)],
    )

    def bias_rows(qv, up):
        q, v = qv[0], qv[1]
        rows = jnp.concatenate([q, jnp.zeros_like(q), v, up.astype(F32)])
        return [rows.reshape(-1, 1, hw)]

    task(
        "b0",
        -1,
        1.5,
        ["qvb", "upb"],
        ["b0"],
        bias_rows,
        [(f"b{d}", "b0", TENSOR, d) for d in parts[1:]],
    )
    task(
        "pick_ou",
        1.0,
        3.2,
        ["i", "out_w0", "up_w0", "qkv0"],
        ["o", "u"],
        pick_ou,
        [(*s, "q.y1") for s in others("o")] + [(*s, "o.y1") for s in others("u")],
    )
    task(
        "pick_d",
        2.5,
        3.0,
        ["i", "down_w0", "h0"],
        ["d"],
        pick_d,
        [(*s, "u.y1") for s in others("d")],
    )
    qkv_from, out_from = [["qkv_w0"]], [["out_w0"]]
    up_from, down_from = [["up_w0"]], [["down_w0"]]
    for d in parts[1:]:
        qkv_from.append(plan.fetch(0.2, "q", d, (X, Z1), 1))
        o = f"o.y{d}"
        task(f"o.sib{d}", 0.3, 0.0, [o], [], None, [(f"o.sib{d}", o, DATA, 1)])
        out_from.append([o, f"o.sib{d}"])
        up_from.append(plan.fetch(0.4, "u", d, (X, Z1), 0))
        down_from.append(plan.fetch(0.5, "d", d, (X, Z1), 0))

    for d in parts:
        made = [f"qkv{d}", f"qkv_w{d}"] if d else [f"qkv{d}"]
        task(
            f"pj{d}",
            2 + d,
            3.0,
            ["i", "x", f"b{d}", *qkv_from[d]],
            made,
            lambda info, x, b, *w: project(info, x, b, *w),
        )
        task(
            f"h{d}",
            2 + d,
            6.5,
            ["ln", f"qkv{d}"],
            [f"h{d}", f"lse{d}"],
            attend,
            [],
        )

    def split_args(a, groups):
        out, at = [], 0
        for g in groups:
            out.append(a[at : at + len(g)])
            at += len(g)
        return out

    def attended_task(info, x, *rest):
        mixed, weights = rest[:n_tensor], split_args(rest[n_tensor:], out_from)
        return attended(
            info, x, out_bias, norm1_gain, norm1_shift, mixed, weights
        )

    task(
        "at",
        20,
        4.2,
        ["i", "x", *keys("h"), *[k for g in out_from for k in g]],
        ["nb", "n1", "sc1", *keys("out_w")[1:]],
        attended_task,
        [(*swap("nb"), "u.y1")],
    )
    for d in parts:
        task(
            f"wd{d}",
            21 + d,
            8.5,
            ["i", "nb", f"b{d}", *up_from[d]],
            [f"a{d}", f"sl{d}"] + [f"up_w{d}"] * (d > 0),
            widened,
            [(*swap(f"a{d}"), "d.y1")],
        )

    def narrowed_task(info, normal1, grad_output, *rest):
        act, weights = rest[:n_tensor], split_args(rest[n_tensor:], down_from)
        low, g_two, result, sums = narrowed(
            info,
            normal1,
            norm1_gain,
            norm1_shift,
            down_bias,
            norm2_gain,
            norm2_shift,
            grad_output,
            act,
            weights,
        )
        return low, g_two, result, sums

    task(
        "nw",
        40,
        12.5,
        ["i", "n1", "go", *keys("a")]
        + [k for g in down_from for k in g],
        ["g2", "gt", "res", "sums2"],
        narrowed_task,
        [swap("g2")],
    )

    block = fw // 4

    def made(name, rank, cost, items, rows, columns, after=None, of=back):
        args = []
        for d in of:
            for a, _, b, _, *_ in items(d):
                args += [a, b, f"{a}.sib", f"{b}.sib"]

        def work(info, *a):
            outs, at = [], 0
            for d in of:
                jobs = []
                for _, ai, _, bi, *rest in items(d):
                    a1, b1, a2, b2 = a[at : at + 4]
                    a1, a2 = ((v if ai is None else (v, ai)) for v in (a1, a2))
                    b1, b2 = ((v if bi is None else (v, bi)) for v in (b1, b2))
                    jobs.append((a1, b1, a2, b2, *rest))
                    at += 4
                outs.append(jobs)
            return grad_stack(info, outs, rows, columns)

        s = n_tensor // 2
        task(
            f"{name}.p{of[0]}",
            rank,
            cost,
            ["i", *args],
            [f"{name}.p{d}" for d in of],
            work,
            [
                (f"{name}.y{d}.{s}", f"{name}.p{d}", TENSOR, s, after)
                for d in of
                if d >= s
            ],
        )

    chunks = {}
    first_y = f"{n_tensor // 2}.{n_tensor // 2}"

    def chunk(rank, name, levels, rows, back=False):
        chunks[name] = (levels, rows)
        plan.reduce(rank, name, levels, back)

    for i, of in enumerate((back[: n_tensor // 2], back[n_tensor // 2 :])):
        made(
            "down",
            50 + 2.5 * i,
            6.0,
            lambda d: [(f"a{d}", None, "g2", None, 4, (0,), (0, 1))],
            block,
            half,
            None,
            of,
        )
    chunk(1.0, "down", (X, *Z), fw)
    for i, d in enumerate(back):
        task(
            f"gb{d}",
            51 + i,
            6.0,
            ["i", "g2", f"sl{d}", *down_from[d], f"down.p{back[0]}"],
            [f"gu{d}", f"us{d}"],
            lambda *a: gelu_back(*a[:-1]),
            [(*swap(f"gu{d}"), None if d else f"down.y{first_y}")]
            + [swap(k) for k in ("x", *keys("h")) if d],
        )
    for i, of in enumerate((back[: n_tensor // 2], back[n_tensor // 2 :])):
        made(
            "up",
            64 + 4 * i,
            4.0,
            lambda d: [("nb", None, f"gu{d}", None, 2, (0, 2), (0,))],
            half // 2,
            fw,
            f"down.y{first_y}",
            of,
        )
    chunk(1.2, "up", (X, *Z), half)

    def attended_back_task(g_two, normal, scale, *rest):
        return attended_back(
            g_two, normal, scale, norm1_gain, rest[:n_tensor], rest[n_tensor:]
        )

    task(
        "ab",
        56,
        7.5,
        ["gt", "n1", "sc1", *keys("gu"), *keys("up_w")],
        ["g1", "go1", "sums1"],
        attended_back_task,
        [(*swap("g1"), f"down.y{first_y}")],
    )
    for i, d in enumerate(back):
        task(
            f"hb{d}",
            62 + i,
            10.8,
            ["ln", f"qkv{d}", "g1", f"out_w{d}", f"lse{d}"],
            [f"gq{d}", f"qs{d}"],
            attend_back,
            [(*swap(f"gq{d}"), f"down.y{first_y}")],
        )

    def out_item(d):
        return (f"h{d}", None, "g1", None, 1, (0,), (0, 1))

    def qkv_item(c):
        return lambda d: ("x", None, f"gq{d}", c, 1, (0, 1), (0,))

    if same:
        groups = {"att0": [out_item, qkv_item(2)], "att1": [qkv_item(1), qkv_item(0)]}
    else:
        groups = {"att0": [out_item], "att1": [qkv_item(c) for c in (2, 1, 0)]}
    for i, (name, items) in enumerate(groups.items()):
        rows = hw if items[0] is out_item else half
        made(
            name,
            66 + i,
            5.2,
            lambda d, items=items: [it(d) for it in items],
            rows,
            half if items[0] is out_item else hw,
            f"{('up', 'att0')[i]}.y{first_y}",
        )
        chunk(1.4 + 0.1 * i, name, (X, *Z), rows * len(items), back=True)

    def pack(one, two, *rest):
        packs = []
        for d in parts:
            g, up = rest[2 * d : 2 * d + 2]
            packs.append(
                jnp.concatenate([one.ravel(), two.ravel(), g[0], g[2], up[0]])
            )
        return packs

    needs = [k for d in parts for k in (f"qs{d}", f"us{d}")]
    packs, s = keys("pk"), n_tensor // 2
    task(
        "pk",
        70,
        1.5,
        ["sums1", "sums2", *needs],
        packs,
        pack,
        [
            (f"pk{d}.y", f"pk{d}", TENSOR, s, f"att1.y{first_y}")
            for d in range(s, n_tensor)
        ],
    )
    while s:
        new = [f"sm{s}.{d}" for d in range(s)]
        for d in range(s):
            if s > 1:
                sends = [(f"{new[d]}.y", new[d], TENSOR, s // 2)] * (d >= s // 2)
            else:
                sends = [("sm.1", new[0], DATA, 1)]
            task(
                new[d],
                2.0,
                0.6,
                [packs[d], f"{packs[d + s]}.y"],
                [new[d]],
                lambda a, b: [a + b],
                sends,
            )
        packs, s = new, s // 2
    last, masks = packs[0], [1, *mv.chip_bits]
    for i, m in enumerate(masks):
        out = f"sm.at{m}"
        nxt = masks[i + 1] if i + 1 < len(masks) else None
        sends = [(f"sm.{nxt}", out, DATA, nxt)] if nxt else []
        task(out, 2.0, 0.6, [last, f"sm.{m}"], [out], lambda a, b: [a + b], sends)
        last = out

    task(
        "ig",
        80,
        7.0,
        ["go1", *keys("gq"), *keys("qkv_w")],
        ["gi"],
        lambda g, *a: [input_grad(g, a[:n_tensor], a[n_tensor:])],
    )

    def results(group, names, outputs, after=None):
        plan.gather(1.9, group, names, after)
        per_device = [chunks[n][1] // (n_dp // 2) for n in names]
        unit = min(per_device)
        total = sum(per_device) // unit
        first = {n: sum(per_device[:i]) // unit for i, n in enumerate(names)}

        def at(c, name, row):
            levels, rows = chunks[name]
            own = rows // (n_dp // 2)
            r, dp = row // own, c
            for i, m in enumerate(reversed(levels)):
                dp |= m * ((r >> i) & 1)
            return dp * total + first[name] + row % own // unit

        for name, cost, blocks, block, shape in outputs:
            tables = [
                ([at(c, n, row + r) for r in range(0, block[0], unit)], place)
                for c, n, row, place in blocks
            ]
            task(
                name,
                85,
                cost,
                [f"{group}.all"],
                [name],
                lambda a, *, rest=(unit, tables, block, shape, name): [
                    spread(a, *rest)
                ],
            )

    results(
        "da",
        ("down",),
        [
            (
                "gd",
                6.0,
                [(c, "down", r * block, (r, c)) for r in range(4) for c in (0, 1)],
                (block, half),
                (fw, width),
            )
        ],
        f"att0.y{first_y}",
    )
    rows = half // 4
    results(
        "ua",
        ("up",),
        [
            (
                "gup",
                6.0,
                [
                    (c, "up", r * rows, (4 * c + r, 0))
                    for c in (0, 1)
                    for r in range(4)
                ],
                (rows, fw),
                (width, fw),
            )
        ],
    )

    def sources(*names):
        return [f"{n}.{k}" for n in names for k in ("mine", "other")]

    def cores_result(name, cost, names, blocks, block, shape):
        tables = [
            [(2 * names.index(n) + (c != bit), r, at) for c, n, r, at in blocks]
            for bit in (0, 1)
        ]
        task(
            name,
            85,
            cost,
            sources(*names),
            [name],
            lambda *a: [widen(core, a, block, shape, tables, name)],
        )

    cores_result(
        "gout",
        3.0,
        ("att0",),
        [(c, "att0", 0, (0, c)) for c in (0, 1)],
        (hw, half),
        (hw, width),
    )
    place = {2: ("att0", 1), 1: ("att1", 0), 0: ("att1", 1)}
    if not same:
        place = {c: ("att1", 2 - c) for c in range(3)}
    cores_result(
        "gqkv",
        5.0,
        ("att0", "att1") if same else ("att1",),
        [(c, *place[i], (i, c, 0)) for i in range(3) for c in (0, 1)],
        (half, hw),
        (3, width, hw),
    )

    plan.run()
    value = {k: b.value for k, b in plan.box.items()}
    small = value[last]
    vec = [small[i * width : (i + 1) * width] for i in range(6)]
    rest = small[6 * width :]
    return (
        value["res"],
        value["gi"],
        value["gqkv"],
        rest[: 2 * hw].reshape(2, hw),
        value["gout"],
        vec[0],
        vec[1],
        vec[2],
        value["gup"],
        rest[2 * hw :],
        value["gd"],
        vec[3],
        vec[4],
        vec[5],
    )


def solution(mesh):
    n_dp, n_tensor = mesh.shape[DATA], mesh.shape[TENSOR]
    pairs = n_tensor == 2 and n_dp >= 8 and n_dp & (n_dp - 1) == 0
    return jax.shard_map(
        functools.partial(body if pairs else plain, n_dp, n_tensor),
        mesh=mesh,
        in_specs=(
            P((DATA, TENSOR), None),
            P(None, None, TENSOR),
            P(None, TENSOR),
            P(TENSOR, None),
            P(),
            P(),
            P(),
            P(None, TENSOR),
            P(TENSOR),
            P(TENSOR, None),
            P(),
            P(),
            P(),
            P(DATA),
            P((DATA, TENSOR), None),
        ),
        out_specs=(
            P((DATA, TENSOR), None),
            P((DATA, TENSOR), None),
            P(None, None, TENSOR),
            P(None, TENSOR),
            P(TENSOR, None),
            P(),
            P(),
            P(),
            P(None, TENSOR),
            P(TENSOR),
            P(TENSOR, None),
            P(),
            P(),
            P(),
        ),
        check_vma=False,
    )
```

```python
import functools

import jax
import jax.numpy as jnp
import numpy as np
from jax import lax
from jax.experimental import pallas as pl
from jax.experimental.pallas import tpu as pltpu
from jax.sharding import PartitionSpec as P

HD = 64
TENSOR, DATA = "tensor", "dp"
F32 = jnp.float32
BF16 = jnp.bfloat16
NEG = -1000000000.0
SCALE = 0
COST = [0.0]
LOG = []
RANKS = ()
FLOWN = []
HELD = []


def cost():
    flops = int(SCALE * COST[0] * 1.15e9)
    return pl.CostEstimate(flops=flops, bytes_accessed=0, transcendentals=0)


ERFC_P = 0.3275911
ERFC_C = (
    0.18510853909898187,
    0.17995808540893535,
    0.21032499893163595,
    0.011746556912990477,
    0.4777504794974274,
    -0.4314195259659222,
    0.5110037999525718,
    -0.14447299033990682,
)


def gelu_both(up):
    size = jnp.abs(up)
    t = 1.0 / (1.0 + (ERFC_P * 0.5**0.5) * size)
    poly = jnp.full_like(t, 0.5 * ERFC_C[-1])
    for c in ERFC_C[-2::-1]:
        poly = poly * t + 0.5 * c
    density = jnp.exp(-0.5 * up * up)
    tail = poly * t * density
    phi = jnp.where(up > 0, 1.0 - tail, tail)
    return up * phi, phi + up * (density * 0.3989422804014327)


def contract(a, b, ca, cb):
    return lax.dot_general(a, b, (((ca,), (cb,)), ((), ())), preferred_element_type=F32)


def params(mib):
    return pltpu.CompilerParams(vmem_limit_bytes=mib * 2**20)


def whole_spec(a):
    return pl.BlockSpec(a.shape, lambda *_: (0,) * len(a.shape))


BROUGHT = ((0, 0), (2, 0), (1, 0), (4, 0), (0, 1), (3, 0), (1, 1), (5, 0))


AT, CORES, DP, BITS = 0, 8, 10, 11


def attend_kernel(len_ref, q_ref, k_ref, v_ref, o_ref, lse_ref):
    length = len_ref[0]
    q, k, v = q_ref[0], k_ref[0], v_ref[0]
    rows, width = q.shape
    head = lax.broadcasted_iota(jnp.int32, (rows, width), 1) // HD
    key_pos = lax.broadcasted_iota(jnp.int32, (rows, rows), 0)
    out = None
    for h in range(width // HD):
        mine = head == h
        kh = jnp.where(mine, k, jnp.zeros_like(k)) * jnp.asarray(HD**-0.5, BF16)
        s = jnp.where(key_pos < length, contract(kh, q, 1, 1), F32(NEG))
        top = jnp.max(s, axis=0, keepdims=True)
        e = jnp.exp(s - top)
        total = jnp.sum(e, axis=0, keepdims=True)
        lse_ref[0, h : h + 1, :] = top + jnp.log(total)
        p = (e * (1.0 / total)).astype(BF16)
        o = contract(p, v, 0, 0)
        out = o if out is None else jnp.where(mine, o, out)
    o_ref[...] = out.astype(BF16)


def third(rows, wide, c):
    return pl.BlockSpec((1, rows, wide), lambda i, c=c: (c, 0, i))


def attend(length, qkv):
    _, rows, width = qkv.shape
    wide = min(2 * HD, width)
    steps = width // wide
    return pl.pallas_call(
        attend_kernel,
        grid=(steps,),
        in_specs=[pl.BlockSpec(memory_space=pltpu.SMEM)]
        + [third(rows, wide, c) for c in range(3)],
        out_specs=[
            pl.BlockSpec((rows, wide), lambda i: (0, i)),
            pl.BlockSpec((1, wide // HD, rows), lambda i: (i, 0, 0)),
        ],
        out_shape=[
            jax.ShapeDtypeStruct((rows, width), BF16),
            jax.ShapeDtypeStruct((steps, wide // HD, rows), F32),
        ],
        compiler_params=params(20),
        cost_estimate=cost(),
    )(length, qkv, qkv, qkv)


def attend_back_kernel(
    len_ref, q_ref, k_ref, v_ref, g1_ref, w_ref, lse_ref, d_ref, sum_ref
):
    length = len_ref[0]
    q, k, v = q_ref[0], k_ref[0], v_ref[0]
    g = contract(g1_ref[...], w_ref[...], 1, 1).astype(BF16)
    rows, width = q.shape
    head = lax.broadcasted_iota(jnp.int32, (rows, width), 1) // HD
    head_t = lax.broadcasted_iota(jnp.int32, (width, rows), 0) // HD
    key_pos = lax.broadcasted_iota(jnp.int32, (rows, rows), 0)
    dq = dk = dv = None
    for h in range(width // HD):
        mine = head == h
        kh = jnp.where(mine, k, jnp.zeros_like(k)) * jnp.asarray(HD**-0.5, BF16)
        vh = jnp.where(mine, v, jnp.zeros_like(v))
        s = jnp.where(key_pos < length, contract(kh, q, 1, 1), F32(NEG))
        p = jnp.exp(s - lse_ref[0, h : h + 1, :])
        dp = contract(vh, g, 1, 1)
        dvh = contract(p.astype(BF16), g, 1, 0)
        center = jnp.sum(p * dp, axis=0, keepdims=True)
        ds = (p * (dp - center)).astype(BF16)
        dkh = contract(ds, q, 1, 0)
        dqh = contract(k, ds, 0, 0)
        dv = dvh if dv is None else jnp.where(mine, dvh, dv)
        dk = dkh if dk is None else jnp.where(mine, dkh, dk)
        dq = dqh if dq is None else jnp.where(head_t == h, dqh, dq)
    out = (
        (dq * (HD**-0.5)).T.astype(BF16),
        (dk * (HD**-0.5)).astype(BF16),
        dv.astype(BF16),
    )
    for c in range(3):
        d_ref[c] = out[c]
        sum_ref[c : c + 1, :] = jnp.sum(out[c].astype(F32), axis=0, keepdims=True)


def attend_back(length, qkv, g_one, out_w, lse):
    _, rows, width = qkv.shape
    wide = min(2 * HD, width)
    d = g_one.shape[1]
    return pl.pallas_call(
        attend_back_kernel,
        grid=(width // wide,),
        in_specs=[pl.BlockSpec(memory_space=pltpu.SMEM)]
        + [third(rows, wide, c) for c in range(3)]
        + [
            whole_spec(g_one),
            pl.BlockSpec((wide, d), lambda i: (i, 0)),
            pl.BlockSpec((1, wide // HD, rows), lambda i: (i, 0, 0)),
        ],
        out_specs=[
            pl.BlockSpec((3, rows, wide), lambda i: (0, 0, i)),
            pl.BlockSpec((3, wide), lambda i: (0, i)),
        ],
        out_shape=[
            jax.ShapeDtypeStruct((3, rows, width), BF16),
            jax.ShapeDtypeStruct((3, width), F32),
        ],
        compiler_params=params(28),
        cost_estimate=cost(),
    )(length, qkv, qkv, qkv, g_one, out_w, lse)


def project(at, x, bias, *pieces):
    n = len(pieces)
    rows, depth = x.shape
    width = pieces[0].shape[2]
    size = depth // len(BROUGHT)

    def kernel(at_ref, x_ref, b_ref, *refs):
        w_ref = refs[0]
        if n > 1:
            w_ref = refs[n + 1]
            for i, (k, j) in enumerate(BROUGHT):
                row = pl.multiple_of(at_ref[i] * size, size)
                w_ref[0, pl.ds(row, size)] = refs[k][0, j * size : (j + 1) * size]
        refs[n][0] = (contract(x_ref[...], w_ref[0], 1, 0) + b_ref[0]).astype(BF16)

    out_specs = [pl.BlockSpec((1, rows, width), lambda c, at: (c, 0, 0))]
    out_shape = [jax.ShapeDtypeStruct((3, rows, width), BF16)]
    if n > 1:
        out_specs.append(pl.BlockSpec((1, depth, width), lambda c, at: (c, 0, 0)))
        out_shape.append(jax.ShapeDtypeStruct((3, depth, width), BF16))
    return pl.pallas_call(
        kernel,
        grid_spec=pltpu.PrefetchScalarGridSpec(
            num_scalar_prefetch=1,
            grid=(3,),
            in_specs=[
                whole_spec(x),
                pl.BlockSpec((1, 1, width), lambda c, at: (c, 0, 0)),
            ]
            + [
                pl.BlockSpec((1, p.shape[1], width), lambda c, at: (c, 0, 0))
                for p in pieces
            ],
            out_specs=out_specs,
        ),
        out_shape=out_shape,
        compiler_params=params(20),
        cost_estimate=cost(),
    )(at, x, bias, *pieces)


def norm(hidden):
    center = hidden - jnp.mean(hidden, axis=-1, keepdims=True)
    spread = jnp.mean(center * center, axis=-1, keepdims=True)
    scale = lax.rsqrt(spread + 1e-05)
    return center * scale, scale


def norm_back(grad, normal, scale, gain):
    gy = grad * gain
    mean = jnp.mean(gy, axis=-1, keepdims=True)
    along = jnp.mean(gy * normal, axis=-1, keepdims=True)
    return scale * (gy - mean - normal * along)


def attended(at, x, bias, gain, shift, mixed, weights):
    rows, d = x.shape
    step = min(128, rows)
    cut = [i for i, w in enumerate(weights) if len(w) > 1]
    flat = [p for w in weights for p in w]
    n = len(mixed)

    def kernel(at_ref, x_ref, b_ref, g_ref, s_ref, *refs):
        m, w = refs[:n], refs[n : n + len(flat)]
        low_ref, normal_ref, scale_ref = refs[n + len(flat) :][:3]
        outs = refs[n + len(flat) + 3 :]
        k = j = 0
        total = x_ref[...].astype(F32) + b_ref[...]
        for i, ps in enumerate(weights):
            if len(ps) > 1:
                size = ps[0].shape[0]
                held = outs[j]

                @pl.when(pl.program_id(0) == 0)
                def _(held=held, k=k, ps=ps, size=size):
                    for q in range(len(ps)):
                        row = pl.multiple_of(at_ref[CORES + q] * size, size)
                        held[pl.ds(row, size), :] = w[k + q][...]

                value = held[...]
                j += 1
            else:
                value = w[k][...]
            k += len(ps)
            total = total + contract(m[i][...], value, 1, 0)
        normal, scale = norm(total)
        normal_ref[...] = normal
        scale_ref[...] = scale
        low_ref[...] = (normal * g_ref[...] + s_ref[...]).astype(BF16)

    row = pl.BlockSpec((step, d), lambda i, at: (i, 0))
    out_specs = [row, row, pl.BlockSpec((step, 1), lambda i, at: (i, 0))]
    out_shape = [
        jax.ShapeDtypeStruct((rows, d), BF16),
        jax.ShapeDtypeStruct((rows, d), F32),
        jax.ShapeDtypeStruct((rows, 1), F32),
    ]
    for i in cut:
        out_shape.append(
            jax.ShapeDtypeStruct((len(weights[i]) * weights[i][0].shape[0], d), BF16)
        )
        out_specs.append(whole_spec(out_shape[-1]))
    vecs = [v.reshape(1, d) for v in (bias, gain, shift)]
    return pl.pallas_call(
        kernel,
        grid_spec=pltpu.PrefetchScalarGridSpec(
            num_scalar_prefetch=1,
            grid=(rows // step,),
            in_specs=[row]
            + [whole_spec(v) for v in vecs]
            + [pl.BlockSpec((step, m.shape[1]), lambda i, at: (i, 0)) for m in mixed]
            + [whole_spec(p) for p in flat],
            out_specs=out_specs,
        ),
        out_shape=out_shape,
        compiler_params=params(20),
        cost_estimate=cost(),
    )(at, x, *vecs, *mixed, *flat)


def widened(at, low, bias, *pieces):
    rows, d = low.shape
    n = len(pieces)
    size, width = d // len(BROUGHT), pieces[0].shape[1]
    block, sub = bias.shape[2], min(128, rows)

    def kernel(at_ref, x_ref, b_ref, *refs):
        act_ref, slope_ref = refs[n : n + 2]
        w_ref = refs[0]
        if n > 1:
            w_ref = refs[n + 2]
            for i, (k, j) in enumerate(BROUGHT):
                row = pl.multiple_of(at_ref[i] * size, size)
                w_ref[pl.ds(row, size), :] = refs[k][j * size : (j + 1) * size, :]
        for i in range(0, rows, sub):
            up = contract(x_ref[i : i + sub, :], w_ref[...], 1, 0) + b_ref[0]
            act, slope = gelu_both(up)
            act_ref[i : i + sub, :] = act.astype(BF16)
            slope_ref[i : i + sub, :] = slope.astype(BF16)

    out = jax.ShapeDtypeStruct((rows, width), BF16)
    out_shape = [out, out]
    if n > 1:
        out_shape.append(jax.ShapeDtypeStruct((d, width), BF16))
    return pl.pallas_call(
        kernel,
        grid_spec=pltpu.PrefetchScalarGridSpec(
            num_scalar_prefetch=1,
            grid=(width // block,),
            in_specs=[
                whole_spec(low),
                pl.BlockSpec((1, 1, block), lambda i, at: (3 + i, 0, 0)),
            ]
            + [pl.BlockSpec((p.shape[0], block), lambda i, at: (0, i)) for p in pieces],
            out_specs=[
                pl.BlockSpec((o.shape[0], block), lambda i, at: (0, i))
                for o in out_shape
            ],
        ),
        out_shape=out_shape,
        compiler_params=params(24),
        cost_estimate=cost(),
    )(at, low, bias, *pieces)


def narrowed(at, normal1, gain1, shift1, bias, gain, shift, grad_output, act, weights):
    rows, d = normal1.shape
    block = 256
    steps = d // block
    flat = [p for w in weights for p in w]
    cut = [w for w in weights if len(w) > 1]
    n = len(act)

    def kernel(at_ref, nm_ref, g1_ref, s1_ref, b_ref, g_ref, s_ref, go_ref, *refs):
        a, w = refs[:n], refs[n : n + len(flat)]
        low_ref, grad_ref, result_ref, sum_ref, acc = refs[n + len(flat) :][:5]
        held = list(refs[n + len(flat) + 5 :])
        total = nm_ref[...] * g1_ref[...] + s1_ref[...] + b_ref[...]
        k = 0
        for i, ps in enumerate(weights):
            value = w[k]
            if len(ps) > 1:
                value = held.pop(0)
                size = value.shape[0] // len(BROUGHT)
                for q, (m, j) in enumerate(BROUGHT):
                    row = pl.multiple_of(at_ref[q] * size, size)
                    value[pl.ds(row, size), :] = w[k + m][j * size : (j + 1) * size, :]
            total = total + contract(a[i][...], value[...], 1, 0)
            k += len(ps)
        acc[pl.program_id(0)] = total

        @pl.when(pl.program_id(0) == steps - 1)
        def _():
            sums = [jnp.zeros((1, d), F32) for _ in range(3)]
            for r in range(0, rows, 64):
                cut = slice(r, r + 64)
                hidden = jnp.concatenate([acc[i, cut, :] for i in range(steps)], axis=1)
                normal, scale = norm(hidden)
                result_ref[cut, :] = (normal * g_ref[...] + s_ref[...]).astype(BF16)
                grad = go_ref[cut, :].astype(F32)
                g_two = norm_back(grad, normal, scale, g_ref[...])
                grad_ref[cut, :] = g_two
                low_ref[cut, :] = g_two.astype(BF16)
                for j, v in enumerate((g_two, grad * normal, grad)):
                    sums[j] = sums[j] + jnp.sum(v, axis=0, keepdims=True)
            for j in range(3):
                sum_ref[j : j + 1, :] = sums[j]

    def col(rows):
        return pl.BlockSpec((rows, block), lambda s, at: (0, s))

    vecs = [v.reshape(1, d) for v in (gain1, shift1, bias, gain, shift)]
    out_shape = [
        jax.ShapeDtypeStruct((rows, d), BF16),
        jax.ShapeDtypeStruct((rows, d), F32),
        jax.ShapeDtypeStruct((rows, d), BF16),
        jax.ShapeDtypeStruct((3, d), F32),
    ]
    return pl.pallas_call(
        kernel,
        grid_spec=pltpu.PrefetchScalarGridSpec(
            num_scalar_prefetch=1,
            grid=(steps,),
            in_specs=[col(rows), col(1), col(1), col(1)]
            + [whole_spec(v) for v in vecs[3:]]
            + [whole_spec(grad_output)]
            + [whole_spec(a) for a in act]
            + [col(p.shape[0]) for p in flat],
            out_specs=[whole_spec(o) for o in out_shape],
            scratch_shapes=[pltpu.VMEM((steps, rows, block), F32)]
            + [pltpu.VMEM((act[0].shape[1], block), BF16) for _ in cut],
        ),
        out_shape=out_shape,
        compiler_params=params(32 if cut else 48),
        cost_estimate=cost(),
    )(at, normal1, *vecs, grad_output, *act, *flat)


def gelu_back(at, g, slope, *pieces):
    rows, d = g.shape
    width = slope.shape[1]
    n = len(pieces)
    size = min(512, width)

    def kernel(at_ref, g_ref, s_ref, *refs):
        out_ref, sum_ref = refs[n : n + 2]
        w = refs[0][...]
        if n > 1:
            held, cut = refs[n + 2], width // len(BROUGHT)

            @pl.when(pl.program_id(0) == 0)
            def _():
                for i, (k, j) in enumerate(BROUGHT):
                    row = pl.multiple_of(at_ref[i] * cut, cut)
                    held[pl.ds(row, cut), :] = refs[k][j * cut : (j + 1) * cut, :]

            w = held[pl.ds(pl.multiple_of(pl.program_id(0) * size, size), size), :]
        low = (contract(g_ref[...], w, 1, 1) * s_ref[...].astype(F32)).astype(BF16)
        out_ref[...] = low
        sum_ref[...] = jnp.sum(low.astype(F32), axis=0, keepdims=True)

    def column(rows):
        return pl.BlockSpec((rows, size), lambda s, at: (0, s))

    w_specs = [pl.BlockSpec((size, d), lambda s, at: (s, 0))]
    return pl.pallas_call(
        kernel,
        grid_spec=pltpu.PrefetchScalarGridSpec(
            num_scalar_prefetch=1,
            grid=(width // size,),
            in_specs=[whole_spec(g), column(rows)]
            + ([whole_spec(p) for p in pieces] if n > 1 else w_specs),
            out_specs=[column(rows), column(1)],
            scratch_shapes=[pltpu.VMEM((width, d), BF16)] if n > 1 else [],
        ),
        out_shape=[
            jax.ShapeDtypeStruct((rows, width), BF16),
            jax.ShapeDtypeStruct((1, width), F32),
        ],
        compiler_params=params(24),
        cost_estimate=cost(),
    )(at, g, slope, *pieces)


def attended_back(g_two, normal, scale, gain, g_up, up_w):
    rows, d = g_two.shape
    block = 256
    steps, n = d // block, len(g_up)

    def kernel(g2_ref, nm_ref, sc_ref, gain_ref, *refs):
        g, w = refs[:n], refs[n : 2 * n]
        low_ref, grad_ref, sum_ref, acc = refs[2 * n :]
        total = g2_ref[...]
        for i in range(n):
            total = total + contract(g[i][...], w[i][...], 1, 1)
        acc[pl.program_id(0)] = total

        @pl.when(pl.program_id(0) == steps - 1)
        def _():
            sums = [jnp.zeros((1, d), F32) for _ in range(3)]
            for r in range(0, rows, 64):
                cut = slice(r, r + 64)
                g_in = jnp.concatenate([acc[i, cut, :] for i in range(steps)], axis=1)
                nm = nm_ref[cut, :]
                g_one = norm_back(g_in, nm, sc_ref[cut, :], gain_ref[...])
                grad_ref[cut, :] = g_one
                low_ref[cut, :] = g_one.astype(BF16)
                for j, v in enumerate((g_one, g_in * nm, g_in)):
                    sums[j] = sums[j] + jnp.sum(v, axis=0, keepdims=True)
            for j in range(3):
                sum_ref[j : j + 1, :] = sums[j]

    out_shape = [
        jax.ShapeDtypeStruct((rows, d), BF16),
        jax.ShapeDtypeStruct((rows, d), F32),
        jax.ShapeDtypeStruct((3, d), F32),
    ]
    gain = gain.reshape(1, d)
    return pl.pallas_call(
        kernel,
        grid=(steps,),
        in_specs=[pl.BlockSpec((rows, block), lambda s: (0, s))]
        + [whole_spec(a) for a in (normal, scale, gain, *g_up)]
        + [pl.BlockSpec((block, w.shape[1]), lambda s: (s, 0)) for w in up_w],
        out_specs=[whole_spec(o) for o in out_shape],
        out_shape=out_shape,
        scratch_shapes=[pltpu.VMEM((steps, rows, block), F32)],
        compiler_params=params(28 if n > 1 else 48),
        cost_estimate=cost(),
    )(g_two, normal, scale, gain, *g_up, *up_w)


def input_grad(g_one, g_proj, qkv_w):
    rows, d = g_one.shape
    width, n = g_proj[0].shape[2], len(g_proj)
    block = 256

    def kernel(g1_ref, *refs):
        g, w, out_ref = refs[:n], refs[n : 2 * n], refs[-1]
        total = g1_ref[...]
        for i in range(n):
            for c in range(3):
                total = total + contract(g[i][c], w[i][c], 1, 1)
        out_ref[...] = total

    col = pl.BlockSpec((rows, block), lambda s: (0, s))
    return pl.pallas_call(
        kernel,
        grid=(d // block,),
        in_specs=[col]
        + [whole_spec(g) for g in g_proj]
        + [pl.BlockSpec((3, block, width), lambda s: (0, s, 0))] * n,
        out_specs=col,
        out_shape=jax.ShapeDtypeStruct((rows, d), F32),
        compiler_params=params(24),
        cost_estimate=cost(),
    )(g_one, *g_proj, *qkv_w)


def pick(index, pieces):
    n = len(pieces)
    views = [(i, j) for i, p in enumerate(pieces) for j in range(len(p[3]))]

    def kernel(index_ref, *refs):
        for v, (i, j) in enumerate(views):
            axis, size = pieces[i][1:3]
            at = tuple([slice(None)] * axis + [slice(j * size, (j + 1) * size)])
            refs[len(views) + i][at] = refs[v][...]

    specs, shapes = [], []
    for i, j in views:
        a, axis, size, places = pieces[i]
        specs.append(
            pl.BlockSpec(
                a.shape[:axis] + (size,) + a.shape[axis + 1 :],
                lambda s, at, p=places[j], axis=axis, n=a.ndim: tuple(
                    at[p] if k == axis else 0 for k in range(n)
                ),
            )
        )
    for a, axis, size, places in pieces:
        shape = a.shape[:axis] + (size * len(places),) + a.shape[axis + 1 :]
        shapes.append(jax.ShapeDtypeStruct(shape, a.dtype))
    return pl.pallas_call(
        kernel,
        grid_spec=pltpu.PrefetchScalarGridSpec(
            num_scalar_prefetch=1,
            grid=(1,),
            in_specs=specs,
            out_specs=[whole_spec(s) for s in shapes],
        ),
        out_shape=shapes,
        compiler_params=params(60),
        cost_estimate=cost(),
    )(index, *[pieces[i][0] for i, _ in views])


def add(a, b):
    return (a.astype(F32) + b.astype(F32)).astype(BF16)


def add_split(bits, which, a, b):
    rows, columns = a.shape
    half = rows // 2
    if half % 16:
        total, bit = add(a, b), bits[BITS + which]
        return (
            lax.dynamic_slice_in_dim(total, bit * half, half, 0),
            lax.dynamic_slice_in_dim(total, (1 - bit) * half, half, 0),
        )
    block = half // 2 if half >= 256 else half
    per = half // block

    def kernel(bits_ref, a0, b0, a1, b1, keep_ref, send_ref):
        send_ref[...] = add(a1[...], b1[...])
        keep_ref[...] = add(a0[...], b0[...])

    def spec(of):
        return pl.BlockSpec((block, columns), lambda s, bits: (of(s, bits), 0))

    kept = spec(lambda s, bits: bits[BITS + which] * per + s)
    sent = spec(lambda s, bits: (1 - bits[BITS + which]) * per + s)
    plain = spec(lambda s, bits: s)
    out = jax.ShapeDtypeStruct((half, columns), BF16)
    return pl.pallas_call(
        kernel,
        grid_spec=pltpu.PrefetchScalarGridSpec(
            num_scalar_prefetch=1,
            grid=(per,),
            in_specs=[kept, kept, sent, sent],
            out_specs=[plain, plain],
        ),
        out_shape=[out, out],
        compiler_params=params(12),
        cost_estimate=cost(),
    )(bits, a, b, a, b)


def grad_stack(bits, outs, rows, width):
    jobs = [job for out in outs for job in out]
    sizes = [sum(job[4] for job in out) for out in outs]

    def depth_of(a):
        a = a[0] if isinstance(a, tuple) else a
        return a.shape[-2]

    depth = depth_of(jobs[0][0])
    total = sum(sizes)

    def kernel(bits_ref, *refs):
        s = pl.program_id(0)
        at = first = 0
        j = 0
        for o, out in enumerate(outs):
            for job in out:

                @pl.when((s >= at) & (s < at + job[4]))
                def _(j=j, o=o):
                    x1, y1, x2, y2 = (
                        r[0] if len(r.shape) == 3 else r[...]
                        for r in refs[4 * j : 4 * j + 4]
                    )
                    value = contract(x1, y1, 0, 0) + contract(x2, y2, 0, 0)
                    refs[4 * len(jobs) + o][...] = value.astype(BF16)

                at += job[4]
                j += 1

    def column(place, bits):
        return place[0] + sum(k * bits[BITS + i] for i, k in enumerate(place[1:]) if k)

    def spec(a, block, of):
        if isinstance(a, tuple):
            return pl.BlockSpec((1, *block), lambda s, bits: (a[1], 0, of(s, bits)))
        return pl.BlockSpec(block, lambda s, bits: (0, of(s, bits)))

    specs, args, at = [], [], 0
    for a1, b1, a2, b2, n, a_at, b_at in jobs:

        def a_of(s, bits, at=at, n=n, p=a_at):
            return column(p, bits) + jnp.clip(s - at, 0, n - 1)

        def b_of(s, bits, p=b_at):
            return column(p, bits)

        for a, b in ((a1, b1), (a2, b2)):
            specs += [spec(a, (depth, rows), a_of), spec(b, (depth, width), b_of)]
            args += [a, b]
        at += n
    out_specs, at = [], 0
    for size in sizes:
        out_specs.append(
            pl.BlockSpec(
                (rows, width),
                lambda s, bits, at=at, n=size: (jnp.clip(s - at, 0, n - 1), 0),
            )
        )
        at += size
    return pl.pallas_call(
        kernel,
        grid_spec=pltpu.PrefetchScalarGridSpec(
            num_scalar_prefetch=1, grid=(total,), in_specs=specs, out_specs=out_specs
        ),
        out_shape=[jax.ShapeDtypeStruct((n * rows, width), BF16) for n in sizes],
        compiler_params=params(24),
        cost_estimate=cost(),
    )(bits, *[a[0] if isinstance(a, tuple) else a for a in args])


class Box:
    def __init__(self, value):
        self.value = value


class Steps:
    def __init__(self):
        self.kept = []

    def keep(self, value):
        self.kept.append(Box(value))
        return self.kept[-1]

    def fence(self):
        held = lax.optimization_barrier(tuple(b.value for b in self.kept))
        for b, value in zip(self.kept, held):
            b.value = value

    def __call__(self, name, work, *ins):
        self.fence()
        with jax.named_scope(name):
            out = work(*[b.value for b in ins])
        out = [self.keep(v) for v in jax.tree.leaves(out)]
        self.fence()
        return out

    def wait(self, flight):
        self.kept.append(flight)
        self.fence()


class Moves:
    def __init__(self, n_dp, n_tensor):
        self.n_dp, self.n_tensor = n_dp, n_tensor
        self.dp = lax.axis_index(DATA)
        self.core = self.dp & 1
        self.chip_bits = [b for b in (2, 4, 8, 16, 32, 64) if b < n_dp]

    def bit(self, mask):
        return (self.dp // mask) & 1

    def index(self, masks):
        return sum(self.bit(m) << i for i, m in enumerate(masks))

    def over(self, a, axis, mask, name):
        with jax.named_scope(name):
            n = self.n_dp if axis == DATA else self.n_tensor
            return Box(lax.ppermute(a.value, axis, [(i, i ^ mask) for i in range(n)]))


def widen(core, sources, block, out_shape, steps, name):
    n, count = len(sources), len(steps[0])
    tables = []
    for bit in (0, 1):
        rows = np.zeros((n + 1 + len(out_shape), count), np.int32)
        for q in range(n):
            used = [s for s in range(count) if steps[bit][s][0] == q]
            for s in range(count):
                later = [u for u in used if u >= s]
                at = later[0] if later else used[-1]
                rows[q, s] = steps[bit][at][1]
        for s in range(count):
            rows[n, s] = steps[bit][s][0]
            rows[n + 1 :, s] = steps[bit][s][2]
        tables.append(rows)
    table = jnp.where(core == 0, jnp.asarray(tables[0]), jnp.asarray(tables[1]))

    def kernel(table_ref, *refs):
        s = pl.program_id(0)
        for q in range(n):

            @pl.when(table_ref[n, s] == q)
            def _():
                refs[n][...] = refs[q][...].astype(F32).reshape(refs[n].shape)

    lead = len(out_shape) - 2
    return pl.pallas_call(
        kernel,
        grid_spec=pltpu.PrefetchScalarGridSpec(
            num_scalar_prefetch=1,
            grid=(count,),
            in_specs=[
                pl.BlockSpec(block, lambda s, t, q=q: (t[q, s], 0)) for q in range(n)
            ],
            out_specs=pl.BlockSpec(
                (1,) * lead + block,
                lambda s, t: tuple(t[n + 1 + j, s] for j in range(len(out_shape))),
            ),
        ),
        out_shape=jax.ShapeDtypeStruct(out_shape, F32),
        compiler_params=params(24),
        cost_estimate=cost(),
        name=name,
    )(table, *sources)


def spread(gathered, unit, tables, block, out_shape, name):
    count, views = len(tables), len(tables[0][0])
    columns = gathered.shape[-1]
    lead = len(out_shape) - 2
    table = np.asarray([list(t[0]) + list(t[1]) for t in tables], np.int32).T

    def kernel(table_ref, *refs):
        out = refs[views]
        for v in range(views):
            part = refs[v][0].astype(F32)
            if lead:
                out[0, v * unit : (v + 1) * unit, :] = part
            else:
                out[v * unit : (v + 1) * unit, :] = part

    return pl.pallas_call(
        kernel,
        grid_spec=pltpu.PrefetchScalarGridSpec(
            num_scalar_prefetch=1,
            grid=(count,),
            in_specs=[
                pl.BlockSpec((1, unit, columns), lambda s, t, v=v: (t[v, s], 0, 0))
                for v in range(views)
            ],
            out_specs=pl.BlockSpec(
                (1,) * lead + block,
                lambda s, t: tuple(t[views + j, s] for j in range(len(out_shape))),
            ),
        ),
        out_shape=jax.ShapeDtypeStruct(out_shape, F32),
        compiler_params=params(40),
        cost_estimate=cost(),
        name=name,
    )(jnp.asarray(table), *[gathered.reshape(-1, unit, columns)] * views)


START, LATENCY = 1.5, 2.5
RATES = {"y": 46.5e3, "x": 46.5e3, "z": 46.5e3, "core": 500e3}
GATHER = 62.0
FLIGHTS = 5
MARGIN, PATIENCE, EARLY = 4.0, 8.0, 2.0


class Plan:
    def __init__(self, mv):
        self.mv, self.steps = mv, Steps()
        self.box, self.when, self.free = {}, {}, {}
        self.tasks, self.flying, self.waiting = [], [], []
        self.clock, self.gap, self.sent, self.flown = 0.0, 0, {}, {}
        LOG.clear()
        FLOWN.clear()

    def given(self, **arrays):
        for key, value in arrays.items():
            self.box[key], self.when[key] = self.steps.keep(value), 0.0

    def task(self, name, rank, cost, needs, makes, work, sends=()):
        self.tasks.append((rank, len(self.tasks), name, cost, needs, makes, work, sends))

    def link(self, axis, mask):
        if axis == TENSOR:
            return "y", mask
        if mask < 4:
            return ("core", "x")[mask // 2], 1
        return "z", mask // 4

    def send(self, new, key, axis, mask):
        a = self.box[key]
        if mask is None:
            with jax.named_scope(new):
                self.box[new] = Box(lax.all_gather(a.value, axis))
            self.clock += 0.7
            self.free["sc"] = max(self.free.get("sc", 0.0), self.clock) + GATHER
            self.when[new] = self.free["sc"]
            return
        while len(self.flying) >= FLIGHTS:
            self.land(min(self.flying, key=lambda k: self.when[k]))
        self.box[new] = self.mv.over(a, axis, mask, new)
        link, often = self.link(axis, mask)
        took = often * a.value.size * a.value.dtype.itemsize / RATES[link]
        self.clock += 0.5 if link == "core" else START
        self.free[link] = max(self.free.get(link, 0.0), self.clock) + took
        self.when[new] = self.free[link] + (1.0 if link == "core" else LATENCY)
        self.flying.append(new)
        self.sent[new] = (self.gap,)
        self.flown[new] = (a.value.size * a.value.dtype.itemsize, link, took)
        FLOWN.append((new, self.clock, self.when[new]))

    def send_due(self):
        for s in list(self.waiting):
            after = s[4] if len(s) > 4 else None
            if after and not (after in self.when and self.when[after] <= self.clock):
                continue
            if after in self.flying:
                self.land(after)
            self.waiting.remove(s)
            value = self.box[s[1]].value
            size = 1e9 if s[3] is None else value.size * value.dtype.itemsize
            held = [
                k
                for k in self.flying
                if self.sent[k][0] < self.gap and self.flown[k][0] <= size
            ]
            for k in [k for k in held if self.when[k] <= self.clock + PATIENCE]:
                self.land(k)
                held.remove(k)
            for k in held:
                self.free[self.flown[k][1]] = max(
                    [self.clock]
                    + [
                        self.when[j] - LATENCY
                        for j in self.flying
                        if j not in held and self.flown[j][1] == self.flown[k][1]
                    ]
                )
            self.send(*s[:4])
            for k in held:
                if k in self.flying:
                    _, link, took = self.flown[k]
                    self.sent[k] = (self.gap,)
                    self.free[link] = max(self.free[link], self.clock) + took
                    self.when[k] = self.free[link] + LATENCY
                    HELD.append((k, s[0]))

    def land(self, key):
        self.flying.remove(key)
        self.steps.wait(self.box[key])
        if self.when[key] > self.clock:
            self.clock = self.when[key]
            self.gap += 1

    def run(self):
        if len(RANKS) == len(self.tasks):
            self.tasks = [(r, *t[1:]) for r, t in zip(RANKS, self.tasks)]
        while self.tasks:
            self.send_due()
            known = [
                t
                for t in sorted(self.tasks, key=lambda t: t[:2])
                if all(k in self.when for k in t[4])
            ]
            start = {
                t[1]: max([self.when[k] for k in t[4]] + [self.clock]) for t in known
            }
            soonest = min(start.values(), default=1e9)
            due = [self.when[s[4]] for s in self.waiting if s[4] in self.when]
            if due and min(due) <= soonest:
                if min(due) > self.clock:
                    self.clock = min(due)
                    self.gap += 1
                continue
            ready = [t for t in known if start[t[1]] <= soonest + 0.01]
            chosen = ready[0]
            soon = min((t for t in due if t > soonest), default=1e9)
            if soonest + chosen[3] > soon + EARLY:
                fits = [t for t in ready if soonest + t[3] <= soon + EARLY]
                if not fits:
                    self.clock = soon
                    self.gap += 1
                    continue
                chosen = fits[0]
            self.tasks.remove(chosen)
            rank, _, name, cost, needs, makes, work, sends = chosen
            if start[chosen[1]] > self.clock:
                self.gap += 1
            self.clock = begun = start[chosen[1]]
            for key in sorted(self.flying, key=lambda k: self.when[k]):
                if self.when[key] <= self.clock - MARGIN and key not in needs:
                    self.land(key)
            for key in needs:
                if key in self.flying:
                    self.flying.remove(key)
                    if work is None:
                        self.steps.wait(self.box[key])
                        self.gap += 1
            if work is not None:
                COST[0] = cost
                out = self.steps(name, work, *[self.box[k] for k in needs])
                self.clock += cost
                self.gap += 1
                for key, b in zip(makes, out, strict=True):
                    self.box[key], self.when[key] = b, self.clock
            LOG.append((name, begun, self.clock, [s[0] for s in sends]))
            self.waiting += sends


    def fetch(self, rank, name, d, masks, axis):
        y, sib = f"{name}.y{d}", f"{name}.sib{d}"
        cut = [f"{name}.cut{i}.{d}" for i in (0, 1)]
        come = [f"{name}.c{i}.{d}" for i in (0, 1)]
        far = [f"{name}.far{i}.{d}" for i in (0, 1)]
        self.task(f"{sib}.send", rank, 0.0, [y], [], None, [(sib, y, DATA, 1)])
        self.task(
            f"{name}.cut{d}",
            rank + 0.01,
            0.4,
            [y],
            cut,
            lambda a: jnp.split(a, 2, axis),
            [(c, k, DATA, m) for c, k, m in zip(come, cut, masks)],
        )
        for c, f in zip(come, far):
            self.task(f, rank, 0.0, [c], [], None, [(f, c, DATA, 1)])
        return [y, sib, *come, *far]


    def reduce(self, rank, name, levels, back=False):
        s = self.mv.n_tensor // 2
        cur = [f"{name}.p{d}" for d in range(2 * s)]
        while s > 1:
            new = [f"{name}.p{d}.{s}" for d in range(s)]
            for d in range(s):
                far = d >= s // 2
                self.task(
                    new[d],
                    rank,
                    1.5,
                    [cur[d], f"{name}.y{d + s}.{s}"],
                    [new[d]],
                    lambda a, b: [add(a, b)],
                    [(f"{name}.y{d}.{s // 2}", new[d], TENSOR, s // 2)] * far,
                )
            cur, s = new, s // 2
        needs = [cur[0], f"{name}.y1.1"]
        costs = (2.4, 0.9, 0.7, 0.7, 0.7)
        for i, m in enumerate(levels):
            keep, send, come = f"{name}.k{i}", f"{name}.s{i}", f"{name}.d{i}"

            def work(info, a, b, m=m):
                return add_split(info, m.bit_length() - 1, a, b)

            self.task(
                send,
                rank,
                costs[i],
                ["i", *needs],
                [keep, send],
                work,
                [(come, send, DATA, m)],
            )
            needs = [keep, come]
        own, up = f"{name}.own", list(reversed(levels)) + [1]
        sends = [(f"{name}.u0", own, DATA, up[0])] if back else []
        self.task(own, rank, 0.7, needs, [own], lambda a, b: [add(a, b)], sends)
        for i, m in enumerate(up[:-1] if back else []):
            last = i + 2 == len(up)
            out = f"{name}.mine" if last else f"{name}.j{i}"
            come = f"{name}.other" if last else f"{name}.u{i + 1}"

            def work(a, b, m=m):
                bit = self.mv.bit(m)
                low, high = jnp.where(bit == 0, a, b), jnp.where(bit == 0, b, a)
                return [jnp.concatenate([low, high], axis=0)]

            self.task(
                out,
                rank,
                0.3,
                [own, f"{name}.u{i}"],
                [out],
                work,
                [(come, out, DATA, up[i + 1])],
            )
            own = out

    def gather(self, rank, name, chunks, after):
        self.task(
            name,
            rank,
            0.8,
            [f"{c}.own" for c in chunks],
            [name],
            lambda *a: [jnp.concatenate(a, axis=0) if len(a) > 1 else a[0]],
            [(f"{name}.all", name, DATA, None, after)],
        )


def plain(
    n_dp,
    n_tensor,
    x,
    qkv_weight,
    qv_bias,
    out_weight,
    out_bias,
    norm1_gain,
    norm1_shift,
    up_weight,
    up_bias,
    down_weight,
    down_bias,
    norm2_gain,
    norm2_shift,
    lengths,
    grad_output,
):
    width = x.shape[1]

    def whole(w, axis):
        return lax.all_gather(w, TENSOR, axis=axis, tiled=True)

    info = jnp.zeros((BITS + 1,), jnp.int32)
    length = lax.dynamic_slice_in_dim(lengths, lax.axis_index(TENSOR), 1, 0)
    q_bias, v_bias = whole(qv_bias, 1)
    bias = [q_bias, jnp.zeros_like(q_bias), v_bias, whole(up_bias, 0).astype(F32)]
    bias = jnp.concatenate(bias).reshape(-1, 1, width)
    qkv_w, out_w = whole(qkv_weight, 2), whole(out_weight, 0)
    up_w, down_w = whole(up_weight, 1), whole(down_weight, 0)
    (qkv,) = project(info, x, bias, qkv_w)
    mixed, lse = attend(length, qkv)
    normed, normal1, scale1 = attended(
        info, x, out_bias, norm1_gain, norm1_shift, [mixed], [[out_w]]
    )
    act, slope = widened(info, normed, bias, up_w)
    g2, g_two, result, sums2 = narrowed(
        info,
        normal1,
        norm1_gain,
        norm1_shift,
        down_bias,
        norm2_gain,
        norm2_shift,
        grad_output,
        [act],
        [[down_w]],
    )
    g_up, up_sum = gelu_back(info, g2, slope, down_w)
    g1, g_one, sums1 = attended_back(
        g_two, normal1, scale1, norm1_gain, [g_up], [up_w]
    )
    g_qkv, qkv_sum = attend_back(length, qkv, g1, out_w, lse)
    g_input = input_grad(g_one, [g_qkv], [qkv_w])

    def total(a, axis):
        part = lax.psum_scatter(a, TENSOR, scatter_dimension=axis, tiled=True)
        return lax.psum(part, DATA)

    grad_qkv = jnp.stack([contract(x, g_qkv[c], 0, 0) for c in range(3)])
    small = lax.psum(jnp.concatenate([sums1, sums2]), (DATA, TENSOR))
    return (
        result,
        g_input,
        total(grad_qkv, 2),
        total(jnp.stack([qkv_sum[0], qkv_sum[2]]), 1),
        total(contract(mixed, g1, 0, 0), 0),
        small[0],
        small[1],
        small[2],
        total(contract(normed, g_up, 0, 0), 1),
        total(up_sum[0], 0),
        total(contract(act, g2, 0, 0), 0),
        small[3],
        small[4],
        small[5],
    )


def body(
    n_dp,
    n_tensor,
    x,
    qkv_weight,
    qv_bias,
    out_weight,
    out_bias,
    norm1_gain,
    norm1_shift,
    up_weight,
    up_bias,
    down_weight,
    down_bias,
    norm2_gain,
    norm2_shift,
    lengths,
    grad_output,
):
    mv = Moves(n_dp, n_tensor)
    plan = Plan(mv)
    task = plan.task
    parts = range(n_tensor)
    back = list(parts)[::-1]
    width = x.shape[1]
    half = width // 2
    core = mv.core
    hw = qkv_weight.shape[2]
    fw = up_weight.shape[1]
    same = hw == half
    X, Z1, Z = 2, 4, tuple(mv.chip_bits[1:])

    mine_x, mine_z = mv.index((X, 1)), mv.index((Z1, 1))
    place = [mine_x ^ i for i in range(4)] + [4 + (mine_z ^ i) for i in range(4)]
    place += [core, 1 - core, mv.dp]
    place += [mv.bit(m) for m in (1, *mv.chip_bits)]

    plan.given(
        i=jnp.stack(place).astype(jnp.int32),
        lns=lengths,
        x=x,
        qkv_w0=qkv_weight,
        out_w0=out_weight,
        up_w0=up_weight,
        down_w0=down_weight,
        qvb=qv_bias,
        upb=up_bias,
        go=grad_output,
    )

    def others(name):
        return [(f"{name}.y{d}", name, TENSOR, d) for d in parts[1:]]

    def swap(key):
        return (f"{key}.sib", key, DATA, 1)

    def keys(name):
        return [f"{name}{d}" for d in parts]

    both = (AT, AT + 4)

    def pick_q(info, q):
        return pick(info, [(q, 1, width // 8, both)])

    def pick_ou(info, o, u, _):
        return pick(info, [(o, 0, hw // 2, (CORES,)), (u, 0, width // 8, both)])

    def pick_d(info, d, _):
        return pick(info, [(d, 0, fw // 8, both)])

    task(
        "pick_q",
        0,
        2.8,
        ["i", "qkv_w0"],
        ["q"],
        pick_q,
        others("q"),
    )
    task(
        "ln",
        0.5,
        1.0,
        ["lns"],
        ["ln"],
        lambda n: [lax.dynamic_slice_in_dim(n, lax.axis_index(TENSOR), 1, 0)],
    )

    def bias_rows(qv, up):
        q, v = qv[0], qv[1]
        rows = jnp.concatenate([q, jnp.zeros_like(q), v, up.astype(F32)])
        return [rows.reshape(-1, 1, hw)]

    task(
        "b0",
        0.6,
        1.5,
        ["qvb", "upb"],
        ["b0"],
        bias_rows,
        [(f"b{d}", "b0", TENSOR, d, "q.y1") for d in parts[1:]],
    )
    task(
        "pick_ou",
        1.0,
        3.2,
        ["i", "out_w0", "up_w0", "qkv0"],
        ["o", "u"],
        pick_ou,
        [(*s, "q.y1") for s in others("o")] + [(*s, "o.y1") for s in others("u")],
    )
    task(
        "pick_d",
        2.5,
        3.0,
        ["i", "down_w0", "h0"],
        ["d"],
        pick_d,
        [(*s, "u.y1") for s in others("d")],
    )
    qkv_from, out_from = [["qkv_w0"]], [["out_w0"]]
    up_from, down_from = [["up_w0"]], [["down_w0"]]
    for d in parts[1:]:
        qkv_from.append(plan.fetch(0.2, "q", d, (X, Z1), 1))
        o = f"o.y{d}"
        task(f"o.sib{d}", 0.3, 0.0, [o], [], None, [(f"o.sib{d}", o, DATA, 1)])
        out_from.append([o, f"o.sib{d}"])
        up_from.append(plan.fetch(0.4, "u", d, (X, Z1), 0))
        down_from.append(plan.fetch(0.5, "d", d, (X, Z1), 0))

    for d in parts:
        made = [f"qkv{d}", f"qkv_w{d}"] if d else [f"qkv{d}"]
        task(
            f"pj{d}",
            2 + d,
            3.0,
            ["i", "x", f"b{d}", *qkv_from[d]],
            made,
            lambda info, x, b, *w: project(info, x, b, *w),
        )
        task(
            f"h{d}",
            2 + d,
            6.5,
            ["ln", f"qkv{d}"],
            [f"h{d}", f"lse{d}"],
            attend,
            [],
        )

    def split_args(a, groups):
        out, at = [], 0
        for g in groups:
            out.append(a[at : at + len(g)])
            at += len(g)
        return out

    def attended_task(info, x, *rest):
        mixed, weights = rest[:n_tensor], split_args(rest[n_tensor:], out_from)
        return attended(
            info, x, out_bias, norm1_gain, norm1_shift, mixed, weights
        )

    task(
        "at",
        20,
        4.2,
        ["i", "x", *keys("h"), *[k for g in out_from for k in g]],
        ["nb", "n1", "sc1", *keys("out_w")[1:]],
        attended_task,
        [(*swap("nb"), "u.y1")],
    )
    for d in parts:
        task(
            f"wd{d}",
            21 + d,
            8.5,
            ["i", "nb", f"b{d}", *up_from[d]],
            [f"a{d}", f"sl{d}"] + [f"up_w{d}"] * (d > 0),
            widened,
            [(*swap(f"a{d}"), "d.y1")],
        )

    def narrowed_task(info, normal1, grad_output, *rest):
        act, weights = rest[:n_tensor], split_args(rest[n_tensor:], down_from)
        low, g_two, result, sums = narrowed(
            info,
            normal1,
            norm1_gain,
            norm1_shift,
            down_bias,
            norm2_gain,
            norm2_shift,
            grad_output,
            act,
            weights,
        )
        return low, g_two, result, sums

    task(
        "nw",
        40,
        11.5,
        ["i", "n1", "go", *keys("a")]
        + [k for g in down_from for k in g],
        ["g2", "gt", "res", "sums2"],
        narrowed_task,
        [swap("g2")],
    )

    block = fw // 4

    def made(name, rank, cost, items, rows, columns, after=None, of=back, extra=[]):
        args = []
        for d in of:
            for a, _, b, _, *_ in items(d):
                args += [a, b, f"{a}.sib", f"{b}.sib"]

        def work(info, *a):
            outs, at = [], 0
            for d in of:
                jobs = []
                for _, ai, _, bi, *rest in items(d):
                    a1, b1, a2, b2 = a[at : at + 4]
                    a1, a2 = ((v if ai is None else (v, ai)) for v in (a1, a2))
                    b1, b2 = ((v if bi is None else (v, bi)) for v in (b1, b2))
                    jobs.append((a1, b1, a2, b2, *rest))
                    at += 4
                outs.append(jobs)
            return grad_stack(info, outs, rows, columns)

        s = n_tensor // 2
        task(
            f"{name}.p{of[0]}",
            rank,
            cost,
            ["i", *args],
            [f"{name}.p{d}" for d in of],
            work,
            [
                (f"{name}.y{d}.{s}", f"{name}.p{d}", TENSOR, s, after)
                for d in of
                if d >= s
            ]
            + extra,
        )

    chunks = {}
    first_y = f"{n_tensor // 2}.{n_tensor // 2}"

    def chunk(rank, name, levels, rows, back=False):
        chunks[name] = (levels, rows)
        plan.reduce(rank, name, levels, back)

    for i, of in enumerate((back[: n_tensor // 2], back[n_tensor // 2 :])):
        made(
            "down",
            50 + 2.5 * i,
            6.0,
            lambda d: [(f"a{d}", None, "g2", None, 4, (0,), (0, 1))],
            block,
            half,
            None,
            of,
            [swap(k) for k in ("x", *keys("h")) if of[0]],
        )
    chunk(1.0, "down", (X, *Z), fw)
    for i, d in enumerate(back):
        task(
            f"gb{d}",
            (49, 52)[min(i, 1)],
            4.6,
            ["i", "g2", f"sl{d}", *down_from[d]],
            [f"gu{d}", f"us{d}"],
            gelu_back,
            [(*swap(f"gu{d}"), None if d else f"down.y{first_y}")]

        )
    for i, of in enumerate((back[: n_tensor // 2], back[n_tensor // 2 :])):
        made(
            "up",
            64 + 4 * i,
            4.0,
            lambda d: [("nb", None, f"gu{d}", None, 2, (0, 2), (0,))],
            half // 2,
            fw,
            f"down.y{first_y}",
            of,
        )
    chunk(1.2, "up", (X, *Z), half)

    def attended_back_task(g_two, normal, scale, *rest):
        return attended_back(
            g_two, normal, scale, norm1_gain, rest[:n_tensor], rest[n_tensor:]
        )

    task(
        "ab",
        56,
        9.5,
        ["gt", "n1", "sc1", *keys("gu"), *keys("up_w")],
        ["g1", "go1", "sums1"],
        attended_back_task,
        [(*swap("g1"), f"down.y{first_y}")],
    )
    for i, d in enumerate(back):
        task(
            f"hb{d}",
            62 + i,
            10.8,
            ["ln", f"qkv{d}", "g1", f"out_w{d}", f"lse{d}"],
            [f"gq{d}", f"qs{d}"],
            attend_back,
            [(*swap(f"gq{d}"), f"down.y{first_y}")],
        )

    def out_item(d):
        return (f"h{d}", None, "g1", None, 1, (0,), (0, 1))

    def qkv_item(c):
        return lambda d: ("x", None, f"gq{d}", c, 1, (0, 1), (0,))

    if same:
        groups = {"att0": [out_item, qkv_item(2)], "att1": [qkv_item(1), qkv_item(0)]}
    else:
        groups = {"att0": [out_item], "att1": [qkv_item(c) for c in (2, 1, 0)]}
    for i, (name, items) in enumerate(groups.items()):
        rows = hw if items[0] is out_item else half
        made(
            name,
            66 + i,
            5.2,
            lambda d, items=items: [it(d) for it in items],
            rows,
            half if items[0] is out_item else hw,
            f"{('up', 'att0')[i]}.y{first_y}",
        )
        chunk(1.4 + 0.1 * i, name, (X, *Z), rows * len(items), back=True)

    def pack(one, two, *rest):
        packs = []
        for d in parts:
            g, up = rest[2 * d : 2 * d + 2]
            packs.append(
                jnp.concatenate([one.ravel(), two.ravel(), g[0], g[2], up[0]])
            )
        return packs

    needs = [k for d in parts for k in (f"qs{d}", f"us{d}")]
    packs, s = keys("pk"), n_tensor // 2
    task(
        "pk",
        70,
        1.5,
        ["sums1", "sums2", *needs],
        packs,
        pack,
        [
            (f"pk{d}.y", f"pk{d}", TENSOR, s, f"att1.y{first_y}")
            for d in range(s, n_tensor)
        ],
    )
    while s:
        new = [f"sm{s}.{d}" for d in range(s)]
        for d in range(s):
            if s > 1:
                sends = [(f"{new[d]}.y", new[d], TENSOR, s // 2)] * (d >= s // 2)
            else:
                sends = [("sm.1", new[0], DATA, 1)]
            task(
                new[d],
                2.0,
                0.6,
                [packs[d], f"{packs[d + s]}.y"],
                [new[d]],
                lambda a, b: [a + b],
                sends,
            )
        packs, s = new, s // 2
    last, masks = packs[0], [1, *mv.chip_bits]
    for i, m in enumerate(masks):
        out = f"sm.at{m}"
        nxt = masks[i + 1] if i + 1 < len(masks) else None
        sends = [(f"sm.{nxt}", out, DATA, nxt)] if nxt else []
        task(out, 2.0, 0.6, [last, f"sm.{m}"], [out], lambda a, b: [a + b], sends)
        last = out

    task(
        "ig",
        80,
        7.0,
        ["go1", *keys("gq"), *keys("qkv_w")],
        ["gi"],
        lambda g, *a: [input_grad(g, a[:n_tensor], a[n_tensor:])],
    )

    def results(group, names, outputs, after=None):
        plan.gather(1.9, group, names, after)
        per_device = [chunks[n][1] // (n_dp // 2) for n in names]
        unit = min(per_device)
        total = sum(per_device) // unit
        first = {n: sum(per_device[:i]) // unit for i, n in enumerate(names)}

        def at(c, name, row):
            levels, rows = chunks[name]
            own = rows // (n_dp // 2)
            r, dp = row // own, c
            for i, m in enumerate(reversed(levels)):
                dp |= m * ((r >> i) & 1)
            return dp * total + first[name] + row % own // unit

        for name, cost, blocks, block, shape in outputs:
            tables = [
                ([at(c, n, row + r) for r in range(0, block[0], unit)], place)
                for c, n, row, place in blocks
            ]
            task(
                name,
                85,
                cost,
                [f"{group}.all"],
                [name],
                lambda a, *, rest=(unit, tables, block, shape, name): [
                    spread(a, *rest)
                ],
            )

    results(
        "da",
        ("down",),
        [
            (
                "gd",
                7.2,
                [(c, "down", r * block, (r, c)) for r in range(4) for c in (0, 1)],
                (block, half),
                (fw, width),
            )
        ],
        f"att0.y{first_y}",
    )
    rows = half // 4
    results(
        "ua",
        ("up",),
        [
            (
                "gup",
                7.2,
                [
                    (c, "up", r * rows, (4 * c + r, 0))
                    for c in (0, 1)
                    for r in range(4)
                ],
                (rows, fw),
                (width, fw),
            )
        ],
    )

    def sources(*names):
        return [f"{n}.{k}" for n in names for k in ("mine", "other")]

    def cores_result(name, cost, names, blocks, block, shape):
        tables = [
            [(2 * names.index(n) + (c != bit), r, at) for c, n, r, at in blocks]
            for bit in (0, 1)
        ]
        task(
            name,
            85,
            cost,
            sources(*names),
            [name],
            lambda *a: [widen(core, a, block, shape, tables, name)],
        )

    cores_result(
        "gout",
        3.0,
        ("att0",),
        [(c, "att0", 0, (0, c)) for c in (0, 1)],
        (hw, half),
        (hw, width),
    )
    place = {2: ("att0", 1), 1: ("att1", 0), 0: ("att1", 1)}
    if not same:
        place = {c: ("att1", 2 - c) for c in range(3)}
    cores_result(
        "gqkv",
        5.0,
        ("att0", "att1") if same else ("att1",),
        [(c, *place[i], (i, c, 0)) for i in range(3) for c in (0, 1)],
        (half, hw),
        (3, width, hw),
    )

    plan.run()
    value = {k: b.value for k, b in plan.box.items()}
    small = value[last]
    vec = [small[i * width : (i + 1) * width] for i in range(6)]
    rest = small[6 * width :]
    return (
        value["res"],
        value["gi"],
        value["gqkv"],
        rest[: 2 * hw].reshape(2, hw),
        value["gout"],
        vec[0],
        vec[1],
        vec[2],
        value["gup"],
        rest[2 * hw :],
        value["gd"],
        vec[3],
        vec[4],
        vec[5],
    )


def solution(mesh):
    n_dp, n_tensor = mesh.shape[DATA], mesh.shape[TENSOR]
    pairs = n_tensor == 2 and n_dp >= 8 and n_dp & (n_dp - 1) == 0
    return jax.shard_map(
        functools.partial(body if pairs else plain, n_dp, n_tensor),
        mesh=mesh,
        in_specs=(
            P((DATA, TENSOR), None),
            P(None, None, TENSOR),
            P(None, TENSOR),
            P(TENSOR, None),
            P(),
            P(),
            P(),
            P(None, TENSOR),
            P(TENSOR),
            P(TENSOR, None),
            P(),
            P(),
            P(),
            P(DATA),
            P((DATA, TENSOR), None),
        ),
        out_specs=(
            P((DATA, TENSOR), None),
            P((DATA, TENSOR), None),
            P(None, None, TENSOR),
            P(None, TENSOR),
            P(TENSOR, None),
            P(),
            P(),
            P(),
            P(None, TENSOR),
            P(TENSOR),
            P(TENSOR, None),
            P(),
            P(),
            P(),
        ),
        check_vma=False,
    )
```

```python
import functools

import jax
import jax.numpy as jnp
import numpy as np
from jax import lax
from jax.experimental import pallas as pl
from jax.experimental.pallas import tpu as pltpu
from jax.sharding import PartitionSpec as P

HD = 64
TENSOR, DATA = "tensor", "dp"
F32 = jnp.float32
BF16 = jnp.bfloat16
NEG = -1000000000.0
SCALE = 0
COST = [0.0]
LOG = []
RANKS = ()
FLOWN = []
HELD = []


def cost():
    flops = int(SCALE * COST[0] * 1.15e9)
    return pl.CostEstimate(flops=flops, bytes_accessed=0, transcendentals=0)


ERFC_P = 0.3275911
ERFC_C = (
    0.18510853909898187,
    0.17995808540893535,
    0.21032499893163595,
    0.011746556912990477,
    0.4777504794974274,
    -0.4314195259659222,
    0.5110037999525718,
    -0.14447299033990682,
)


def gelu_both(up):
    size = jnp.abs(up)
    t = 1.0 / (1.0 + (ERFC_P * 0.5**0.5) * size)
    poly = jnp.full_like(t, 0.5 * ERFC_C[-1])
    for c in ERFC_C[-2::-1]:
        poly = poly * t + 0.5 * c
    density = jnp.exp(-0.5 * up * up)
    tail = poly * t * density
    phi = jnp.where(up > 0, 1.0 - tail, tail)
    return up * phi, phi + up * (density * 0.3989422804014327)


def contract(a, b, ca, cb):
    return lax.dot_general(a, b, (((ca,), (cb,)), ((), ())), preferred_element_type=F32)


def params(mib):
    return pltpu.CompilerParams(vmem_limit_bytes=mib * 2**20)


def whole_spec(a):
    return pl.BlockSpec(a.shape, lambda *_: (0,) * len(a.shape))


BROUGHT = ((0, 0), (2, 0), (1, 0), (4, 0), (0, 1), (3, 0), (1, 1), (5, 0))


AT, CORES, DP, BITS = 0, 8, 10, 11


def attend_kernel(len_ref, q_ref, k_ref, v_ref, o_ref, lse_ref):
    length = len_ref[0]
    q, k, v = q_ref[0], k_ref[0], v_ref[0]
    rows, width = q.shape
    head = lax.broadcasted_iota(jnp.int32, (rows, width), 1) // HD
    key_pos = lax.broadcasted_iota(jnp.int32, (rows, rows), 0)
    out = None
    for h in range(width // HD):
        mine = head == h
        kh = jnp.where(mine, k, jnp.zeros_like(k)) * jnp.asarray(HD**-0.5, BF16)
        s = jnp.where(key_pos < length, contract(kh, q, 1, 1), F32(NEG))
        top = jnp.max(s, axis=0, keepdims=True)
        e = jnp.exp(s - top)
        total = jnp.sum(e, axis=0, keepdims=True)
        lse_ref[0, h : h + 1, :] = top + jnp.log(total)
        p = (e * (1.0 / total)).astype(BF16)
        o = contract(p, v, 0, 0)
        out = o if out is None else jnp.where(mine, o, out)
    o_ref[...] = out.astype(BF16)


def third(rows, wide, c):
    return pl.BlockSpec((1, rows, wide), lambda i, c=c: (c, 0, i))


def attend(length, qkv):
    _, rows, width = qkv.shape
    wide = min(2 * HD, width)
    steps = width // wide
    return pl.pallas_call(
        attend_kernel,
        grid=(steps,),
        in_specs=[pl.BlockSpec(memory_space=pltpu.SMEM)]
        + [third(rows, wide, c) for c in range(3)],
        out_specs=[
            pl.BlockSpec((rows, wide), lambda i: (0, i)),
            pl.BlockSpec((1, wide // HD, rows), lambda i: (i, 0, 0)),
        ],
        out_shape=[
            jax.ShapeDtypeStruct((rows, width), BF16),
            jax.ShapeDtypeStruct((steps, wide // HD, rows), F32),
        ],
        compiler_params=params(20),
        cost_estimate=cost(),
    )(length, qkv, qkv, qkv)


def attend_back_kernel(
    len_ref, q_ref, k_ref, v_ref, g1_ref, w_ref, lse_ref, d_ref, sum_ref
):
    length = len_ref[0]
    q, k, v = q_ref[0], k_ref[0], v_ref[0]
    g = contract(g1_ref[...], w_ref[...], 1, 1).astype(BF16)
    rows, width = q.shape
    head = lax.broadcasted_iota(jnp.int32, (rows, width), 1) // HD
    head_t = lax.broadcasted_iota(jnp.int32, (width, rows), 0) // HD
    key_pos = lax.broadcasted_iota(jnp.int32, (rows, rows), 0)
    dq = dk = dv = None
    for h in range(width // HD):
        mine = head == h
        kh = jnp.where(mine, k, jnp.zeros_like(k)) * jnp.asarray(HD**-0.5, BF16)
        vh = jnp.where(mine, v, jnp.zeros_like(v))
        s = jnp.where(key_pos < length, contract(kh, q, 1, 1), F32(NEG))
        p = jnp.exp(s - lse_ref[0, h : h + 1, :])
        dp = contract(vh, g, 1, 1)
        dvh = contract(p.astype(BF16), g, 1, 0)
        center = jnp.sum(p * dp, axis=0, keepdims=True)
        ds = (p * (dp - center)).astype(BF16)
        dkh = contract(ds, q, 1, 0)
        dqh = contract(k, ds, 0, 0)
        dv = dvh if dv is None else jnp.where(mine, dvh, dv)
        dk = dkh if dk is None else jnp.where(mine, dkh, dk)
        dq = dqh if dq is None else jnp.where(head_t == h, dqh, dq)
    out = (
        (dq * (HD**-0.5)).T.astype(BF16),
        (dk * (HD**-0.5)).astype(BF16),
        dv.astype(BF16),
    )
    for c in range(3):
        d_ref[c] = out[c]
        sum_ref[c : c + 1, :] = jnp.sum(out[c].astype(F32), axis=0, keepdims=True)


def attend_back(length, qkv, g_one, out_w, lse):
    _, rows, width = qkv.shape
    wide = min(2 * HD, width)
    d = g_one.shape[1]
    return pl.pallas_call(
        attend_back_kernel,
        grid=(width // wide,),
        in_specs=[pl.BlockSpec(memory_space=pltpu.SMEM)]
        + [third(rows, wide, c) for c in range(3)]
        + [
            whole_spec(g_one),
            pl.BlockSpec((wide, d), lambda i: (i, 0)),
            pl.BlockSpec((1, wide // HD, rows), lambda i: (i, 0, 0)),
        ],
        out_specs=[
            pl.BlockSpec((3, rows, wide), lambda i: (0, 0, i)),
            pl.BlockSpec((3, wide), lambda i: (0, i)),
        ],
        out_shape=[
            jax.ShapeDtypeStruct((3, rows, width), BF16),
            jax.ShapeDtypeStruct((3, width), F32),
        ],
        compiler_params=params(28),
        cost_estimate=cost(),
    )(length, qkv, qkv, qkv, g_one, out_w, lse)


def project(at, x, bias, *pieces):
    n = len(pieces)
    rows, depth = x.shape
    width = pieces[0].shape[2]
    size = depth // len(BROUGHT)

    def kernel(at_ref, x_ref, b_ref, *refs):
        w_ref = refs[0]
        if n > 1:
            w_ref = refs[n + 1]
            for i, (k, j) in enumerate(BROUGHT):
                row = pl.multiple_of(at_ref[i] * size, size)
                w_ref[0, pl.ds(row, size)] = refs[k][0, j * size : (j + 1) * size]
        refs[n][0] = (contract(x_ref[...], w_ref[0], 1, 0) + b_ref[0]).astype(BF16)

    out_specs = [pl.BlockSpec((1, rows, width), lambda c, at: (c, 0, 0))]
    out_shape = [jax.ShapeDtypeStruct((3, rows, width), BF16)]
    if n > 1:
        out_specs.append(pl.BlockSpec((1, depth, width), lambda c, at: (c, 0, 0)))
        out_shape.append(jax.ShapeDtypeStruct((3, depth, width), BF16))
    return pl.pallas_call(
        kernel,
        grid_spec=pltpu.PrefetchScalarGridSpec(
            num_scalar_prefetch=1,
            grid=(3,),
            in_specs=[
                whole_spec(x),
                pl.BlockSpec((1, 1, width), lambda c, at: (c, 0, 0)),
            ]
            + [
                pl.BlockSpec((1, p.shape[1], width), lambda c, at: (c, 0, 0))
                for p in pieces
            ],
            out_specs=out_specs,
        ),
        out_shape=out_shape,
        compiler_params=params(20),
        cost_estimate=cost(),
    )(at, x, bias, *pieces)


def norm(hidden):
    center = hidden - jnp.mean(hidden, axis=-1, keepdims=True)
    spread = jnp.mean(center * center, axis=-1, keepdims=True)
    scale = lax.rsqrt(spread + 1e-05)
    return center * scale, scale


def norm_back(grad, normal, scale, gain):
    gy = grad * gain
    mean = jnp.mean(gy, axis=-1, keepdims=True)
    along = jnp.mean(gy * normal, axis=-1, keepdims=True)
    return scale * (gy - mean - normal * along)


def attended(at, x, bias, gain, shift, mixed, weights):
    rows, d = x.shape
    step = min(128, rows)
    cut = [i for i, w in enumerate(weights) if len(w) > 1]
    flat = [p for w in weights for p in w]
    n = len(mixed)

    def kernel(at_ref, x_ref, b_ref, g_ref, s_ref, *refs):
        m, w = refs[:n], refs[n : n + len(flat)]
        low_ref, normal_ref, scale_ref = refs[n + len(flat) :][:3]
        outs = refs[n + len(flat) + 3 :]
        k = j = 0
        total = x_ref[...].astype(F32) + b_ref[...]
        for i, ps in enumerate(weights):
            if len(ps) > 1:
                size = ps[0].shape[0]
                held = outs[j]

                @pl.when(pl.program_id(0) == 0)
                def _(held=held, k=k, ps=ps, size=size):
                    for q in range(len(ps)):
                        row = pl.multiple_of(at_ref[CORES + q] * size, size)
                        held[pl.ds(row, size), :] = w[k + q][...]

                value = held[...]
                j += 1
            else:
                value = w[k][...]
            k += len(ps)
            total = total + contract(m[i][...], value, 1, 0)
        normal, scale = norm(total)
        normal_ref[...] = normal
        scale_ref[...] = scale
        low_ref[...] = (normal * g_ref[...] + s_ref[...]).astype(BF16)

    row = pl.BlockSpec((step, d), lambda i, at: (i, 0))
    out_specs = [row, row, pl.BlockSpec((step, 1), lambda i, at: (i, 0))]
    out_shape = [
        jax.ShapeDtypeStruct((rows, d), BF16),
        jax.ShapeDtypeStruct((rows, d), F32),
        jax.ShapeDtypeStruct((rows, 1), F32),
    ]
    for i in cut:
        out_shape.append(
            jax.ShapeDtypeStruct((len(weights[i]) * weights[i][0].shape[0], d), BF16)
        )
        out_specs.append(whole_spec(out_shape[-1]))
    vecs = [v.reshape(1, d) for v in (bias, gain, shift)]
    return pl.pallas_call(
        kernel,
        grid_spec=pltpu.PrefetchScalarGridSpec(
            num_scalar_prefetch=1,
            grid=(rows // step,),
            in_specs=[row]
            + [whole_spec(v) for v in vecs]
            + [pl.BlockSpec((step, m.shape[1]), lambda i, at: (i, 0)) for m in mixed]
            + [whole_spec(p) for p in flat],
            out_specs=out_specs,
        ),
        out_shape=out_shape,
        compiler_params=params(20),
        cost_estimate=cost(),
    )(at, x, *vecs, *mixed, *flat)


def widened(at, low, bias, *pieces):
    rows, d = low.shape
    n = len(pieces)
    size, width = d // len(BROUGHT), pieces[0].shape[1]
    block, sub = bias.shape[2], min(128, rows)

    def kernel(at_ref, x_ref, b_ref, *refs):
        act_ref, slope_ref = refs[n : n + 2]
        w_ref = refs[0]
        if n > 1:
            w_ref = refs[n + 2]
            for i, (k, j) in enumerate(BROUGHT):
                row = pl.multiple_of(at_ref[i] * size, size)
                w_ref[pl.ds(row, size), :] = refs[k][j * size : (j + 1) * size, :]
        for i in range(0, rows, sub):
            up = contract(x_ref[i : i + sub, :], w_ref[...], 1, 0) + b_ref[0]
            act, slope = gelu_both(up)
            act_ref[i : i + sub, :] = act.astype(BF16)
            slope_ref[i : i + sub, :] = slope.astype(BF16)

    out = jax.ShapeDtypeStruct((rows, width), BF16)
    out_shape = [out, out]
    if n > 1:
        out_shape.append(jax.ShapeDtypeStruct((d, width), BF16))
    return pl.pallas_call(
        kernel,
        grid_spec=pltpu.PrefetchScalarGridSpec(
            num_scalar_prefetch=1,
            grid=(width // block,),
            in_specs=[
                whole_spec(low),
                pl.BlockSpec((1, 1, block), lambda i, at: (3 + i, 0, 0)),
            ]
            + [pl.BlockSpec((p.shape[0], block), lambda i, at: (0, i)) for p in pieces],
            out_specs=[
                pl.BlockSpec((o.shape[0], block), lambda i, at: (0, i))
                for o in out_shape
            ],
        ),
        out_shape=out_shape,
        compiler_params=params(24),
        cost_estimate=cost(),
    )(at, low, bias, *pieces)


def narrowed(at, normal1, gain1, shift1, bias, gain, shift, grad_output, act, weights):
    rows, d = normal1.shape
    block = 256
    steps = d // block
    flat = [p for w in weights for p in w]
    cut = [w for w in weights if len(w) > 1]
    n = len(act)

    def kernel(at_ref, nm_ref, g1_ref, s1_ref, b_ref, g_ref, s_ref, go_ref, *refs):
        a, w = refs[:n], refs[n : n + len(flat)]
        low_ref, grad_ref, result_ref, sum_ref, acc = refs[n + len(flat) :][:5]
        held = list(refs[n + len(flat) + 5 :])
        total = nm_ref[...] * g1_ref[...] + s1_ref[...] + b_ref[...]
        k = 0
        for i, ps in enumerate(weights):
            value = w[k]
            if len(ps) > 1:
                value = held.pop(0)
                size = value.shape[0] // len(BROUGHT)
                for q, (m, j) in enumerate(BROUGHT):
                    row = pl.multiple_of(at_ref[q] * size, size)
                    value[pl.ds(row, size), :] = w[k + m][j * size : (j + 1) * size, :]
            total = total + contract(a[i][...], value[...], 1, 0)
            k += len(ps)
        acc[pl.program_id(0)] = total

        @pl.when(pl.program_id(0) == steps - 1)
        def _():
            sums = [jnp.zeros((1, d), F32) for _ in range(3)]
            for r in range(0, rows, 64):
                cut = slice(r, r + 64)
                hidden = jnp.concatenate([acc[i, cut, :] for i in range(steps)], axis=1)
                normal, scale = norm(hidden)
                result_ref[cut, :] = (normal * g_ref[...] + s_ref[...]).astype(BF16)
                grad = go_ref[cut, :].astype(F32)
                g_two = norm_back(grad, normal, scale, g_ref[...])
                grad_ref[cut, :] = g_two
                low_ref[cut, :] = g_two.astype(BF16)
                for j, v in enumerate((g_two, grad * normal, grad)):
                    sums[j] = sums[j] + jnp.sum(v, axis=0, keepdims=True)
            for j in range(3):
                sum_ref[j : j + 1, :] = sums[j]

    def col(rows):
        return pl.BlockSpec((rows, block), lambda s, at: (0, s))

    vecs = [v.reshape(1, d) for v in (gain1, shift1, bias, gain, shift)]
    out_shape = [
        jax.ShapeDtypeStruct((rows, d), BF16),
        jax.ShapeDtypeStruct((rows, d), F32),
        jax.ShapeDtypeStruct((rows, d), BF16),
        jax.ShapeDtypeStruct((3, d), F32),
    ]
    return pl.pallas_call(
        kernel,
        grid_spec=pltpu.PrefetchScalarGridSpec(
            num_scalar_prefetch=1,
            grid=(steps,),
            in_specs=[col(rows), col(1), col(1), col(1)]
            + [whole_spec(v) for v in vecs[3:]]
            + [whole_spec(grad_output)]
            + [whole_spec(a) for a in act]
            + [col(p.shape[0]) for p in flat],
            out_specs=[whole_spec(o) for o in out_shape],
            scratch_shapes=[pltpu.VMEM((steps, rows, block), F32)]
            + [pltpu.VMEM((act[0].shape[1], block), BF16) for _ in cut],
        ),
        out_shape=out_shape,
        compiler_params=params(32 if cut else 48),
        cost_estimate=cost(),
    )(at, normal1, *vecs, grad_output, *act, *flat)


def gelu_back(at, g, slope, *pieces):
    rows, d = g.shape
    width = slope.shape[1]
    n = len(pieces)
    size = min(512, width)

    def kernel(at_ref, g_ref, s_ref, *refs):
        out_ref, sum_ref = refs[n : n + 2]
        w = refs[0][...]
        if n > 1:
            held, cut = refs[n + 2], width // len(BROUGHT)

            @pl.when(pl.program_id(0) == 0)
            def _():
                for i, (k, j) in enumerate(BROUGHT):
                    row = pl.multiple_of(at_ref[i] * cut, cut)
                    held[pl.ds(row, cut), :] = refs[k][j * cut : (j + 1) * cut, :]

            w = held[pl.ds(pl.multiple_of(pl.program_id(0) * size, size), size), :]
        low = (contract(g_ref[...], w, 1, 1) * s_ref[...].astype(F32)).astype(BF16)
        out_ref[...] = low
        sum_ref[...] = jnp.sum(low.astype(F32), axis=0, keepdims=True)

    def column(rows):
        return pl.BlockSpec((rows, size), lambda s, at: (0, s))

    w_specs = [pl.BlockSpec((size, d), lambda s, at: (s, 0))]
    return pl.pallas_call(
        kernel,
        grid_spec=pltpu.PrefetchScalarGridSpec(
            num_scalar_prefetch=1,
            grid=(width // size,),
            in_specs=[whole_spec(g), column(rows)]
            + ([whole_spec(p) for p in pieces] if n > 1 else w_specs),
            out_specs=[column(rows), column(1)],
            scratch_shapes=[pltpu.VMEM((width, d), BF16)] if n > 1 else [],
        ),
        out_shape=[
            jax.ShapeDtypeStruct((rows, width), BF16),
            jax.ShapeDtypeStruct((1, width), F32),
        ],
        compiler_params=params(24),
        cost_estimate=cost(),
    )(at, g, slope, *pieces)


def attended_back(g_two, normal, scale, gain, g_up, up_w):
    rows, d = g_two.shape
    block = 256
    steps, n = d // block, len(g_up)

    def kernel(g2_ref, nm_ref, sc_ref, gain_ref, *refs):
        g, w = refs[:n], refs[n : 2 * n]
        low_ref, grad_ref, sum_ref, acc = refs[2 * n :]
        total = g2_ref[...]
        for i in range(n):
            total = total + contract(g[i][...], w[i][...], 1, 1)
        acc[pl.program_id(0)] = total

        @pl.when(pl.program_id(0) == steps - 1)
        def _():
            sums = [jnp.zeros((1, d), F32) for _ in range(3)]
            for r in range(0, rows, 64):
                cut = slice(r, r + 64)
                g_in = jnp.concatenate([acc[i, cut, :] for i in range(steps)], axis=1)
                nm = nm_ref[cut, :]
                g_one = norm_back(g_in, nm, sc_ref[cut, :], gain_ref[...])
                grad_ref[cut, :] = g_one
                low_ref[cut, :] = g_one.astype(BF16)
                for j, v in enumerate((g_one, g_in * nm, g_in)):
                    sums[j] = sums[j] + jnp.sum(v, axis=0, keepdims=True)
            for j in range(3):
                sum_ref[j : j + 1, :] = sums[j]

    out_shape = [
        jax.ShapeDtypeStruct((rows, d), BF16),
        jax.ShapeDtypeStruct((rows, d), F32),
        jax.ShapeDtypeStruct((3, d), F32),
    ]
    gain = gain.reshape(1, d)
    return pl.pallas_call(
        kernel,
        grid=(steps,),
        in_specs=[pl.BlockSpec((rows, block), lambda s: (0, s))]
        + [whole_spec(a) for a in (normal, scale, gain, *g_up)]
        + [pl.BlockSpec((block, w.shape[1]), lambda s: (s, 0)) for w in up_w],
        out_specs=[whole_spec(o) for o in out_shape],
        out_shape=out_shape,
        scratch_shapes=[pltpu.VMEM((steps, rows, block), F32)],
        compiler_params=params(28 if n > 1 else 48),
        cost_estimate=cost(),
    )(g_two, normal, scale, gain, *g_up, *up_w)


def input_grad(g_one, g_proj, qkv_w):
    rows, d = g_one.shape
    width, n = g_proj[0].shape[2], len(g_proj)
    block = 256

    def kernel(g1_ref, *refs):
        g, w, out_ref = refs[:n], refs[n : 2 * n], refs[-1]
        total = g1_ref[...]
        for i in range(n):
            for c in range(3):
                total = total + contract(g[i][c], w[i][c], 1, 1)
        out_ref[...] = total

    col = pl.BlockSpec((rows, block), lambda s: (0, s))
    return pl.pallas_call(
        kernel,
        grid=(d // block,),
        in_specs=[col]
        + [whole_spec(g) for g in g_proj]
        + [pl.BlockSpec((3, block, width), lambda s: (0, s, 0))] * n,
        out_specs=col,
        out_shape=jax.ShapeDtypeStruct((rows, d), F32),
        compiler_params=params(24),
        cost_estimate=cost(),
    )(g_one, *g_proj, *qkv_w)


def pick(index, pieces):
    n = len(pieces)
    views = [(i, j) for i, p in enumerate(pieces) for j in range(len(p[3]))]

    def kernel(index_ref, *refs):
        for v, (i, j) in enumerate(views):
            axis, size = pieces[i][1:3]
            at = tuple([slice(None)] * axis + [slice(j * size, (j + 1) * size)])
            refs[len(views) + i][at] = refs[v][...]

    specs, shapes = [], []
    for i, j in views:
        a, axis, size, places = pieces[i]
        specs.append(
            pl.BlockSpec(
                a.shape[:axis] + (size,) + a.shape[axis + 1 :],
                lambda s, at, p=places[j], axis=axis, n=a.ndim: tuple(
                    at[p] if k == axis else 0 for k in range(n)
                ),
            )
        )
    for a, axis, size, places in pieces:
        shape = a.shape[:axis] + (size * len(places),) + a.shape[axis + 1 :]
        shapes.append(jax.ShapeDtypeStruct(shape, a.dtype))
    return pl.pallas_call(
        kernel,
        grid_spec=pltpu.PrefetchScalarGridSpec(
            num_scalar_prefetch=1,
            grid=(1,),
            in_specs=specs,
            out_specs=[whole_spec(s) for s in shapes],
        ),
        out_shape=shapes,
        compiler_params=params(60),
        cost_estimate=cost(),
    )(index, *[pieces[i][0] for i, _ in views])


def add(a, b):
    return (a.astype(F32) + b.astype(F32)).astype(BF16)


def add_split(bits, which, a, b):
    rows, columns = a.shape
    half = rows // 2
    if half % 16:
        total, bit = add(a, b), bits[BITS + which]
        return (
            lax.dynamic_slice_in_dim(total, bit * half, half, 0),
            lax.dynamic_slice_in_dim(total, (1 - bit) * half, half, 0),
        )
    block = half // 2 if half >= 256 else half
    per = half // block

    def kernel(bits_ref, a0, b0, a1, b1, keep_ref, send_ref):
        send_ref[...] = add(a1[...], b1[...])
        keep_ref[...] = add(a0[...], b0[...])

    def spec(of):
        return pl.BlockSpec((block, columns), lambda s, bits: (of(s, bits), 0))

    kept = spec(lambda s, bits: bits[BITS + which] * per + s)
    sent = spec(lambda s, bits: (1 - bits[BITS + which]) * per + s)
    plain = spec(lambda s, bits: s)
    out = jax.ShapeDtypeStruct((half, columns), BF16)
    return pl.pallas_call(
        kernel,
        grid_spec=pltpu.PrefetchScalarGridSpec(
            num_scalar_prefetch=1,
            grid=(per,),
            in_specs=[kept, kept, sent, sent],
            out_specs=[plain, plain],
        ),
        out_shape=[out, out],
        compiler_params=params(12),
        cost_estimate=cost(),
    )(bits, a, b, a, b)


def grad_stack(bits, outs, rows, width):
    jobs = [job for out in outs for job in out]
    sizes = [sum(job[4] for job in out) for out in outs]

    def depth_of(a):
        a = a[0] if isinstance(a, tuple) else a
        return a.shape[-2]

    depth = depth_of(jobs[0][0])
    total = sum(sizes)

    def kernel(bits_ref, *refs):
        s = pl.program_id(0)
        at = first = 0
        j = 0
        for o, out in enumerate(outs):
            for job in out:

                @pl.when((s >= at) & (s < at + job[4]))
                def _(j=j, o=o):
                    x1, y1, x2, y2 = (
                        r[0] if len(r.shape) == 3 else r[...]
                        for r in refs[4 * j : 4 * j + 4]
                    )
                    value = contract(x1, y1, 0, 0) + contract(x2, y2, 0, 0)
                    refs[4 * len(jobs) + o][...] = value.astype(BF16)

                at += job[4]
                j += 1

    def column(place, bits):
        return place[0] + sum(k * bits[BITS + i] for i, k in enumerate(place[1:]) if k)

    def spec(a, block, of):
        if isinstance(a, tuple):
            return pl.BlockSpec((1, *block), lambda s, bits: (a[1], 0, of(s, bits)))
        return pl.BlockSpec(block, lambda s, bits: (0, of(s, bits)))

    specs, args, at = [], [], 0
    for a1, b1, a2, b2, n, a_at, b_at in jobs:

        def a_of(s, bits, at=at, n=n, p=a_at):
            return column(p, bits) + jnp.clip(s - at, 0, n - 1)

        def b_of(s, bits, p=b_at):
            return column(p, bits)

        for a, b in ((a1, b1), (a2, b2)):
            specs += [spec(a, (depth, rows), a_of), spec(b, (depth, width), b_of)]
            args += [a, b]
        at += n
    out_specs, at = [], 0
    for size in sizes:
        out_specs.append(
            pl.BlockSpec(
                (rows, width),
                lambda s, bits, at=at, n=size: (jnp.clip(s - at, 0, n - 1), 0),
            )
        )
        at += size
    return pl.pallas_call(
        kernel,
        grid_spec=pltpu.PrefetchScalarGridSpec(
            num_scalar_prefetch=1, grid=(total,), in_specs=specs, out_specs=out_specs
        ),
        out_shape=[jax.ShapeDtypeStruct((n * rows, width), BF16) for n in sizes],
        compiler_params=params(24),
        cost_estimate=cost(),
    )(bits, *[a[0] if isinstance(a, tuple) else a for a in args])


class Box:
    def __init__(self, value):
        self.value = value


class Steps:
    def __init__(self):
        self.kept = []

    def keep(self, value):
        self.kept.append(Box(value))
        return self.kept[-1]

    def fence(self):
        held = lax.optimization_barrier(tuple(b.value for b in self.kept))
        for b, value in zip(self.kept, held):
            b.value = value

    def __call__(self, name, work, *ins):
        self.fence()
        with jax.named_scope(name):
            out = work(*[b.value for b in ins])
        out = [self.keep(v) for v in jax.tree.leaves(out)]
        self.fence()
        return out

    def wait(self, flight):
        self.kept.append(flight)
        self.fence()


class Moves:
    def __init__(self, n_dp, n_tensor):
        self.n_dp, self.n_tensor = n_dp, n_tensor
        self.dp = lax.axis_index(DATA)
        self.core = self.dp & 1
        self.chip_bits = [b for b in (2, 4, 8, 16, 32, 64) if b < n_dp]

    def bit(self, mask):
        return (self.dp // mask) & 1

    def index(self, masks):
        return sum(self.bit(m) << i for i, m in enumerate(masks))

    def over(self, a, axis, mask, name):
        with jax.named_scope(name):
            n = self.n_dp if axis == DATA else self.n_tensor
            return Box(lax.ppermute(a.value, axis, [(i, i ^ mask) for i in range(n)]))


def widen(core, sources, block, out_shape, steps, name):
    n, count = len(sources), len(steps[0])
    tables = []
    for bit in (0, 1):
        rows = np.zeros((n + 1 + len(out_shape), count), np.int32)
        for q in range(n):
            used = [s for s in range(count) if steps[bit][s][0] == q]
            for s in range(count):
                later = [u for u in used if u >= s]
                at = later[0] if later else used[-1]
                rows[q, s] = steps[bit][at][1]
        for s in range(count):
            rows[n, s] = steps[bit][s][0]
            rows[n + 1 :, s] = steps[bit][s][2]
        tables.append(rows)
    table = jnp.where(core == 0, jnp.asarray(tables[0]), jnp.asarray(tables[1]))

    def kernel(table_ref, *refs):
        s = pl.program_id(0)
        for q in range(n):

            @pl.when(table_ref[n, s] == q)
            def _():
                refs[n][...] = refs[q][...].astype(F32).reshape(refs[n].shape)

    lead = len(out_shape) - 2
    return pl.pallas_call(
        kernel,
        grid_spec=pltpu.PrefetchScalarGridSpec(
            num_scalar_prefetch=1,
            grid=(count,),
            in_specs=[
                pl.BlockSpec(block, lambda s, t, q=q: (t[q, s], 0)) for q in range(n)
            ],
            out_specs=pl.BlockSpec(
                (1,) * lead + block,
                lambda s, t: tuple(t[n + 1 + j, s] for j in range(len(out_shape))),
            ),
        ),
        out_shape=jax.ShapeDtypeStruct(out_shape, F32),
        compiler_params=params(24),
        cost_estimate=cost(),
        name=name,
    )(table, *sources)


def spread(gathered, unit, tables, block, out_shape, name):
    count, views = len(tables), len(tables[0][0])
    columns = gathered.shape[-1]
    lead = len(out_shape) - 2
    table = np.asarray([list(t[0]) + list(t[1]) for t in tables], np.int32).T

    def kernel(table_ref, *refs):
        out = refs[views]
        for v in range(views):
            part = refs[v][0].astype(F32)
            if lead:
                out[0, v * unit : (v + 1) * unit, :] = part
            else:
                out[v * unit : (v + 1) * unit, :] = part

    return pl.pallas_call(
        kernel,
        grid_spec=pltpu.PrefetchScalarGridSpec(
            num_scalar_prefetch=1,
            grid=(count,),
            in_specs=[
                pl.BlockSpec((1, unit, columns), lambda s, t, v=v: (t[v, s], 0, 0))
                for v in range(views)
            ],
            out_specs=pl.BlockSpec(
                (1,) * lead + block,
                lambda s, t: tuple(t[views + j, s] for j in range(len(out_shape))),
            ),
        ),
        out_shape=jax.ShapeDtypeStruct(out_shape, F32),
        compiler_params=params(40),
        cost_estimate=cost(),
        name=name,
    )(jnp.asarray(table), *[gathered.reshape(-1, unit, columns)] * views)


START, LATENCY = 1.5, 2.5
RATES = {"y": 46.5e3, "x": 46.5e3, "z": 46.5e3, "core": 500e3}
GATHER = 62.0
FLIGHTS = 5
MARGIN, PATIENCE, EARLY = 4.0, 8.0, 2.0


class Plan:
    def __init__(self, mv):
        self.mv, self.steps = mv, Steps()
        self.box, self.when, self.free = {}, {}, {}
        self.tasks, self.flying, self.waiting = [], [], []
        self.clock, self.gap, self.sent, self.flown = 0.0, 0, {}, {}
        LOG.clear()
        FLOWN.clear()

    def given(self, **arrays):
        for key, value in arrays.items():
            self.box[key], self.when[key] = self.steps.keep(value), 0.0

    def task(self, name, rank, cost, needs, makes, work, sends=()):
        self.tasks.append((rank, len(self.tasks), name, cost, needs, makes, work, sends))

    def link(self, axis, mask):
        if axis == TENSOR:
            return "y", mask
        if mask < 4:
            return ("core", "x")[mask // 2], 1
        return "z", mask // 4

    def send(self, new, key, axis, mask):
        a = self.box[key]
        if mask is None:
            with jax.named_scope(new):
                self.box[new] = Box(lax.all_gather(a.value, axis))
            self.clock += 0.7
            self.free["sc"] = max(self.free.get("sc", 0.0), self.clock) + GATHER
            self.when[new] = self.free["sc"]
            return
        while len(self.flying) >= FLIGHTS:
            self.land(min(self.flying, key=lambda k: self.when[k]))
        self.box[new] = self.mv.over(a, axis, mask, new)
        link, often = self.link(axis, mask)
        took = often * a.value.size * a.value.dtype.itemsize / RATES[link]
        self.clock += 0.5 if link == "core" else START
        self.free[link] = max(self.free.get(link, 0.0), self.clock) + took
        self.when[new] = self.free[link] + (1.0 if link == "core" else LATENCY)
        self.flying.append(new)
        self.sent[new] = (self.gap,)
        self.flown[new] = (a.value.size * a.value.dtype.itemsize, link, took)
        FLOWN.append((new, self.clock, self.when[new]))

    def send_due(self):
        for s in list(self.waiting):
            after = s[4] if len(s) > 4 else None
            if after and not (after in self.when and self.when[after] <= self.clock):
                continue
            if after in self.flying:
                self.land(after)
            self.waiting.remove(s)
            value = self.box[s[1]].value
            size = 1e9 if s[3] is None else value.size * value.dtype.itemsize
            held = [
                k
                for k in self.flying
                if self.sent[k][0] < self.gap and self.flown[k][0] <= size
            ]
            for k in [k for k in held if self.when[k] <= self.clock + PATIENCE]:
                self.land(k)
                held.remove(k)
            for k in held:
                self.free[self.flown[k][1]] = max(
                    [self.clock]
                    + [
                        self.when[j] - LATENCY
                        for j in self.flying
                        if j not in held and self.flown[j][1] == self.flown[k][1]
                    ]
                )
            self.send(*s[:4])
            for k in held:
                if k in self.flying:
                    _, link, took = self.flown[k]
                    self.sent[k] = (self.gap,)
                    self.free[link] = max(self.free[link], self.clock) + took
                    self.when[k] = self.free[link] + LATENCY
                    HELD.append((k, s[0]))

    def land(self, key):
        self.flying.remove(key)
        self.steps.wait(self.box[key])
        if self.when[key] > self.clock:
            self.clock = self.when[key]
            self.gap += 1

    def run(self):
        if len(RANKS) == len(self.tasks):
            self.tasks = [(r, *t[1:]) for r, t in zip(RANKS, self.tasks)]
        while self.tasks:
            self.send_due()
            known = [
                t
                for t in sorted(self.tasks, key=lambda t: t[:2])
                if all(k in self.when for k in t[4])
            ]
            start = {
                t[1]: max([self.when[k] for k in t[4]] + [self.clock]) for t in known
            }
            soonest = min(start.values(), default=1e9)
            due = [self.when[s[4]] for s in self.waiting if s[4] in self.when]
            if due and min(due) <= soonest:
                if min(due) > self.clock:
                    self.clock = min(due)
                    self.gap += 1
                continue
            ready = [t for t in known if start[t[1]] <= soonest + 0.01]
            chosen = ready[0]
            soon = min((t for t in due if t > soonest), default=1e9)
            if soonest + chosen[3] > soon + EARLY:
                fits = [t for t in ready if soonest + t[3] <= soon + EARLY]
                if not fits:
                    self.clock = soon
                    self.gap += 1
                    continue
                chosen = fits[0]
            self.tasks.remove(chosen)
            rank, _, name, cost, needs, makes, work, sends = chosen
            if start[chosen[1]] > self.clock:
                self.gap += 1
            self.clock = begun = start[chosen[1]]
            for key in sorted(self.flying, key=lambda k: self.when[k]):
                if self.when[key] <= self.clock - MARGIN and key not in needs:
                    self.land(key)
            for key in needs:
                if key in self.flying:
                    self.flying.remove(key)
                    if work is None:
                        self.steps.wait(self.box[key])
                        self.gap += 1
            if work is not None:
                COST[0] = cost
                out = self.steps(name, work, *[self.box[k] for k in needs])
                self.clock += cost
                self.gap += 1
                for key, b in zip(makes, out, strict=True):
                    self.box[key], self.when[key] = b, self.clock
            LOG.append((name, begun, self.clock, [s[0] for s in sends]))
            self.waiting += sends


    def fetch(self, rank, name, d, masks, axis):
        y, sib = f"{name}.y{d}", f"{name}.sib{d}"
        cut = [f"{name}.cut{i}.{d}" for i in (0, 1)]
        come = [f"{name}.c{i}.{d}" for i in (0, 1)]
        far = [f"{name}.far{i}.{d}" for i in (0, 1)]
        self.task(f"{sib}.send", rank, 0.0, [y], [], None, [(sib, y, DATA, 1)])
        self.task(
            f"{name}.cut{d}",
            rank + 0.01,
            0.4,
            [y],
            cut,
            lambda a: jnp.split(a, 2, axis),
            [(c, k, DATA, m) for c, k, m in zip(come, cut, masks)],
        )
        for c, f in zip(come, far):
            self.task(f, rank, 0.0, [c], [], None, [(f, c, DATA, 1)])
        return [y, sib, *come, *far]


    def reduce(self, rank, name, levels, back=False):
        s = self.mv.n_tensor // 2
        cur = [f"{name}.p{d}" for d in range(2 * s)]
        while s > 1:
            new = [f"{name}.p{d}.{s}" for d in range(s)]
            for d in range(s):
                far = d >= s // 2
                self.task(
                    new[d],
                    rank,
                    1.5,
                    [cur[d], f"{name}.y{d + s}.{s}"],
                    [new[d]],
                    lambda a, b: [add(a, b)],
                    [(f"{name}.y{d}.{s // 2}", new[d], TENSOR, s // 2)] * far,
                )
            cur, s = new, s // 2
        needs = [cur[0], f"{name}.y1.1"]
        costs = (2.4, 0.9, 0.7, 0.7, 0.7)
        for i, m in enumerate(levels):
            keep, send, come = f"{name}.k{i}", f"{name}.s{i}", f"{name}.d{i}"

            def work(info, a, b, m=m):
                return add_split(info, m.bit_length() - 1, a, b)

            self.task(
                send,
                rank,
                costs[i],
                ["i", *needs],
                [keep, send],
                work,
                [(come, send, DATA, m)],
            )
            needs = [keep, come]
        own, up = f"{name}.own", list(reversed(levels)) + [1]
        sends = [(f"{name}.u0", own, DATA, up[0])] if back else []
        self.task(own, rank, 0.7, needs, [own], lambda a, b: [add(a, b)], sends)
        for i, m in enumerate(up[:-1] if back else []):
            last = i + 2 == len(up)
            out = f"{name}.mine" if last else f"{name}.j{i}"
            come = f"{name}.other" if last else f"{name}.u{i + 1}"

            def work(a, b, m=m):
                bit = self.mv.bit(m)
                low, high = jnp.where(bit == 0, a, b), jnp.where(bit == 0, b, a)
                return [jnp.concatenate([low, high], axis=0)]

            self.task(
                out,
                rank,
                0.3,
                [own, f"{name}.u{i}"],
                [out],
                work,
                [(come, out, DATA, up[i + 1])],
            )
            own = out

    def gather(self, rank, name, chunks, after):
        self.task(
            name,
            rank,
            0.8,
            [f"{c}.own" for c in chunks],
            [name],
            lambda *a: [jnp.concatenate(a, axis=0) if len(a) > 1 else a[0]],
            [(f"{name}.all", name, DATA, None, after)],
        )


def plain(
    n_dp,
    n_tensor,
    x,
    qkv_weight,
    qv_bias,
    out_weight,
    out_bias,
    norm1_gain,
    norm1_shift,
    up_weight,
    up_bias,
    down_weight,
    down_bias,
    norm2_gain,
    norm2_shift,
    lengths,
    grad_output,
):
    width = x.shape[1]

    def whole(w, axis):
        return lax.all_gather(w, TENSOR, axis=axis, tiled=True)

    info = jnp.zeros((BITS + 1,), jnp.int32)
    length = lax.dynamic_slice_in_dim(lengths, lax.axis_index(TENSOR), 1, 0)
    q_bias, v_bias = whole(qv_bias, 1)
    bias = [q_bias, jnp.zeros_like(q_bias), v_bias, whole(up_bias, 0).astype(F32)]
    bias = jnp.concatenate(bias).reshape(-1, 1, width)
    qkv_w, out_w = whole(qkv_weight, 2), whole(out_weight, 0)
    up_w, down_w = whole(up_weight, 1), whole(down_weight, 0)
    (qkv,) = project(info, x, bias, qkv_w)
    mixed, lse = attend(length, qkv)
    normed, normal1, scale1 = attended(
        info, x, out_bias, norm1_gain, norm1_shift, [mixed], [[out_w]]
    )
    act, slope = widened(info, normed, bias, up_w)
    g2, g_two, result, sums2 = narrowed(
        info,
        normal1,
        norm1_gain,
        norm1_shift,
        down_bias,
        norm2_gain,
        norm2_shift,
        grad_output,
        [act],
        [[down_w]],
    )
    g_up, up_sum = gelu_back(info, g2, slope, down_w)
    g1, g_one, sums1 = attended_back(
        g_two, normal1, scale1, norm1_gain, [g_up], [up_w]
    )
    g_qkv, qkv_sum = attend_back(length, qkv, g1, out_w, lse)
    g_input = input_grad(g_one, [g_qkv], [qkv_w])

    def total(a, axis):
        part = lax.psum_scatter(a, TENSOR, scatter_dimension=axis, tiled=True)
        return lax.psum(part, DATA)

    grad_qkv = jnp.stack([contract(x, g_qkv[c], 0, 0) for c in range(3)])
    small = lax.psum(jnp.concatenate([sums1, sums2]), (DATA, TENSOR))
    return (
        result,
        g_input,
        total(grad_qkv, 2),
        total(jnp.stack([qkv_sum[0], qkv_sum[2]]), 1),
        total(contract(mixed, g1, 0, 0), 0),
        small[0],
        small[1],
        small[2],
        total(contract(normed, g_up, 0, 0), 1),
        total(up_sum[0], 0),
        total(contract(act, g2, 0, 0), 0),
        small[3],
        small[4],
        small[5],
    )


def body(
    n_dp,
    n_tensor,
    x,
    qkv_weight,
    qv_bias,
    out_weight,
    out_bias,
    norm1_gain,
    norm1_shift,
    up_weight,
    up_bias,
    down_weight,
    down_bias,
    norm2_gain,
    norm2_shift,
    lengths,
    grad_output,
):
    mv = Moves(n_dp, n_tensor)
    plan = Plan(mv)
    task = plan.task
    parts = range(n_tensor)
    back = list(parts)[::-1]
    width = x.shape[1]
    half = width // 2
    core = mv.core
    hw = qkv_weight.shape[2]
    fw = up_weight.shape[1]
    same = hw == half
    X, Z1, Z = 2, 4, tuple(mv.chip_bits[1:])

    mine_x, mine_z = mv.index((X, 1)), mv.index((Z1, 1))
    place = [mine_x ^ i for i in range(4)] + [4 + (mine_z ^ i) for i in range(4)]
    place += [core, 1 - core, mv.dp]
    place += [mv.bit(m) for m in (1, *mv.chip_bits)]

    plan.given(
        i=jnp.stack(place).astype(jnp.int32),
        lns=lengths,
        x=x,
        qkv_w0=qkv_weight,
        out_w0=out_weight,
        up_w0=up_weight,
        down_w0=down_weight,
        qvb=qv_bias,
        upb=up_bias,
        go=grad_output,
    )

    def others(name):
        return [(f"{name}.y{d}", name, TENSOR, d) for d in parts[1:]]

    def swap(key):
        return (f"{key}.sib", key, DATA, 1)

    def keys(name):
        return [f"{name}{d}" for d in parts]

    both = (AT, AT + 4)

    def pick_q(info, q):
        return pick(info, [(q, 1, width // 8, both)])

    def pick_ou(info, o, u, _):
        return pick(info, [(o, 0, hw // 2, (CORES,)), (u, 0, width // 8, both)])

    def pick_d(info, d, _):
        return pick(info, [(d, 0, fw // 8, both)])

    task(
        "pick_q",
        0,
        2.8,
        ["i", "qkv_w0"],
        ["q"],
        pick_q,
        others("q"),
    )
    task(
        "ln",
        0.5,
        1.0,
        ["lns"],
        ["ln"],
        lambda n: [lax.dynamic_slice_in_dim(n, lax.axis_index(TENSOR), 1, 0)],
    )

    def bias_rows(qv, up):
        q, v = qv[0], qv[1]
        rows = jnp.concatenate([q, jnp.zeros_like(q), v, up.astype(F32)])
        return [rows.reshape(-1, 1, hw)]

    task(
        "b0",
        0.6,
        1.5,
        ["qvb", "upb"],
        ["b0"],
        bias_rows,
        [(f"b{d}", "b0", TENSOR, d, "q.y1") for d in parts[1:]],
    )
    task(
        "pick_ou",
        1.0,
        3.2,
        ["i", "out_w0", "up_w0", "qkv0"],
        ["o", "u"],
        pick_ou,
        [(*s, "q.y1") for s in others("o")] + [(*s, "o.y1") for s in others("u")],
    )
    task(
        "pick_d",
        2.5,
        3.0,
        ["i", "down_w0", "h0"],
        ["d"],
        pick_d,
        [(*s, "u.y1") for s in others("d")],
    )
    qkv_from, out_from = [["qkv_w0"]], [["out_w0"]]
    up_from, down_from = [["up_w0"]], [["down_w0"]]
    for d in parts[1:]:
        qkv_from.append(plan.fetch(0.2, "q", d, (X, Z1), 1))
        o = f"o.y{d}"
        task(f"o.sib{d}", 0.3, 0.0, [o], [], None, [(f"o.sib{d}", o, DATA, 1)])
        out_from.append([o, f"o.sib{d}"])
        up_from.append(plan.fetch(0.4, "u", d, (X, Z1), 0))
        down_from.append(plan.fetch(0.5, "d", d, (X, Z1), 0))

    for d in parts:
        made = [f"qkv{d}", f"qkv_w{d}"] if d else [f"qkv{d}"]
        task(
            f"pj{d}",
            2 + d,
            3.0,
            ["i", "x", f"b{d}", *qkv_from[d]],
            made,
            lambda info, x, b, *w: project(info, x, b, *w),
        )
        task(
            f"h{d}",
            2 + d,
            6.5,
            ["ln", f"qkv{d}"],
            [f"h{d}", f"lse{d}"],
            attend,
            [],
        )

    def split_args(a, groups):
        out, at = [], 0
        for g in groups:
            out.append(a[at : at + len(g)])
            at += len(g)
        return out

    def attended_task(info, x, *rest):
        mixed, weights = rest[:n_tensor], split_args(rest[n_tensor:], out_from)
        return attended(
            info, x, out_bias, norm1_gain, norm1_shift, mixed, weights
        )

    task(
        "at",
        20,
        4.2,
        ["i", "x", *keys("h"), *[k for g in out_from for k in g]],
        ["nb", "n1", "sc1", *keys("out_w")[1:]],
        attended_task,
        [(*swap("nb"), "u.y1")],
    )
    for d in parts:
        task(
            f"wd{d}",
            21 + d,
            8.5,
            ["i", "nb", f"b{d}", *up_from[d]],
            [f"a{d}", f"sl{d}"] + [f"up_w{d}"] * (d > 0),
            widened,
            [(*swap(f"a{d}"), "d.y1")],
        )

    def narrowed_task(info, normal1, grad_output, *rest):
        act, weights = rest[:n_tensor], split_args(rest[n_tensor:], down_from)
        low, g_two, result, sums = narrowed(
            info,
            normal1,
            norm1_gain,
            norm1_shift,
            down_bias,
            norm2_gain,
            norm2_shift,
            grad_output,
            act,
            weights,
        )
        return low, g_two, result, sums

    task(
        "nw",
        40,
        11.5,
        ["i", "n1", "go", *keys("a")]
        + [k for g in down_from for k in g],
        ["g2", "gt", "res", "sums2"],
        narrowed_task,
        [swap("g2")],
    )

    block = fw // 4

    def made(name, rank, cost, items, rows, columns, after=None, of=back, extra=[]):
        args = []
        for d in of:
            for a, _, b, _, *_ in items(d):
                args += [a, b, f"{a}.sib", f"{b}.sib"]

        def work(info, *a):
            outs, at = [], 0
            for d in of:
                jobs = []
                for _, ai, _, bi, *rest in items(d):
                    a1, b1, a2, b2 = a[at : at + 4]
                    a1, a2 = ((v if ai is None else (v, ai)) for v in (a1, a2))
                    b1, b2 = ((v if bi is None else (v, bi)) for v in (b1, b2))
                    jobs.append((a1, b1, a2, b2, *rest))
                    at += 4
                outs.append(jobs)
            return grad_stack(info, outs, rows, columns)

        s = n_tensor // 2
        task(
            f"{name}.p{of[0]}",
            rank,
            cost,
            ["i", *args],
            [f"{name}.p{d}" for d in of],
            work,
            [
                (f"{name}.y{d}.{s}", f"{name}.p{d}", TENSOR, s, after)
                for d in of
                if d >= s
            ]
            + extra,
        )

    chunks = {}
    first_y = f"{n_tensor // 2}.{n_tensor // 2}"

    def chunk(rank, name, levels, rows, back=False):
        chunks[name] = (levels, rows)
        plan.reduce(rank, name, levels, back)

    for i, of in enumerate((back[: n_tensor // 2], back[n_tensor // 2 :])):
        made(
            "down",
            50 + 2.5 * i,
            6.0,
            lambda d: [(f"a{d}", None, "g2", None, 4, (0,), (0, 1))],
            block,
            half,
            None,
            of,
            [swap(k) for k in ("x", *keys("h")) if of[0]],
        )
    chunk(1.0, "down", (X, *Z), fw)
    for i, d in enumerate(back):
        task(
            f"gb{d}",
            (49, 52)[min(i, 1)],
            4.6,
            ["i", "g2", f"sl{d}", *down_from[d]],
            [f"gu{d}", f"us{d}"],
            gelu_back,
            [(*swap(f"gu{d}"), None if d else f"down.y{first_y}")]

        )
    for i, of in enumerate((back[: n_tensor // 2], back[n_tensor // 2 :])):
        made(
            "up",
            64 + 4 * i,
            4.0,
            lambda d: [("nb", None, f"gu{d}", None, 2, (0, 2), (0,))],
            half // 2,
            fw,
            f"down.y{first_y}",
            of,
        )
    chunk(1.2, "up", (X, *Z), half)

    def attended_back_task(g_two, normal, scale, *rest):
        return attended_back(
            g_two, normal, scale, norm1_gain, rest[:n_tensor], rest[n_tensor:]
        )

    task(
        "ab",
        56,
        9.5,
        ["gt", "n1", "sc1", *keys("gu"), *keys("up_w")],
        ["g1", "go1", "sums1"],
        attended_back_task,
        [(*swap("g1"), f"down.y{first_y}")],
    )
    for i, d in enumerate(back):
        task(
            f"hb{d}",
            62 + i,
            10.8,
            ["ln", f"qkv{d}", "g1", f"out_w{d}", f"lse{d}"],
            [f"gq{d}", f"qs{d}"],
            attend_back,
            [(*swap(f"gq{d}"), f"down.y{first_y}")],
        )

    def out_item(d):
        return (f"h{d}", None, "g1", None, 1, (0,), (0, 1))

    def qkv_item(c):
        return lambda d: ("x", None, f"gq{d}", c, 1, (0, 1), (0,))

    if same:
        groups = {"att0": [out_item, qkv_item(2)], "att1": [qkv_item(1), qkv_item(0)]}
    else:
        groups = {"att0": [out_item], "att1": [qkv_item(c) for c in (2, 1, 0)]}
    for i, (name, items) in enumerate(groups.items()):
        rows = hw if items[0] is out_item else half
        made(
            name,
            66 + i,
            5.2,
            lambda d, items=items: [it(d) for it in items],
            rows,
            half if items[0] is out_item else hw,
            f"{('up', 'att0')[i]}.y{first_y}",
        )
        chunk(1.4 + 0.1 * i, name, (X, *Z), rows * len(items), back=True)

    def pack(one, two, *rest):
        packs = []
        for d in parts:
            g, up = rest[2 * d : 2 * d + 2]
            packs.append(
                jnp.concatenate([one.ravel(), two.ravel(), g[0], g[2], up[0]])
            )
        return packs

    needs = [k for d in parts for k in (f"qs{d}", f"us{d}")]
    packs, s = keys("pk"), n_tensor // 2
    task(
        "pk",
        70,
        1.5,
        ["sums1", "sums2", *needs],
        packs,
        pack,
        [
            (f"pk{d}.y", f"pk{d}", TENSOR, s, f"att1.y{first_y}")
            for d in range(s, n_tensor)
        ],
    )
    while s:
        new = [f"sm{s}.{d}" for d in range(s)]
        for d in range(s):
            if s > 1:
                sends = [(f"{new[d]}.y", new[d], TENSOR, s // 2)] * (d >= s // 2)
            else:
                sends = [("sm.1", new[0], DATA, 1)]
            task(
                new[d],
                2.0,
                0.6,
                [packs[d], f"{packs[d + s]}.y"],
                [new[d]],
                lambda a, b: [a + b],
                sends,
            )
        packs, s = new, s // 2
    last, masks = packs[0], [1, *mv.chip_bits]
    for i, m in enumerate(masks):
        out = f"sm.at{m}"
        nxt = masks[i + 1] if i + 1 < len(masks) else None
        sends = [(f"sm.{nxt}", out, DATA, nxt)] if nxt else []
        task(out, 2.0, 0.6, [last, f"sm.{m}"], [out], lambda a, b: [a + b], sends)
        last = out

    def unpack(a):
        rest = a[6 * width :]
        vec = [a[i * width : (i + 1) * width] for i in range(6)]
        return [*vec, rest[: 2 * hw].reshape(2, hw), rest[2 * hw :]]

    task("cut", 2.0, 1.8, [last], [f"v{i}" for i in range(8)], unpack)
    task(
        "ig",
        80,
        7.0,
        ["go1", *keys("gq"), *keys("qkv_w")],
        ["gi"],
        lambda g, *a: [input_grad(g, a[:n_tensor], a[n_tensor:])],
    )

    def results(group, names, outputs, after=None):
        plan.gather(1.9, group, names, after)
        per_device = [chunks[n][1] // (n_dp // 2) for n in names]
        unit = min(per_device)
        total = sum(per_device) // unit
        first = {n: sum(per_device[:i]) // unit for i, n in enumerate(names)}

        def at(c, name, row):
            levels, rows = chunks[name]
            own = rows // (n_dp // 2)
            r, dp = row // own, c
            for i, m in enumerate(reversed(levels)):
                dp |= m * ((r >> i) & 1)
            return dp * total + first[name] + row % own // unit

        for name, cost, blocks, block, shape in outputs:
            tables = [
                ([at(c, n, row + r) for r in range(0, block[0], unit)], place)
                for c, n, row, place in blocks
            ]
            task(
                name,
                85,
                cost,
                [f"{group}.all"],
                [name],
                lambda a, *, rest=(unit, tables, block, shape, name): [
                    spread(a, *rest)
                ],
            )

    results(
        "da",
        ("down",),
        [
            (
                "gd",
                7.2,
                [(c, "down", r * block, (r, c)) for r in range(4) for c in (0, 1)],
                (block, half),
                (fw, width),
            )
        ],
        f"att0.y{first_y}",
    )
    rows = half // 4
    results(
        "ua",
        ("up",),
        [
            (
                "gup",
                7.2,
                [
                    (c, "up", r * rows, (4 * c + r, 0))
                    for c in (0, 1)
                    for r in range(4)
                ],
                (rows, fw),
                (width, fw),
            )
        ],
    )

    def sources(*names):
        return [f"{n}.{k}" for n in names for k in ("mine", "other")]

    def cores_result(name, cost, names, blocks, block, shape):
        tables = [
            [(2 * names.index(n) + (c != bit), r, at) for c, n, r, at in blocks]
            for bit in (0, 1)
        ]
        task(
            name,
            85,
            cost,
            sources(*names),
            [name],
            lambda *a: [widen(core, a, block, shape, tables, name)],
        )

    cores_result(
        "gout",
        3.0,
        ("att0",),
        [(c, "att0", 0, (0, c)) for c in (0, 1)],
        (hw, half),
        (hw, width),
    )
    place = {2: ("att0", 1), 1: ("att1", 0), 0: ("att1", 1)}
    if not same:
        place = {c: ("att1", 2 - c) for c in range(3)}
    cores_result(
        "gqkv",
        5.0,
        ("att0", "att1") if same else ("att1",),
        [(c, *place[i], (i, c, 0)) for i in range(3) for c in (0, 1)],
        (half, hw),
        (3, width, hw),
    )

    plan.run()
    value = {k: b.value for k, b in plan.box.items()}
    vec = [value[f"v{i}"] for i in range(6)]
    return (
        value["res"],
        value["gi"],
        value["gqkv"],
        value["v6"],
        value["gout"],
        vec[0],
        vec[1],
        vec[2],
        value["gup"],
        value["v7"],
        value["gd"],
        vec[3],
        vec[4],
        vec[5],
    )


def solution(mesh):
    n_dp, n_tensor = mesh.shape[DATA], mesh.shape[TENSOR]
    pairs = n_tensor == 2 and n_dp >= 8 and n_dp & (n_dp - 1) == 0
    return jax.shard_map(
        functools.partial(body if pairs else plain, n_dp, n_tensor),
        mesh=mesh,
        in_specs=(
            P((DATA, TENSOR), None),
            P(None, None, TENSOR),
            P(None, TENSOR),
            P(TENSOR, None),
            P(),
            P(),
            P(),
            P(None, TENSOR),
            P(TENSOR),
            P(TENSOR, None),
            P(),
            P(),
            P(),
            P(DATA),
            P((DATA, TENSOR), None),
        ),
        out_specs=(
            P((DATA, TENSOR), None),
            P((DATA, TENSOR), None),
            P(None, None, TENSOR),
            P(None, TENSOR),
            P(TENSOR, None),
            P(),
            P(),
            P(),
            P(None, TENSOR),
            P(TENSOR),
            P(TENSOR, None),
            P(),
            P(),
            P(),
        ),
        check_vma=False,
    )
```
